32 devices in a mesh: level: 2 (over core), dp: 16 (over z, y, x).
Axes of the slice: x: 2, y: 2, z: 4, core: 2. Of those that a mesh axis runs over, the one named last changes fastest.
Arguments:
- image: bfloat16 [3, 3, 512, 128], P(None, None, 'dp'), may hold values from -6 to 6
- mask: int32 [3, 512, 128], P(None, 'dp'), may hold values from 0 to 1
- codes: int32 [2, 3, 512, 128], P('level', None, 'dp'), may hold values from 0 to 511
- ema_count: float32 [2, 512], P('level'), may hold values from 0.5 to 3
- ema_sum: float32 [2, 512, 64], P('level'), may hold values from -6 to 6
- encoder_weight: float32 [2, 27, 128], P('level'), may hold values from -1.25 to 1.25
- encoder_first: float32 [2, 27, 128], P('level'), may hold values from -0.013671875 to 0.013671875
- encoder_second: float32 [2, 27, 128], P('level'), may hold values from 8.138021e-07 to 3.2552084e-06
- latent_weight: float32 [2, 128, 64], P('level'), may hold values from -0.5 to 0.5
- latent_first: float32 [2, 128, 64], P('level'), may hold values from -0.01953125 to 0.01953125
- latent_second: float32 [2, 128, 64], P('level'), may hold values from 1.8310546e-06 to 7.3242186e-06
- decoder_weight: float32 [2, 1152, 128], P('level'), may hold values from -0.1875 to 0.1875
- decoder_first: float32 [2, 1152, 128], P('level'), may hold values from -0.009765625 to 0.009765625
- decoder_second: float32 [2, 1152, 128], P('level'), may hold values from 4.5776366e-07 to 1.8310546e-06
- readout_weight: float32 [2, 128, 3], P('level'), may hold values from -0.5 to 0.5
- readout_first: float32 [2, 128, 3], P('level'), may hold values from -0.0625 to 0.0625
- readout_second: float32 [2, 128, 3], P('level'), may hold values from 1.6276043e-05 to 6.612142e-05
Outputs:
- loss_sum: float32 [], replicated
- valid_count: float32 [], replicated
- count_new: float32 [2, 512], P('level')
- sum_new: float32 [2, 512, 64], P('level')
- encoder_moment: float32 [2, 27, 128], P('level')
- encoder_square: float32 [2, 27, 128], P('level')
- encoder_master: float32 [2, 27, 128], P('level')
- encoder_copy: bfloat16 [2, 27, 128], P('level')
- latent_moment: float32 [2, 128, 64], P('level')
- latent_square: float32 [2, 128, 64], P('level')
- latent_master: float32 [2, 128, 64], P('level')
- latent_copy: bfloat16 [2, 128, 64], P('level')
- decoder_moment: float32 [2, 1152, 128], P('level')
- decoder_square: float32 [2, 1152, 128], P('level')
- decoder_master: float32 [2, 1152, 128], P('level')
- decoder_copy: bfloat16 [2, 1152, 128], P('level')
- readout_moment: float32 [2, 128, 3], P('level')
- readout_square: float32 [2, 128, 3], P('level')
- readout_master: float32 [2, 128, 3], P('level')
- readout_copy: bfloat16 [2, 128, 3], P('level')
The draws below stay inside these ranges and needn't reach their ends.
All inputs are finite; a program needn't handle non-finite values.
Results may differ from the reference program's by a relative error of at most 0.0059.
The reference program's roundings to bfloat16 on the way count: a program that leaves them out, or rounds other values in their place, can miss the bound.
Values may be sent and summed in bfloat16 or wider, within the bound.
No kernel may reach another device: no remote copies, remote signals or barrier semaphores. Data moves between devices by JAX's collectives and lax.ppermute only.
A program may use at most 128 MiB of HBM per device.

```python
import math
import jax
import jax.numpy as jnp
from jax import lax

CH = 128
LAT = 64
CODES = 512
WIDE = 128
CROP = 128
BAND = 32
MB = 3
STEP = 5
CANVAS = 512
PIX = 196608


def draw_mask(key, part):
    key = jax.random.fold_in(key, 3)
    positions = jnp.arange(CANVAS, dtype=jnp.int32)
    limit = 250 + 500 * positions // CANVAS
    ticket = jax.random.randint(key, (MB, CANVAS, WIDE), 0, 1000)
    return (ticket < limit[None, :, None]).astype(jnp.int32)


def place_ends(entries, rng, least, high):
    spot = [jax.random.randint(jax.random.fold_in(rng, axis), (), 0, length) for axis, length in enumerate(entries.shape)]
    main_axis = entries.shape.index(max(entries.shape))
    neighbour = spot[:main_axis] + [(spot[main_axis] + 1) % entries.shape[main_axis]] + spot[main_axis + 1:]
    return entries.at[tuple(spot)].set(least).at[tuple(neighbour)].set(high)


def steps_of(stream_key, extent, pieces, low, high):
    loudness = 1.0
    for axis_at, shards_of in pieces:
        heights = jax.random.uniform(jax.random.fold_in(jax.random.fold_in(stream_key, 6), axis_at), (shards_of,), jnp.float32, low / len(pieces), high / len(pieces))
        loudness = loudness * jnp.repeat(jnp.exp(heights), extent[axis_at] // shards_of).reshape((-1,) + (1,) * (len(extent) - 1 - axis_at))
    return loudness


def normal_values(stream_key, shape, scale, most, pieces=(), held_as=jnp.bfloat16):
    values = scale * jax.random.normal(stream_key, shape, jnp.float32)
    if pieces:
        values = values * steps_of(stream_key, shape, pieces, -0.22, 0.18)
    return jnp.clip(values, -most, most).astype(held_as)


def setup_inputs(seed: int = 0) -> dict:
    arg_keys = jax.random.split(jax.random.key(seed), 18)
    return {
        "image": normal_values(arg_keys[0], (MB, 3, CANVAS, WIDE), 1.0, 6.0, ((2, 16),)),
        "mask": draw_mask(jax.random.fold_in(arg_keys[17], 71), 0),
        "codes": place_ends(jax.random.randint(arg_keys[2], (2, MB, CANVAS, WIDE), 0, CODES), jax.random.fold_in(arg_keys[2], 1), 0, CODES - 1).astype(jnp.int32),
        "ema_count": jnp.clip(jnp.exp(math.log(3.0) - 1.7917595 * jax.random.uniform(arg_keys[3], (2, CODES), jnp.float32) ** steps_of(arg_keys[3], (2, CODES), ((0, 2),), -0.2, 0.2)), 0.5, 3.0),
        "ema_sum": normal_values(arg_keys[4], (2, CODES, LAT), (max(0.002 * PIX // CODES, 0.5)), 6.0, ((0, 2),), jnp.float32),
        "encoder_weight": normal_values(arg_keys[5], (2, 27, CH), 27 ** -0.5, 1.25, ((0, 2),), jnp.float32),
        "encoder_first": normal_values(arg_keys[6], (2, 27, CH), (0.4 * PIX ** -0.5), 0.013671875, ((0, 2),), jnp.float32),
        "encoder_second": jnp.clip(jnp.exp(math.log(3.2552084121562075e-06) - 1.3862944 * jax.random.uniform(arg_keys[7], (2, 27, CH), jnp.float32) ** steps_of(arg_keys[7], (2, 27, CH), ((0, 2),), -0.2, 0.2)), 8.138021030390519e-07, 3.2552084121562075e-06),
        "latent_weight": normal_values(arg_keys[8], (2, CH, LAT), CH ** -0.5, 0.5, ((0, 2),), jnp.float32),
        "latent_first": normal_values(arg_keys[9], (2, CH, LAT), (0.6 * PIX ** -0.5), 0.01953125, ((0, 2),), jnp.float32),
        "latent_second": jnp.clip(jnp.exp(math.log(7.324218586290954e-06) - 1.3862944 * jax.random.uniform(arg_keys[10], (2, CH, LAT), jnp.float32) ** steps_of(arg_keys[10], (2, CH, LAT), ((0, 2),), -0.2, 0.2)), 1.8310546465727384e-06, 7.324218586290954e-06),
        "decoder_weight": normal_values(arg_keys[11], (2, 18 * LAT, CH), (18 * LAT) ** -0.5, 0.1875, ((0, 2),), jnp.float32),
        "decoder_first": normal_values(arg_keys[12], (2, 18 * LAT, CH), (0.3 * PIX ** -0.5), 0.009765625, ((0, 2),), jnp.float32),
        "decoder_second": jnp.clip(jnp.exp(math.log(1.8310546465727384e-06) - 1.3862944 * jax.random.uniform(arg_keys[13], (2, 18 * LAT, CH), jnp.float32) ** steps_of(arg_keys[13], (2, 18 * LAT, CH), ((0, 2),), -0.2, 0.2)), 4.577636616431846e-07, 1.8310546465727384e-06),
        "readout_weight": normal_values(arg_keys[14], (2, CH, 3), CH ** -0.5, 0.5, ((0, 2),), jnp.float32),
        "readout_first": normal_values(arg_keys[15], (2, CH, 3), (1.8 * PIX ** -0.5), 0.0625, ((0, 2),), jnp.float32),
        "readout_second": jnp.clip(jnp.exp(math.log(6.612142169615254e-05) - 1.4017985 * jax.random.uniform(arg_keys[16], (2, CH, 3), jnp.float32) ** steps_of(arg_keys[16], (2, CH, 3), ((0, 2),), -0.2, 0.2)), 1.627604251552839e-05, 6.612142169615254e-05),
    }


@jax.custom_vjp
def low(v):
    return lax.optimization_barrier(v.astype(jnp.bfloat16)).astype(jnp.float32)

@jax.custom_vjp
def low_back(v):
    return v

def low_keep(v):
    return (low(v), None)

def low_pass(kept, grad):
    return (grad,)

def back_keep(v):
    return (v, None)

def back_low(kept, grad):
    return (low(grad),)
low.defvjp(low_keep, low_pass)
low_back.defvjp(back_keep, back_low)
HIGH = lax.Precision.HIGHEST
RATES = (0.05, 0.03, 0.01, 0.03)

def block_starts():
    height = math.gcd(CANVAS, 512)
    return (height, jnp.arange(CANVAS // height, dtype=jnp.int32) * height)

def row_gate(start, height, down):
    rows = start + jnp.arange(height, dtype=jnp.int32) + BAND
    other = rows + (down - 1)
    return (jnp.floor_divide(other, CROP) == jnp.floor_divide(rows, CROP)).astype(jnp.float32)

def encode(pad_image, encoder, latent_map):
    height, starts = block_starts()

    def one_block(start):
        piece = lax.dynamic_slice_in_dim(pad_image, start, height + 2, 1)
        patches = jnp.concatenate([piece[:, down:down + height, across:across + WIDE] * row_gate(start, height, down)[None, :, None] for down in range(3) for across in range(3)], 0)
        before = low_back(jnp.einsum('krw,ko->rwo', patches, encoder, precision=HIGH))
        hidden = low(jax.nn.silu(before))
        return jnp.einsum('rwc,cl->rwl', hidden, latent_map, precision=HIGH)
    return lax.map(jax.checkpoint(one_block), starts).reshape(CANVAS, WIDE, LAT)

def decode(joined, decoder, readout, picture, keep):
    height, starts = block_starts()
    padded = jnp.pad(joined, ((1, 1), (1, 1), (0, 0)))
    taps = decoder.reshape(9, 2 * LAT, CH)

    def one_block(start):
        piece = lax.dynamic_slice_in_dim(padded, start, height + 2, 0)
        before = jnp.zeros((height, WIDE, CH), joined.dtype)
        for tap in range(9):
            down, across = (tap // 3, tap % 3)
            shifted = piece[down:down + height, across:across + WIDE] * row_gate(start, height, down)[:, None, None]
            before = before + jnp.einsum('rwc,co->rwo', shifted, taps[tap], precision=HIGH)
        before = low_back(before)
        active = low(jax.nn.silu(before))
        recon = low_back(jnp.einsum('rwc,co->orw', active, readout, precision=HIGH))
        target = lax.dynamic_slice_in_dim(picture, start, height, 1)
        weight = lax.dynamic_slice_in_dim(keep, start, height, 0)
        return jnp.sum(weight[None] * (recon - target) ** 2)
    return jnp.sum(lax.map(jax.checkpoint(one_block), starts))

def forward(params, pad_image, picture, keep, code_maps, fixed, books):
    encoder, latent_map, decoder, readout = [low(item) for item in params]
    total = jnp.zeros((), picture.dtype)
    sent = None
    for level in range(2):
        latent = low_back(encode(pad_image, encoder[level], latent_map[level]))
        quant = jnp.take(books[level], code_maps[level], axis=0)
        straight = quant + (latent - fixed[level])
        if level == 0:
            other = jnp.zeros_like(straight)
        else:
            other = low_back(sent)
        sent = straight
        gap = latent - quant
        total = total + 0.25 * jnp.sum(keep[..., None] * gap * gap)
        total = total + decode(jnp.concatenate([straight, other], -1), decoder[level], readout[level], picture, keep)
    return total

def adamw(weight, grad, first, second, rate):
    moment = 0.5 * first + 0.5 * grad
    square = 0.5 * second + 0.5 * grad * grad
    scale = 1.0 - 0.5 ** STEP
    master = weight - rate * (moment / scale / (jnp.sqrt(square / scale) + 1e-08) + 0.01 * weight)
    return (moment, square, master, master.astype(jnp.bfloat16))

def reference(image, mask, codes, ema_count, ema_sum, encoder_weight, encoder_first, encoder_second, latent_weight, latent_first, latent_second, decoder_weight, decoder_first, decoder_second, readout_weight, readout_first, readout_second):
    params = (encoder_weight, latent_weight, decoder_weight, readout_weight)
    books = low(ema_sum / ema_count[..., None])
    lowered = [low(item) for item in params]
    grads = [jnp.zeros_like(item) for item in params]
    loss_sum = jnp.zeros((), ema_sum.dtype)
    counts = jnp.zeros_like(ema_count)
    sums = jnp.zeros_like(ema_sum)
    for index in range(MB):
        picture = image[index].astype(jnp.float32)
        keep = mask[index].astype(jnp.float32)
        pad_image = jnp.pad(picture, ((0, 0), (1, 1), (1, 1)))
        code_maps = codes[:, index]
        fixed = [encode(pad_image, lowered[0][level], lowered[1][level]) for level in range(2)]
        value, pullback = jax.vjp(lambda p: forward(p, pad_image, picture, keep, code_maps, fixed, books), params)
        parts = pullback(jnp.ones_like(value))[0]
        grads = [total + part for total, part in zip(grads, parts)]
        loss_sum = loss_sum + value
        flat_keep = keep.reshape(-1)
        count_rows = []
        sum_rows = []
        for level in range(2):
            flat_codes = code_maps[level].reshape(-1).astype(jnp.int32)
            count_rows.append(jax.ops.segment_sum(flat_keep, flat_codes, CODES))
            rounded = low(fixed[level]).reshape(-1, LAT)
            sum_rows.append(jax.ops.segment_sum(flat_keep[:, None] * rounded, flat_codes, CODES))
        counts = counts + jnp.stack(count_rows)
        sums = sums + jnp.stack(sum_rows)
    valid = jnp.sum(mask.astype(jnp.float32))
    count_new = 0.99 * ema_count + 0.01 * counts
    sum_new = 0.99 * ema_sum + 0.01 * sums
    firsts = (encoder_first, latent_first, decoder_first, readout_first)
    seconds = (encoder_second, latent_second, decoder_second, readout_second)
    result = []
    for kind in range(4):
        result.extend(adamw(params[kind], grads[kind] / valid, firsts[kind], seconds[kind], RATES[kind]))
    return (loss_sum, valid, count_new, sum_new, result[0], result[1], result[2], result[3], result[4], result[5], result[6], result[7], result[8], result[9], result[10], result[11], result[12], result[13], result[14], result[15])
```

```python
import functools
import math

import jax
import jax.numpy as jnp
from jax import lax
from jax.experimental import pallas as pl
from jax.experimental.pallas import tpu as pltpu
from jax.sharding import PartitionSpec as P

CROP = 128
STEP = 5
RATES = (0.05, 0.03, 0.01, 0.03)

F32 = jnp.float32
BF = jnp.bfloat16
W = 128
NOBODY = 300.0

TAPS = 9 * 128
R_ET = TAPS
R_ZN = R_ET + 128
R_ZT = R_ZN + 128
R_OT = R_ZT + 64
R_BT = R_OT + 16
R_CODE = R_BT + 256
BIG = TAPS + 256
S_Z, S_E, S_O, S_X = 0, 64, 96, 112
SMALL = 128
EXACT = 5

NN = (((1,), (0,)), ((), ()))
NT = (((1,), (1,)), ((), ()))
VMEM = pl.BlockSpec(memory_space=pltpu.VMEM)
SMEM = pl.BlockSpec(memory_space=pltpu.SMEM)


def dot(a, b, dims=NN):
    return lax.dot_general(a, b, dims, preferred_element_type=F32)


def part(value, count):
    out = []
    for _ in range(count):
        piece = value.astype(BF)
        out.append(piece)
        value = value - piece.astype(F32)
    return out


def pack_kernel(
    place, image, mask, codes, count, total, enc, lat, dec, read,
    tile, near, across, pack, code_rows, flat,
):
    level = place[0]
    batches, _, band, _ = image.shape
    for b in range(batches):
        base = b * band * 8
        shown = image[b].astype(F32)
        for c in range(3):
            tile[pl.ds(base + c, band, stride=8), :] = shown[c]
        tile[pl.ds(base + 3, band, stride=8), :] = mask[b].astype(F32)
        code = codes[0, b]
        code = jnp.where(code < 256, code, code - 512).astype(F32)
        code_rows[b * band : (b + 1) * band] = code
        tile[pl.ds(base + 4, band, stride=8), :] = code
        for c in range(5, 8):
            tile[pl.ds(base + c, band, stride=8), :] = jnp.zeros((band, W), F32)
    ends = []
    for b in range(batches):
        row = jnp.where(level == 0, band - 2, 0)
        start = pl.multiple_of((b * band + row) * 8, 8)
        near[b * 16 : (b + 1) * 16] = tile[pl.ds(start, 16), :].astype(BF)
        for r in range(2):
            ends.append(
                jnp.where(
                    level == 0,
                    code_rows[b * band + r : b * band + r + 1],
                    code_rows[(b + 1) * band - 2 + r : (b + 1) * band - 1 + r],
                )
            )
    fill = across.shape[0] - len(ends)
    across[...] = jnp.concatenate(ends + [jnp.zeros((fill, W), F32)], 0).astype(BF)

    pack[0:TAPS] = dec[0].astype(BF)
    flat[...] = jnp.zeros_like(flat)
    for t in range(9):
        flat[8 * t : 8 * t + 3] = enc[0, 3 * t : 3 * t + 3]
    pack[R_ET : R_ET + 128] = flat[...].T.astype(BF)
    flat[...] = jnp.zeros_like(flat)
    flat[:, 0:64] = lat[0]
    pack[R_ZN : R_ZN + 128] = flat[...].astype(BF)
    pack[R_ZT : R_ZT + 64] = flat[...].T[0:64].astype(BF)
    flat[...] = jnp.zeros_like(flat)
    flat[:, 0:3] = read[0]
    pack[R_OT : R_OT + 16] = flat[...].T[0:16].astype(BF)
    for quarter in range(4):
        flat[:, 0:64] = total[0, quarter * 128 : (quarter + 1) * 128]
        book = flat[...].T[0:64] / count[0:1, quarter * 128 : (quarter + 1) * 128]
        row = R_BT + (quarter % 2) * 128 + (quarter // 2) * 64
        pack[row : row + 64] = book.astype(BF)
    pack[R_CODE : R_CODE + batches * band] = code_rows[...].astype(BF)


def sides(v):
    lane = lax.broadcasted_iota(jnp.int32, (v.shape[0], W), 1)
    before, after = [], []
    for i in range(v.shape[1] // W):
        row = v[:, i * W : (i + 1) * W]
        before.append(jnp.where(lane == 0, 0.0, pltpu.roll(row, 1, 1)))
        after.append(jnp.where(lane == W - 1, 0.0, pltpu.roll(row, W - 1, 1)))
    if len(before) == 1:
        return before[0], v, after[0]
    return jnp.concatenate(before, 1), v, jnp.concatenate(after, 1)


def at(row, rows):
    return pl.ds(pl.multiple_of(row * W, W), rows * W)


def fold(v, width):
    return sum(v[:, i : i + width] for i in range(0, v.shape[1], width))


def silu_parts(v):
    s = 0.5 * jnp.tanh(0.5 * v) + 0.5
    out = v * s
    return out, s + out * (1.0 - s)


def step_kernel(
    place, tile, near, across, mine, theirs,
    keep_big, keep_small, send,
    t_s, far_s, dn, dt, et, zn, zt, ot, on, bt,
    u_s, p_s, h_s, slope_s, gap_s, da_s, g_d, g_o, g_e, g_z, g_s, l_s,
    *, batches, rows, step_e, step_d, step_b,
):
    level, valid = place[0], place[1]
    band, ext = 2 * rows, rows + 4
    bottom = level == 1

    def pair(start, size):
        a, b = mine[start : start + size], theirs[start : start + size]
        return jnp.where(bottom, a, b), jnp.where(bottom, b, a)

    for t in range(9):
        one, zero = pair(t * 128, 128)
        zero = jnp.concatenate([jnp.zeros((64, 128), BF), zero[0:64]], 0)
        dn[t * 128 : (t + 1) * 128, 0:128] = one
        dn[t * 128 : (t + 1) * 128, 128:256] = zero
        dt[0:128, t * 128 : (t + 1) * 128] = one.astype(F32).T.astype(BF)
        dt[128:256, t * 128 : (t + 1) * 128] = zero.astype(F32).T.astype(BF)
    one, zero = pair(R_ET, 128)
    et[0:128], et[128:256] = one, zero
    one, zero = pair(R_ZN, 128)
    zn[0:128] = one
    zn[128:256] = pltpu.roll(zero.astype(F32), 64, 1).astype(BF)
    one, zero = pair(R_ZT, 64)
    blank = jnp.zeros((64, 128), BF)
    zt[0:64] = jnp.concatenate([one, blank], 1)
    zt[64:128] = jnp.concatenate([blank, zero], 1)
    one, zero = pair(R_OT, 16)
    blank = jnp.zeros((8, 128), F32)
    out_t = jnp.concatenate(
        [
            jnp.concatenate([one[0:8].astype(F32), blank], 1),
            jnp.concatenate([blank, zero[0:8].astype(F32)], 1),
        ],
        0,
    )
    ot[...] = out_t.astype(BF)
    on[...] = out_t.T.astype(BF)
    for half in range(2):
        one, zero = pair(R_BT + half * 128, 128)
        bt[0, :, half * 128 : (half + 1) * 128] = one
        bt[1, :, half * 128 : (half + 1) * 128] = zero

    far_s[0 : batches * band] = theirs[R_CODE : R_CODE + batches * band].astype(F32)
    far_s[batches * band : batches * band + across.shape[0]] = across[...].astype(F32)
    sub = lax.broadcasted_iota(jnp.int32, (8, W), 0)
    own_sub = jnp.where(bottom, 4, 5)

    def lay(b, e, shown, other):
        code = shown[4:5]
        t_s[b, e] = jnp.where(sub < 4, shown, jnp.where(sub == own_sub, code, other))

    def inner(i, _):
        b, e = i // (rows + 2), i % (rows + 2)
        row = b * band + level * (rows - 2) + e
        lay(
            b,
            e + jnp.where(bottom, 0, 2),
            tile[pl.ds(pl.multiple_of(row * 8, 8), 8), :],
            far_s[pl.ds(row, 1), :],
        )
        return 0

    lax.fori_loop(0, batches * (rows + 2), inner, 0, unroll=2)
    for b in range(batches):
        both = near[b * 16 : (b + 1) * 16].astype(F32)
        for r in range(2):
            row = batches * band + b * 2 + r
            shown = jnp.where(valid > 0, both[r * 8 : (r + 1) * 8], jnp.where(sub == 4, NOBODY, 0.0))
            other = jnp.where(valid > 0, far_s[row : row + 1], NOBODY)
            lay(b, jnp.where(bottom, rows + 2 + r, r), shown, other)

    for ref in (g_d, g_o, g_e, g_z, g_s, l_s):
        ref[...] = jnp.zeros_like(ref)

    def patch(i, _):
        b, e = i // rows, i % rows + 2
        views = [view for dr in range(3) for view in sides(t_s[b, e + dr - 1])]
        value = jnp.concatenate(views + [jnp.zeros((56, W), F32)], 0)
        p_s[:, at(i, 1)] = value.astype(BF)
        return 0

    lax.fori_loop(0, batches * rows, patch, 0, unroll=2)

    def lookup(b, e, n):
        here = jnp.concatenate([t_s[b, e + i] for i in range(n)], 1)
        ids = lax.broadcasted_iota(jnp.int32, (256, n * W), 0).astype(F32)
        quants, onehots, highs = [], [], []
        for v in range(2):
            code = here[4 + v : 5 + v]
            high = code < 0.0
            low = jnp.where(high, code + 256.0, code)
            onehot = jnp.where(ids == low, 1.0, 0.0).astype(BF)
            both = dot(bt[v], onehot)
            quants.append(jnp.where(high, both[64:128], both[0:64]))
            onehots.append(onehot)
            highs.append(high)
        u = jnp.concatenate(quants, 0)
        for k, view in enumerate(sides(u)):
            u_s[k, :, at(b * ext + e, n)] = view.astype(BF)
        return here, u, onehots, highs

    def outer(i, _):
        lookup(i // 2, (i % 2) * (rows + 2), 2)
        return 0

    lax.fori_loop(0, batches * 2, outer, 0)

    def encode(i, _):
        n = step_e
        b, e = i // (rows // n), (i % (rows // n)) * n + 2
        here, u, onehots, highs = lookup(b, e, n)
        own = at(i * n, n)
        h, slope = silu_parts(dot(et[...], p_s[:, own]))
        slope_s[:, own] = slope
        h = h.astype(BF)
        h_s[:, own] = h
        z = dot(zt[...], h)
        k = here[3:4]
        gap = z - u
        kept = k * gap
        l_s[0:128] += fold(kept * gap, 256)
        gap_s[:, own] = 0.5 * kept
        z = k * z.astype(BF).astype(F32)
        row = lax.broadcasted_iota(jnp.int32, (16, n * W), 0)
        for v in range(2):
            part_z = z[v * 64 : v * 64 + 64]
            low_k = jnp.where(highs[v], 0.0, k)
            high_k = jnp.where(highs[v], k, 0.0)
            left = jnp.concatenate(
                [
                    jnp.where(highs[v], 0.0, part_z),
                    jnp.where(highs[v], part_z, 0.0),
                    jnp.where(row == 0, low_k, jnp.where(row == 1, high_k, 0.0)),
                ],
                0,
            ).astype(BF)
            g_s[v] += dot(left, onehots[v], NT)
        return 0

    lax.fori_loop(0, batches * (rows // step_e), encode, 0)

    def decode(b, spans, own):
        views = []
        for dr in range(3):
            for dc in range(3):
                runs = [u_s[dc, :, at(b * ext + e + dr - 1, n)] for e, n in spans]
                views.append(runs[0] if len(runs) == 1 else jnp.concatenate(runs, 1))
        u = jnp.concatenate(views, 0)
        g, slope = silu_parts(dot(dt[...], u))
        g = g.astype(BF)
        y = dot(ot[...], g)
        here = jnp.concatenate([t_s[b, e + i] for e, n in spans for i in range(n)], 1)
        k = here[3:4]
        x = jnp.where(lax.broadcasted_iota(jnp.int32, here.shape, 0) < 3, here, 0.0)
        diff = y - jnp.concatenate([x, x], 0)
        kept = k * diff
        dy = (2.0 * kept).astype(BF)
        da = dot(on[...], dy) * slope
        for dc, view in enumerate(sides(da)):
            first = 0
            for e, n in spans:
                da_s[dc, :, at(b * (rows + 2) + e - 1, n)] = view[:, first : first + n * W].astype(BF)
                first += n * W
        if own:
            l_s[128:144] += fold(kept * diff, 256)
            g_o[...] += dot(dy, g, NT)
            g_d[...] += dot(u, da.astype(BF), NT)

    def edge(b, _):
        decode(b, [(1, 1), (rows + 2, 1)], False)
        return 0

    lax.fori_loop(0, batches, edge, 0)

    def middle(i, _):
        n = step_d
        decode(i // (rows // n), [((i % (rows // n)) * n + 2, n)], True)
        return 0

    lax.fori_loop(0, batches * (rows // step_d), middle, 0)

    def back(i, _):
        n = step_b
        b, r = i // (rows // n), (i % (rows // n)) * n
        own = at(i * n, n)
        du = jnp.zeros((128, n * W), F32)
        for dr in range(3):
            for dc in range(3):
                t = 3 * dr + dc
                view = da_s[2 - dc, :, at(b * (rows + 2) + r + 2 - dr, n)]
                du = du + dot(dn[t * 128 : (t + 1) * 128], view)
        dz = (du + gap_s[:, own]).astype(BF)
        g_z[...] += dot(dz, h_s[:, own], NT)
        dpre = (dot(zn[...], dz) * slope_s[:, own]).astype(BF)
        g_e[...] += dot(p_s[:, own], dpre, NT)
        return 0

    lax.fori_loop(0, batches * (rows // step_b), back, 0)

    def give(start, one, zero, keep, offset):
        n = one.shape[0]
        keep[start : start + n] = jnp.where(bottom, one, zero).astype(keep.dtype)
        send[offset + start : offset + start + n] = jnp.where(bottom, zero, one).astype(BF)

    for t in range(9):
        top = jnp.concatenate([g_d[t * 128 + 64 : (t + 1) * 128, 128:256], jnp.zeros((64, 128), F32)], 0)
        give(t * 128, g_d[t * 128 : (t + 1) * 128, 0:128], top, keep_big, 0)
    for half in range(2):
        cols = slice(half * 128, (half + 1) * 128)
        give(TAPS + half * 128, g_s[0, 0:128, cols], g_s[1, 0:128, cols], keep_big, 0)
    give(S_Z, g_z[0:64, 0:128], g_z[64:128, 128:256], keep_small, BIG)
    enc = []
    for cols in (slice(0, 128), slice(128, 256)):
        runs = [g_e[8 * t : 8 * t + 3, cols] for t in range(9)]
        enc.append(jnp.concatenate(runs + [jnp.zeros((5, 128), F32)], 0))
    give(S_E, enc[0], enc[1], keep_small, BIG)
    blank = jnp.zeros((8, 128), F32)
    give(
        S_O,
        jnp.concatenate([g_o[0:8, 0:128], blank], 0),
        jnp.concatenate([g_o[8:16, 128:256], blank], 0),
        keep_small,
        BIG,
    )
    valid_sum = jnp.sum(g_s[0, 128:130])
    loss = 0.25 * jnp.sum(l_s[0:128]) + jnp.sum(l_s[128:144])
    lane = lax.broadcasted_iota(jnp.int32, (1, W), 1)
    other = jnp.where(lane == 0, loss, jnp.where(lane == 1, valid_sum, 0.0))
    exact = []
    for v in range(2):
        runs = [g_s[v, 128 + hi : 129 + hi, half * 128 : (half + 1) * 128] for hi in range(2) for half in range(2)]
        pieces = part(jnp.concatenate(runs + [other], 0), 3)
        exact.append(jnp.concatenate([p.astype(F32) for p in pieces] + [jnp.zeros((1, 128), F32)], 0))
    give(S_X, exact[0], exact[1], keep_small, BIG)


def update_kernel(
    order, *refs, stages
):
    (parts, refs) = refs[:stages], refs[stages:]
    (count, total, ew, e1, e2, zw, z1, z2, dw, d1, d2, ow, o1, o2,
     loss_out, valid_out, count_out, total_out,
     em, es, ep, ec, zm, zs, zp, zc, dm, ds, dp, dc, om, os, op, oc, big, flat) = refs
    share = BIG // stages
    small = jnp.zeros((SMALL, W), F32)
    for n, ref in enumerate(parts):
        big[pl.ds(pl.multiple_of(order[n] * share, 16), share), :] = ref[0:share].astype(F32)
        small = small + ref[share : share + SMALL].astype(F32)
    exact = sum(small[S_X + EXACT * i : S_X + EXACT * (i + 1)] for i in range(3))
    loss = jnp.sum(exact[4:5, 0:1])
    valid = jnp.sum(exact[4:5, 1:2])
    loss_out[0, 0] = loss
    valid_out[0, 0] = valid
    counts = jnp.concatenate([exact[i : i + 1] for i in range(4)], 1)
    count_out[...] = 0.99 * count[...] + 0.01 * counts
    for quarter in range(4):
        row = TAPS + (quarter % 2) * 128 + (quarter // 2) * 64
        flat[0:64] = big[row : row + 64]
        rows = slice(quarter * 128, (quarter + 1) * 128)
        total_out[0, rows] = 0.99 * total[0, rows] + 0.01 * flat[...].T[:, 0:64]

    scale = 1.0 - 0.5**STEP

    def adamw(grad, w, first, second, rate, outs):
        grad = grad / valid
        moment = 0.5 * first[0] + 0.5 * grad
        square = 0.5 * second[0] + 0.5 * grad * grad
        weight = w[0]
        master = weight - rate * (moment / scale / (jnp.sqrt(square / scale) + 1e-08) + 0.01 * weight)
        outs[0][0] = moment
        outs[1][0] = square
        outs[2][0] = master
        outs[3][0] = master.astype(BF)

    adamw(small[S_E : S_E + 27], ew, e1, e2, RATES[0], (em, es, ep, ec))
    flat[0:64] = small[S_Z : S_Z + 64]
    adamw(flat[...].T[:, 0:64], zw, z1, z2, RATES[1], (zm, zs, zp, zc))
    adamw(big[0:TAPS], dw, d1, d2, RATES[2], (dm, ds, dp, dc))
    flat[0:16] = small[S_O : S_O + 16]
    adamw(flat[...].T[:, 0:3], ow, o1, o2, RATES[3], (om, os, op, oc))


def radices(devices):
    bits = devices.bit_length() - 1
    return [(start, min(2, bits - start)) for start in range(0, bits, 2)]


def partners(start, width):
    return [k << start for k in range(1, 1 << width)]


def xor_pairs(devices, by):
    return [(i, i ^ by) for i in range(devices)]


def lowered(value):
    return lax.reduce_precision(value, 8, 7)


def sum_small(parts):
    total = sum(item.astype(F32) for item in parts)
    value = sum(total[S_X + EXACT * i : S_X + EXACT * (i + 1)] for i in range(3))
    high = lowered(value)
    middle = lowered(value - high)
    low = value - high - middle
    rest = total[S_X + 3 * EXACT :]
    return jnp.concatenate([total[:S_X], high, middle, low, rest], 0).astype(BF)


def local(
    image, mask, codes, ema_count, ema_sum,
    encoder_weight, encoder_first, encoder_second,
    latent_weight, latent_first, latent_second,
    decoder_weight, decoder_first, decoder_second,
    readout_weight, readout_first, readout_second,
):
    batches, _, band, width = image.shape
    rows = band // 2
    level, me = lax.axis_index("level"), lax.axis_index("dp")
    devices = lax.axis_size("dp")
    row_first = me * band + band
    top_ok = (row_first % CROP != 0) & (me > 0)
    bottom_ok = ((row_first + band) % CROP != 0) & (me < devices - 1)
    valid = jnp.where(level == 0, top_ok, bottom_ok)
    place = jnp.stack([level, valid.astype(jnp.int32)]).astype(jnp.int32)

    limit = pltpu.CompilerParams(vmem_limit_bytes=56 * 1024 * 1024)
    packed = R_CODE + batches * band
    tile, near, across, pack = pl.pallas_call(
        pack_kernel,
        out_shape=[
            jax.ShapeDtypeStruct((batches * band * 8, W), F32),
            jax.ShapeDtypeStruct((batches * 16, W), BF),
            jax.ShapeDtypeStruct((16, W), BF),
            jax.ShapeDtypeStruct((packed, W), BF),
        ],
        in_specs=[SMEM] + [VMEM] * 9,
        out_specs=[VMEM] * 4,
        scratch_shapes=[pltpu.VMEM((batches * band, W), F32), pltpu.VMEM((128, 128), F32)],
        compiler_params=limit,
    )(place, image, mask, codes, ema_count, ema_sum, encoder_weight, latent_weight, decoder_weight, readout_weight)

    both = ("level", "dp")
    same = [(d - 1, d) for d in range(1, devices)] + [(devices + d + 1, devices + d) for d in range(devices - 1)]
    cross = [(devices + d - 1, d) for d in range(1, devices)] + [(d + 1, devices + d) for d in range(devices - 1)]
    near = lax.ppermute(near, both, same)
    across = lax.ppermute(across, both, cross)
    theirs = lax.ppermute(pack, "level", [(0, 1), (1, 0)])

    ext = rows + 4
    pixels = batches * rows * W
    keep_big, keep_small, send = pl.pallas_call(
        functools.partial(step_kernel, batches=batches, rows=rows, step_e=rows, step_d=rows, step_b=rows // 2),
        out_shape=[
            jax.ShapeDtypeStruct((BIG, W), F32),
            jax.ShapeDtypeStruct((SMALL, W), BF),
            jax.ShapeDtypeStruct((BIG + SMALL, W), BF),
        ],
        in_specs=[SMEM] + [VMEM] * 5,
        out_specs=[VMEM] * 3,
        scratch_shapes=[
            pltpu.VMEM((batches, ext, 8, W), F32),
            pltpu.VMEM((batches * band + 16, W), F32),
            pltpu.VMEM((TAPS, 256), BF),
            pltpu.VMEM((256, TAPS), BF),
            pltpu.VMEM((256, 128), BF),
            pltpu.VMEM((256, 128), BF),
            pltpu.VMEM((128, 256), BF),
            pltpu.VMEM((16, 256), BF),
            pltpu.VMEM((256, 16), BF),
            pltpu.VMEM((2, 128, 256), BF),
            pltpu.VMEM((3, 128, batches * ext * W), BF),
            pltpu.VMEM((128, pixels), BF),
            pltpu.VMEM((256, pixels), BF),
            pltpu.VMEM((256, pixels), F32),
            pltpu.VMEM((128, pixels), F32),
            pltpu.VMEM((3, 256, batches * (rows + 2) * W), BF),
            pltpu.VMEM((TAPS, 256), F32),
            pltpu.VMEM((16, 256), F32),
            pltpu.VMEM((128, 256), F32),
            pltpu.VMEM((128, 256), F32),
            pltpu.VMEM((2, 144, 256), F32),
            pltpu.VMEM((144, 256), F32),
        ],
        compiler_params=limit,
    )(place, tile, near, across, pack, theirs)

    got = lax.ppermute(send, "level", [(0, 1), (1, 0)])
    small = sum_small([keep_small, got[BIG:]])
    big = keep_big + got[:BIG].astype(F32)

    stages = radices(devices)
    for start, width_bits in stages:
        count = 1 << width_bits
        index = (me >> start) & (count - 1)
        pieces = big.reshape(count, -1, W)
        total = lax.dynamic_index_in_dim(pieces, index, 0, False)
        for k in range(count - 1, 0, -1):
            out = lax.dynamic_index_in_dim(pieces, index ^ k, 0, False).astype(BF)
            total = total + lax.ppermute(out, "dp", xor_pairs(devices, k << start)).astype(F32)
        big = total
    big = big.astype(BF)
    for number, (start, width_bits) in enumerate(reversed(stages)):
        count = 1 << width_bits
        index = (me >> start) & (count - 1)
        payload = jnp.concatenate([big, small], 0)
        parts = [payload] + [lax.ppermute(payload, "dp", xor_pairs(devices, k << start)) for k in range(1, count)]
        order = jnp.stack([index ^ k for k in range(count)]).astype(jnp.int32)
        if number == len(stages) - 1:
            break
        size = big.shape[0]
        stacked = jnp.zeros((count, size, W), BF)
        for k in range(count):
            stacked = lax.dynamic_update_index_in_dim(stacked, parts[k][:size], index ^ k, 0)
        big = stacked.reshape(count * size, W)
        small = sum_small([item[size:] for item in parts])

    state = (
        ema_count, ema_sum,
        encoder_weight, encoder_first, encoder_second, latent_weight, latent_first, latent_second,
        decoder_weight, decoder_first, decoder_second, readout_weight, readout_first, readout_second,
    )
    outs = [jax.ShapeDtypeStruct((1, 1), F32)] * 2
    outs += [jax.ShapeDtypeStruct(ema_count.shape, F32), jax.ShapeDtypeStruct(ema_sum.shape, F32)]
    for item in (encoder_weight, latent_weight, decoder_weight, readout_weight):
        outs += [jax.ShapeDtypeStruct(item.shape, F32)] * 3 + [jax.ShapeDtypeStruct(item.shape, BF)]
    result = pl.pallas_call(
        functools.partial(update_kernel, stages=len(parts)),
        out_shape=outs,
        in_specs=[SMEM] + [VMEM] * (len(parts) + len(state)),
        out_specs=[SMEM] * 2 + [VMEM] * (len(outs) - 2),
        scratch_shapes=[pltpu.VMEM((BIG, W), F32), pltpu.VMEM((128, 128), F32)],
        compiler_params=limit,
    )(order, *parts, *state)
    return (result[0].reshape(()), result[1].reshape(()), *result[2:])


def solution(mesh):
    rank = (0, 0, 2, 3) + (3,) * 16
    in_specs = (P(None, None, "dp", None), P(None, "dp", None), P("level", None, "dp", None), P("level", None))
    in_specs += (P("level", None, None),) * 13
    out_specs = tuple(P(*(("level",) + (None,) * (n - 1) if n else ())) for n in rank)
    return jax.shard_map(local, mesh=mesh, in_specs=in_specs, out_specs=out_specs, check_vma=False)
```

```python
import functools

import jax
import jax.numpy as jnp
from jax import lax
from jax.experimental import pallas as pl
from jax.experimental.pallas import tpu as pltpu
from jax.sharding import PartitionSpec as P

CROP = 128
STEP = 5
RATES = (0.05, 0.03, 0.01, 0.03)

F32 = jnp.float32
BF = jnp.bfloat16
W = 128
NOBODY = 300.0

TAPS = 9 * 128
R_ET = TAPS
R_ZN = R_ET + 128
R_ZT = R_ZN + 128
R_OT = R_ZT + 64
R_BT = R_OT + 16
R_CODE = R_BT + 256
BIG = TAPS + 256
S_Z, S_E, S_O, S_X = 0, 64, 96, 112
SMALL = 128
EXACT = 5

NN = (((1,), (0,)), ((), ()))
NT = (((1,), (1,)), ((), ()))
VMEM = pl.BlockSpec(memory_space=pltpu.VMEM)
SMEM = pl.BlockSpec(memory_space=pltpu.SMEM)


def dot(a, b, dims=NN):
    return lax.dot_general(a, b, dims, preferred_element_type=F32)


def part(value, count):
    out = []
    for _ in range(count):
        piece = value.astype(BF)
        out.append(piece)
        value = value - piece.astype(F32)
    return out


def pack_kernel(
    image, mask, codes, count, total, enc, lat, dec, read,
    tile, near, across, pack, code_rows, flat,
):
    level = lax.axis_index("level")
    batches, _, band, _ = image.shape
    for b in range(batches):
        base = b * band * 8
        shown = image[b].astype(F32)
        for c in range(3):
            tile[pl.ds(base + c, band, stride=8), :] = shown[c]
        tile[pl.ds(base + 3, band, stride=8), :] = mask[b].astype(F32)
        code = codes[0, b]
        code = jnp.where(code < 256, code, code - 512).astype(F32)
        code_rows[b * band : (b + 1) * band] = code
        tile[pl.ds(base + 4, band, stride=8), :] = code
        for c in range(5, 8):
            tile[pl.ds(base + c, band, stride=8), :] = jnp.zeros((band, W), F32)
    ends = []
    for b in range(batches):
        row = jnp.where(level == 0, band - 2, 0)
        start = pl.multiple_of((b * band + row) * 8, 8)
        near[b * 16 : (b + 1) * 16] = tile[pl.ds(start, 16), :].astype(BF)
        for r in range(2):
            ends.append(
                jnp.where(
                    level == 0,
                    code_rows[b * band + r : b * band + r + 1],
                    code_rows[(b + 1) * band - 2 + r : (b + 1) * band - 1 + r],
                )
            )
    fill = across.shape[0] - len(ends)
    across[...] = jnp.concatenate(ends + [jnp.zeros((fill, W), F32)], 0).astype(BF)

    pack[0:TAPS] = dec[0].astype(BF)
    flat[...] = jnp.zeros_like(flat)
    for t in range(9):
        for c in range(3):
            flat[8 * t + c : 8 * t + c + 1] = enc[3 * t + c]
    pack[R_ET : R_ET + 128] = flat[...].T.astype(BF)
    flat[...] = jnp.zeros_like(flat)
    flat[0:64] = lat[0]
    pack[R_ZT : R_ZT + 64] = lat[0].astype(BF)
    pack[R_ZN : R_ZN + 128] = flat[...].T.astype(BF)
    blank = jnp.zeros((13, 128), F32)
    pack[R_OT : R_OT + 16] = jnp.concatenate([read[0], read[1], read[2], blank], 0).astype(BF)
    book = total[0] / count[...]
    for quarter in range(4):
        row = R_BT + (quarter % 2) * 128 + (quarter // 2) * 64
        pack[row : row + 64] = book[:, quarter * 128 : (quarter + 1) * 128].astype(BF)
    pack[R_CODE : R_CODE + batches * band] = code_rows[...].astype(BF)


def sides(v):
    lane = lax.broadcasted_iota(jnp.int32, (v.shape[0], W), 1)
    before, after = [], []
    for i in range(v.shape[1] // W):
        row = v[:, i * W : (i + 1) * W]
        before.append(jnp.where(lane == 0, 0.0, pltpu.roll(row, 1, 1)))
        after.append(jnp.where(lane == W - 1, 0.0, pltpu.roll(row, W - 1, 1)))
    if len(before) == 1:
        return before[0], v, after[0]
    return jnp.concatenate(before, 1), v, jnp.concatenate(after, 1)


def at(row, rows):
    return pl.ds(pl.multiple_of(row * W, W), rows * W)


def fold(v, width):
    return sum(v[:, i : i + width] for i in range(0, v.shape[1], width))


def silu_parts(v):
    s = 0.5 * jnp.tanh(0.5 * v) + 0.5
    out = v * s
    return out, s + out * (1.0 - s)


def step_kernel(
    tile, near, across, mine, theirs,
    keep_big, keep_small, send,
    t_s, far_s, dn, dt, et, zn, zt, ot, on, bt,
    u_s, p_s, h_s, slope_s, gap_s, da_s, g_d, g_o, g_e, g_z, g_s, l_s,
    *, batches, rows, step_e, step_d, step_b,
):
    level, me, devices = lax.axis_index("level"), lax.axis_index("dp"), lax.axis_size("dp")
    band, ext = 2 * rows, rows + 4
    above, below = (me + 1) * band, (me + 2) * band
    top_ok = (lax.rem(above, CROP) != 0) & (me > 0)
    bottom_ok = (lax.rem(below, CROP) != 0) & (me < devices - 1)
    valid = jnp.where(level == 0, top_ok.astype(jnp.int32), bottom_ok.astype(jnp.int32))
    bottom = level == 1

    def pair(start, size):
        a, b = mine[start : start + size], theirs[start : start + size]
        return jnp.where(bottom, a, b), jnp.where(bottom, b, a)

    for t in range(9):
        one, zero = pair(t * 128, 128)
        zero = jnp.concatenate([jnp.zeros((64, 128), BF), zero[0:64]], 0)
        dn[t * 128 : (t + 1) * 128, 0:128] = one
        dn[t * 128 : (t + 1) * 128, 128:256] = zero
        dt[0:128, t * 128 : (t + 1) * 128] = one.astype(F32).T.astype(BF)
        dt[128:256, t * 128 : (t + 1) * 128] = zero.astype(F32).T.astype(BF)
    one, zero = pair(R_ET, 128)
    et[0:128], et[128:256] = one, zero
    one, zero = pair(R_ZN, 128)
    zn[0:128] = one
    zn[128:256] = pltpu.roll(zero.astype(F32), 64, 1).astype(BF)
    one, zero = pair(R_ZT, 64)
    blank = jnp.zeros((64, 128), BF)
    zt[0:64] = jnp.concatenate([one, blank], 1)
    zt[64:128] = jnp.concatenate([blank, zero], 1)
    one, zero = pair(R_OT, 16)
    blank = jnp.zeros((8, 128), F32)
    out_t = jnp.concatenate(
        [
            jnp.concatenate([one[0:8].astype(F32), blank], 1),
            jnp.concatenate([blank, zero[0:8].astype(F32)], 1),
        ],
        0,
    )
    ot[...] = out_t.astype(BF)
    on[...] = out_t.T.astype(BF)
    for half in range(2):
        one, zero = pair(R_BT + half * 128, 128)
        bt[0, :, half * 128 : (half + 1) * 128] = one
        bt[1, :, half * 128 : (half + 1) * 128] = zero

    far_s[0 : batches * band] = theirs[R_CODE : R_CODE + batches * band].astype(F32)
    far_s[batches * band : batches * band + across.shape[0]] = across[...].astype(F32)
    sub = lax.broadcasted_iota(jnp.int32, (8, W), 0)
    own_sub = jnp.where(bottom, 4, 5)

    def lay(b, e, shown, other):
        code = shown[4:5]
        t_s[b, e] = jnp.where(sub < 4, shown, jnp.where(sub == own_sub, code, other))

    def inner(i, _):
        b, e = i // (rows + 2), i % (rows + 2)
        row = b * band + level * (rows - 2) + e
        lay(
            b,
            e + jnp.where(bottom, 0, 2),
            tile[pl.ds(pl.multiple_of(row * 8, 8), 8), :],
            far_s[pl.ds(row, 1), :],
        )
        return 0

    lax.fori_loop(0, batches * (rows + 2), inner, 0, unroll=2)
    for b in range(batches):
        both = near[b * 16 : (b + 1) * 16].astype(F32)
        for r in range(2):
            row = batches * band + b * 2 + r
            shown = jnp.where(valid > 0, both[r * 8 : (r + 1) * 8], jnp.where(sub == 4, NOBODY, 0.0))
            other = jnp.where(valid > 0, far_s[row : row + 1], NOBODY)
            lay(b, jnp.where(bottom, rows + 2 + r, r), shown, other)

    for ref in (g_d, g_o, g_e, g_z, g_s, l_s):
        ref[...] = jnp.zeros_like(ref)

    def patch(i, _):
        b, e = i // rows, i % rows + 2
        views = [view for dr in range(3) for view in sides(t_s[b, e + dr - 1])]
        value = jnp.concatenate(views + [jnp.zeros((56, W), F32)], 0)
        p_s[:, at(i, 1)] = value.astype(BF)
        return 0

    lax.fori_loop(0, batches * rows, patch, 0, unroll=2)

    def lookup(b, e, n):
        here = jnp.concatenate([t_s[b, e + i] for i in range(n)], 1)
        ids = lax.broadcasted_iota(jnp.int32, (256, n * W), 0).astype(F32)
        quants, onehots, highs = [], [], []
        for v in range(2):
            code = here[4 + v : 5 + v]
            high = code < 0.0
            low = jnp.where(high, code + 256.0, code)
            onehot = jnp.where(ids == low, 1.0, 0.0).astype(BF)
            both = dot(bt[v], onehot)
            quants.append(jnp.where(high, both[64:128], both[0:64]))
            onehots.append(onehot)
            highs.append(high)
        u = jnp.concatenate(quants, 0)
        for k, view in enumerate(sides(u)):
            u_s[k, :, at(b * ext + e, n)] = view.astype(BF)
        return here, u, onehots, highs

    def outer(i, _):
        lookup(i // 2, (i % 2) * (rows + 2), 2)
        return 0

    lax.fori_loop(0, batches * 2, outer, 0)

    def encode(i, _):
        n = step_e
        b, e = i // (rows // n), (i % (rows // n)) * n + 2
        here, u, onehots, highs = lookup(b, e, n)
        own = at(i * n, n)
        h, slope = silu_parts(dot(et[...], p_s[:, own]))
        slope_s[:, own] = slope
        h = h.astype(BF)
        h_s[:, own] = h
        z = dot(zt[...], h)
        k = here[3:4]
        gap = z - u
        kept = k * gap
        l_s[0:128] += fold(kept * gap, 256)
        gap_s[:, own] = 0.5 * kept
        z = k * z.astype(BF).astype(F32)
        row = lax.broadcasted_iota(jnp.int32, (16, n * W), 0)
        for v in range(2):
            part_z = z[v * 64 : v * 64 + 64]
            low_k = jnp.where(highs[v], 0.0, k)
            high_k = jnp.where(highs[v], k, 0.0)
            left = jnp.concatenate(
                [
                    jnp.where(highs[v], 0.0, part_z),
                    jnp.where(highs[v], part_z, 0.0),
                    jnp.where(row == 0, low_k, jnp.where(row == 1, high_k, 0.0)),
                ],
                0,
            ).astype(BF)
            g_s[v] += dot(left, onehots[v], NT)
        return 0

    lax.fori_loop(0, batches * (rows // step_e), encode, 0)

    def decode(b, spans, own):
        views = []
        for dr in range(3):
            for dc in range(3):
                runs = [u_s[dc, :, at(b * ext + e + dr - 1, n)] for e, n in spans]
                views.append(runs[0] if len(runs) == 1 else jnp.concatenate(runs, 1))
        u = jnp.concatenate(views, 0)
        g, slope = silu_parts(dot(dt[...], u))
        g = g.astype(BF)
        y = dot(ot[...], g)
        here = jnp.concatenate([t_s[b, e + i] for e, n in spans for i in range(n)], 1)
        k = here[3:4]
        x = jnp.where(lax.broadcasted_iota(jnp.int32, here.shape, 0) < 3, here, 0.0)
        diff = y - jnp.concatenate([x, x], 0)
        kept = k * diff
        dy = (2.0 * kept).astype(BF)
        da = dot(on[...], dy) * slope
        for dc, view in enumerate(sides(da)):
            first = 0
            for e, n in spans:
                da_s[dc, :, at(b * (rows + 2) + e - 1, n)] = view[:, first : first + n * W].astype(BF)
                first += n * W
        if own:
            l_s[128:144] += fold(kept * diff, 256)
            g_o[...] += dot(dy, g, NT)
            g_d[...] += dot(u, da.astype(BF), NT)

    def edge(b, _):
        decode(b, [(1, 1), (rows + 2, 1)], False)
        return 0

    lax.fori_loop(0, batches, edge, 0)

    def middle(i, _):
        n = step_d
        decode(i // (rows // n), [((i % (rows // n)) * n + 2, n)], True)
        return 0

    lax.fori_loop(0, batches * (rows // step_d), middle, 0)

    def back(i, _):
        n = step_b
        b, r = i // (rows // n), (i % (rows // n)) * n
        own = at(i * n, n)
        du = jnp.zeros((128, n * W), F32)
        for dr in range(3):
            for dc in range(3):
                t = 3 * dr + dc
                view = da_s[2 - dc, :, at(b * (rows + 2) + r + 2 - dr, n)]
                du = du + dot(dn[t * 128 : (t + 1) * 128], view)
        dz = (du + gap_s[:, own]).astype(BF)
        g_z[...] += dot(dz, h_s[:, own], NT)
        dpre = (dot(zn[...], dz) * slope_s[:, own]).astype(BF)
        g_e[...] += dot(p_s[:, own], dpre, NT)
        return 0

    lax.fori_loop(0, batches * (rows // step_b), back, 0)

    def give(start, one, zero, keep, offset):
        n = one.shape[0]
        keep[start : start + n] = jnp.where(bottom, one, zero).astype(keep.dtype)
        send[offset + start : offset + start + n] = jnp.where(bottom, zero, one).astype(BF)

    for t in range(9):
        top = jnp.concatenate([g_d[t * 128 + 64 : (t + 1) * 128, 128:256], jnp.zeros((64, 128), F32)], 0)
        give(t * 128, g_d[t * 128 : (t + 1) * 128, 0:128], top, keep_big, 0)
    for half in range(2):
        cols = slice(half * 128, (half + 1) * 128)
        give(TAPS + half * 128, g_s[0, 0:128, cols], g_s[1, 0:128, cols], keep_big, 0)
    give(S_Z, g_z[0:64, 0:128], g_z[64:128, 128:256], keep_small, BIG)
    enc = []
    for cols in (slice(0, 128), slice(128, 256)):
        runs = [g_e[8 * t : 8 * t + 3, cols] for t in range(9)]
        enc.append(jnp.concatenate(runs + [jnp.zeros((5, 128), F32)], 0))
    give(S_E, enc[0], enc[1], keep_small, BIG)
    blank = jnp.zeros((8, 128), F32)
    give(
        S_O,
        jnp.concatenate([g_o[0:8, 0:128], blank], 0),
        jnp.concatenate([g_o[8:16, 128:256], blank], 0),
        keep_small,
        BIG,
    )
    valid_sum = jnp.sum(g_s[0, 128:130])
    loss = 0.25 * jnp.sum(l_s[0:128]) + jnp.sum(l_s[128:144])
    lane = lax.broadcasted_iota(jnp.int32, (1, W), 1)
    other = jnp.where(lane == 0, loss, jnp.where(lane == 1, valid_sum, 0.0))
    exact = []
    for v in range(2):
        runs = [g_s[v, 128 + hi : 129 + hi, half * 128 : (half + 1) * 128] for hi in range(2) for half in range(2)]
        pieces = part(jnp.concatenate(runs + [other], 0), 3)
        exact.append(jnp.concatenate([p.astype(F32) for p in pieces] + [jnp.zeros((1, 128), F32)], 0))
    give(S_X, exact[0], exact[1], keep_small, BIG)


def update_kernel(
    *refs, stages, start
):
    (parts, refs) = refs[:stages], refs[stages:]
    (count, total, ew, e1, e2, zw, z1, z2, dw, d1, d2, ow, o1, o2,
     loss_out, valid_out, count_out, total_out,
     em, es, ep, ec, zm, zs, zp, zc, dm, ds, dp, dc, om, os, op, oc, big, rows) = refs
    share = BIG // stages
    index = (lax.axis_index("dp") >> start) & (stages - 1)
    small = jnp.zeros((SMALL, W), F32)
    for n, ref in enumerate(parts):
        big[pl.ds(pl.multiple_of((index ^ n) * share, 16), share), :] = ref[0:share].astype(F32)
        small = small + ref[share : share + SMALL].astype(F32)
    exact = sum(small[S_X + EXACT * i : S_X + EXACT * (i + 1)] for i in range(3))
    loss = jnp.sum(exact[4:5, 0:1])
    valid = jnp.sum(exact[4:5, 1:2])
    loss_out[0, 0] = loss
    valid_out[0, 0] = valid
    counts = jnp.concatenate([exact[i : i + 1] for i in range(4)], 1)
    count_out[...] = 0.99 * count[...] + 0.01 * counts
    for quarter in range(4):
        row = TAPS + (quarter % 2) * 128 + (quarter // 2) * 64
        cols = slice(quarter * 128, (quarter + 1) * 128)
        total_out[0, :, cols] = 0.99 * total[0, :, cols] + 0.01 * big[row : row + 64]

    scale = 1.0 - 0.5**STEP

    def adamw(grad, weight, first, second, rate):
        grad = grad / valid
        moment = 0.5 * first + 0.5 * grad
        square = 0.5 * second + 0.5 * grad * grad
        master = weight - rate * (moment / scale / (jnp.sqrt(square / scale) + 1e-08) + 0.01 * weight)
        return moment, square, master

    def whole(grad, w, first, second, rate, outs):
        outs[0][0], outs[1][0], master = adamw(grad, w[0], first[0], second[0], rate)
        outs[2][0] = master
        outs[3][0] = master.astype(BF)

    def by_row(grad, w, first, second, rate, outs):
        n = w.shape[0]
        for i in range(n):
            outs[0][i], outs[1][i], master = adamw(grad[i : i + 1], w[i], first[i], second[i], rate)
            outs[2][i] = master
            rows[i : i + 1] = master
        outs[3][0] = rows[0:n].astype(BF)

    by_row(small[S_E : S_E + 27], ew, e1, e2, RATES[0], (em, es, ep, ec))
    whole(small[S_Z : S_Z + 64], zw, z1, z2, RATES[1], (zm, zs, zp, zc))
    whole(big[0:TAPS], dw, d1, d2, RATES[2], (dm, ds, dp, dc))
    by_row(small[S_O : S_O + 3], ow, o1, o2, RATES[3], (om, os, op, oc))


def radices(devices):
    bits = devices.bit_length() - 1
    return [(start, min(2, bits - start)) for start in range(0, bits, 2)]


def partners(start, width):
    return [k << start for k in range(1, 1 << width)]


def xor_pairs(devices, by):
    return [(i, i ^ by) for i in range(devices)]


def lowered(value):
    return lax.reduce_precision(value, 8, 7)


def sum_small(parts):
    total = sum(item.astype(F32) for item in parts)
    value = sum(total[S_X + EXACT * i : S_X + EXACT * (i + 1)] for i in range(3))
    high = lowered(value)
    middle = lowered(value - high)
    low = value - high - middle
    rest = total[S_X + 3 * EXACT :]
    return jnp.concatenate([total[:S_X], high, middle, low, rest], 0).astype(BF)


def local(
    image, mask, codes, ema_count, ema_sum,
    encoder_weight, encoder_first, encoder_second,
    latent_weight, latent_first, latent_second,
    decoder_weight, decoder_first, decoder_second,
    readout_weight, readout_first, readout_second,
):
    batches, _, band, width = image.shape
    rows = band // 2
    me, devices = lax.axis_index("dp"), lax.axis_size("dp")
    ema_sum = jnp.swapaxes(ema_sum, 1, 2)
    encoder_weight, encoder_first, encoder_second = (
        jnp.swapaxes(item, 0, 1) for item in (encoder_weight, encoder_first, encoder_second)
    )
    latent_weight, latent_first, latent_second = (
        jnp.swapaxes(item, 1, 2) for item in (latent_weight, latent_first, latent_second)
    )
    readout_weight, readout_first, readout_second = (
        jnp.transpose(item, (2, 0, 1)) for item in (readout_weight, readout_first, readout_second)
    )

    limit = pltpu.CompilerParams(vmem_limit_bytes=56 * 1024 * 1024)
    packed = R_CODE + batches * band
    tile, near, across, pack = pl.pallas_call(
        pack_kernel,
        out_shape=[
            jax.ShapeDtypeStruct((batches * band * 8, W), F32),
            jax.ShapeDtypeStruct((batches * 16, W), BF),
            jax.ShapeDtypeStruct((16, W), BF),
            jax.ShapeDtypeStruct((packed, W), BF),
        ],
        in_specs=[VMEM] * 9,
        out_specs=[VMEM] * 4,
        scratch_shapes=[pltpu.VMEM((batches * band, W), F32), pltpu.VMEM((128, 128), F32)],
        compiler_params=limit,
    )(image, mask, codes, ema_count, ema_sum, encoder_weight, latent_weight, decoder_weight, readout_weight)

    both = ("level", "dp")
    same = [(d - 1, d) for d in range(1, devices)] + [(devices + d + 1, devices + d) for d in range(devices - 1)]
    cross = [(devices + d - 1, d) for d in range(1, devices)] + [(d + 1, devices + d) for d in range(devices - 1)]
    near = lax.ppermute(near, both, same)
    across = lax.ppermute(across, both, cross)
    theirs = lax.ppermute(pack, "level", [(0, 1), (1, 0)])

    ext = rows + 4
    pixels = batches * rows * W
    keep_big, keep_small, send = pl.pallas_call(
        functools.partial(step_kernel, batches=batches, rows=rows, step_e=rows, step_d=rows, step_b=rows // 2),
        out_shape=[
            jax.ShapeDtypeStruct((BIG, W), F32),
            jax.ShapeDtypeStruct((SMALL, W), BF),
            jax.ShapeDtypeStruct((BIG + SMALL, W), BF),
        ],
        in_specs=[VMEM] * 5,
        out_specs=[VMEM] * 3,
        scratch_shapes=[
            pltpu.VMEM((batches, ext, 8, W), F32),
            pltpu.VMEM((batches * band + 16, W), F32),
            pltpu.VMEM((TAPS, 256), BF),
            pltpu.VMEM((256, TAPS), BF),
            pltpu.VMEM((256, 128), BF),
            pltpu.VMEM((256, 128), BF),
            pltpu.VMEM((128, 256), BF),
            pltpu.VMEM((16, 256), BF),
            pltpu.VMEM((256, 16), BF),
            pltpu.VMEM((2, 128, 256), BF),
            pltpu.VMEM((3, 128, batches * ext * W), BF),
            pltpu.VMEM((128, pixels), BF),
            pltpu.VMEM((256, pixels), BF),
            pltpu.VMEM((256, pixels), F32),
            pltpu.VMEM((128, pixels), F32),
            pltpu.VMEM((3, 256, batches * (rows + 2) * W), BF),
            pltpu.VMEM((TAPS, 256), F32),
            pltpu.VMEM((16, 256), F32),
            pltpu.VMEM((128, 256), F32),
            pltpu.VMEM((128, 256), F32),
            pltpu.VMEM((2, 144, 256), F32),
            pltpu.VMEM((144, 256), F32),
        ],
        compiler_params=limit,
    )(tile, near, across, pack, theirs)

    got = lax.ppermute(send, "level", [(0, 1), (1, 0)])
    small = sum_small([keep_small, got[BIG:]])
    big = keep_big + got[:BIG].astype(F32)

    stages = radices(devices)
    for start, width_bits in stages:
        count = 1 << width_bits
        index = (me >> start) & (count - 1)
        pieces = big.reshape(count, -1, W)
        total = lax.dynamic_index_in_dim(pieces, index, 0, False)
        for k in range(count - 1, 0, -1):
            out = lax.dynamic_index_in_dim(pieces, index ^ k, 0, False).astype(BF)
            total = total + lax.ppermute(out, "dp", xor_pairs(devices, k << start)).astype(F32)
        big = total
    big = big.astype(BF)
    for number, (start, width_bits) in enumerate(reversed(stages)):
        count = 1 << width_bits
        index = (me >> start) & (count - 1)
        payload = jnp.concatenate([big, small], 0)
        parts = [payload] + [lax.ppermute(payload, "dp", xor_pairs(devices, k << start)) for k in range(1, count)]
        if number == len(stages) - 1:
            break
        size = big.shape[0]
        stacked = jnp.zeros((count, size, W), BF)
        for k in range(count):
            stacked = lax.dynamic_update_index_in_dim(stacked, parts[k][:size], index ^ k, 0)
        big = stacked.reshape(count * size, W)
        small = sum_small([item[size:] for item in parts])

    state = (
        ema_count, ema_sum,
        encoder_weight, encoder_first, encoder_second, latent_weight, latent_first, latent_second,
        decoder_weight, decoder_first, decoder_second, readout_weight, readout_first, readout_second,
    )
    outs = [jax.ShapeDtypeStruct((1, 1), F32)] * 2
    outs += [jax.ShapeDtypeStruct(ema_count.shape, F32), jax.ShapeDtypeStruct(ema_sum.shape, F32)]
    for item in (encoder_weight, latent_weight, decoder_weight, readout_weight):
        copy = item.shape if item.shape[0] == 1 else (1, item.shape[0], item.shape[2])
        outs += [jax.ShapeDtypeStruct(item.shape, F32)] * 3 + [jax.ShapeDtypeStruct(copy, BF)]
    result = pl.pallas_call(
        functools.partial(update_kernel, stages=len(parts), start=start),
        out_shape=outs,
        in_specs=[VMEM] * (len(parts) + len(state)),
        out_specs=[SMEM] * 2 + [VMEM] * (len(outs) - 2),
        scratch_shapes=[pltpu.VMEM((BIG, W), F32), pltpu.VMEM((32, W), F32)],
        compiler_params=pltpu.CompilerParams(vmem_limit_bytes=24 * 1024 * 1024),
    )(*parts, *state)
    loss, valid, count_new, total_new = result[:4]
    enc, lat, dec, read = (list(result[4 * n : 4 * n + 4]) for n in range(1, 5))
    enc[:3] = [jnp.swapaxes(item, 0, 1) for item in enc[:3]]
    lat = [jnp.swapaxes(item, 1, 2) for item in lat]
    read = [jnp.transpose(item, (1, 2, 0)) for item in read[:3]] + [jnp.swapaxes(read[3], 1, 2)]
    return (loss.reshape(()), valid.reshape(()), count_new, jnp.swapaxes(total_new, 1, 2), *enc, *lat, *dec, *read)


def solution(mesh):
    rank = (0, 0, 2, 3) + (3,) * 16
    in_specs = (P(None, None, "dp", None), P(None, "dp", None), P("level", None, "dp", None), P("level", None))
    in_specs += (P("level", None, None),) * 13
    out_specs = tuple(P(*(("level",) + (None,) * (n - 1) if n else ())) for n in rank)
    return jax.shard_map(local, mesh=mesh, in_specs=in_specs, out_specs=out_specs, check_vma=False)
```

```python
import functools

import jax
import jax.numpy as jnp
from jax import lax
from jax.experimental import pallas as pl
from jax.experimental.pallas import tpu as pltpu
from jax.sharding import PartitionSpec as P

CROP = 128
STEP = 5
RATES = (0.05, 0.03, 0.01, 0.03)

F32 = jnp.float32
BF = jnp.bfloat16
W = 128
STEP_MIB, BACK_MIB = 56, 56
NOBODY = 300.0

TAPS = 9 * 128
R_ET = TAPS
R_ZN = R_ET + 128
R_ZT = R_ZN + 128
R_OT = R_ZT + 64
R_BT = R_OT + 16
R_CODE = R_BT + 256
BIG = TAPS + 256
S_Z, S_E, S_O, S_X = 0, 64, 96, 112
LATE, SMALL = 96, 128
EXACT = 5
PATCH = 96

NN = (((1,), (0,)), ((), ()))
NT = (((1,), (1,)), ((), ()))
VMEM = pl.BlockSpec(memory_space=pltpu.VMEM)
SMEM = pl.BlockSpec(memory_space=pltpu.SMEM)
AWAY = pl.BlockSpec(memory_space=pl.ANY)


def dot(a, b, dims=NN):
    return lax.dot_general(a, b, dims, preferred_element_type=F32)


def part(value, count):
    out = []
    for _ in range(count):
        piece = value.astype(BF)
        out.append(piece)
        value = value - piece.astype(F32)
    return out


def patch_row(t):
    dr, dc = t // 3, t % 3
    return ((dr // 2) * 3 + dc) * 16 + (dr % 2) * 8


def pack_kernel(
    image, mask, codes, count, total, enc, lat, dec, read,
    tile, near, across, pack, code_rows, flat,
):
    level = lax.axis_index("level")
    batches, _, band, _ = image.shape
    for b in range(batches):
        base = b * band * 8
        shown = image[b].astype(F32)
        for c in range(3):
            tile[pl.ds(base + c, band, stride=8), :] = shown[c]
        tile[pl.ds(base + 3, band, stride=8), :] = mask[b].astype(F32)
        code = codes[0, b]
        code = jnp.where(code < 256, code, code - 512).astype(F32)
        code_rows[b * band : (b + 1) * band] = code
        tile[pl.ds(base + 4, band, stride=8), :] = code
        for c in range(5, 8):
            tile[pl.ds(base + c, band, stride=8), :] = jnp.zeros((band, W), F32)
    ends = []
    for b in range(batches):
        row = jnp.where(level == 0, band - 2, 0)
        start = pl.multiple_of((b * band + row) * 8, 8)
        near[b * 16 : (b + 1) * 16] = tile[pl.ds(start, 16), :].astype(BF)
        for r in range(2):
            ends.append(
                jnp.where(
                    level == 0,
                    code_rows[b * band + r : b * band + r + 1],
                    code_rows[(b + 1) * band - 2 + r : (b + 1) * band - 1 + r],
                )
            )
    fill = across.shape[0] - len(ends)
    across[...] = jnp.concatenate(ends + [jnp.zeros((fill, W), F32)], 0).astype(BF)

    pack[0:TAPS] = dec[0].astype(BF)
    flat[...] = jnp.zeros_like(flat)
    for t in range(9):
        for c in range(3):
            row = patch_row(t) + c
            flat[row : row + 1] = enc[3 * t + c]
    pack[R_ET : R_ET + 128] = flat[...].T.astype(BF)
    flat[...] = jnp.zeros_like(flat)
    flat[0:64] = lat[0]
    pack[R_ZT : R_ZT + 64] = lat[0].astype(BF)
    pack[R_ZN : R_ZN + 128] = flat[...].T.astype(BF)
    blank = jnp.zeros((13, 128), F32)
    pack[R_OT : R_OT + 16] = jnp.concatenate([read[0], read[1], read[2], blank], 0).astype(BF)
    book = total[0] / count[...]
    for quarter in range(4):
        row = R_BT + (quarter % 2) * 128 + (quarter // 2) * 64
        pack[row : row + 64] = book[:, quarter * 128 : (quarter + 1) * 128].astype(BF)
    pack[R_CODE : R_CODE + batches * band] = code_rows[...].astype(BF)


def sides(v):
    lane = lax.broadcasted_iota(jnp.int32, (v.shape[0], W), 1)
    before, after = [], []
    for i in range(v.shape[1] // W):
        row = v[:, i * W : (i + 1) * W]
        before.append(jnp.where(lane == 0, 0.0, pltpu.roll(row, 1, 1)))
        after.append(jnp.where(lane == W - 1, 0.0, pltpu.roll(row, W - 1, 1)))
    if len(before) == 1:
        return before[0], v, after[0]
    return jnp.concatenate(before, 1), v, jnp.concatenate(after, 1)


def at(row, rows):
    return pl.ds(pl.multiple_of(row * W, W), rows * W)


def fold(v, width):
    return sum(v[:, i : i + width] for i in range(0, v.shape[1], width))


def silu_parts(half):
    p = jnp.tanh(half) + 1.0
    out = half * p
    return out, p + out * (2.0 - p)


def patches(x_s, row, n):
    return jnp.concatenate([x_s[dc, :, at(row + pair, n)] for pair in (0, 2) for dc in range(3)], 0)


def giver(bottom, send):
    def give(start, one, zero, keep, offset, shift=0):
        n = one.shape[0]
        keep[start - shift : start - shift + n] = jnp.where(bottom, one, zero).astype(keep.dtype)
        start = offset + start - shift
        send[start : start + n] = jnp.where(bottom, zero, one).astype(BF)

    return give


def spread_back(dn, da):
    rows = da.shape[1] // W - 2
    near = jnp.concatenate([da[:, (2 - dr) * W : (2 - dr + rows) * W] for dr in range(3)], 0)
    spread = dot(dn[...], near)
    _, _, after = sides(spread[0:128])
    before, _, _ = sides(spread[256:384])
    return after + spread[128:256] + before


def encoder_back(du, gap, h, slope, x, zn, g_z, g_e):
    dz = (du + gap).astype(BF)
    g_z[...] += dot(dz, h, NT)
    dpre = (dot(zn[...], dz) * slope).astype(BF)
    g_e[...] += dot(x, dpre, NT)


def step_kernel(
    tile, near, across, mine, theirs,
    keep_big, keep_small, send, h_out, slope_out, gap_out, da_out, x_out, dn_out, zn_out,
    t_s, far_s, dt, et, zt, ot, on, bt, u_s, h_s, slope_s, gap_s, da_s, x_s, dn, zn, g_d, g_o, g_s, l_s, sems, fixed_sems,
    *, batches, rows,
):
    level, me, devices = lax.axis_index("level"), lax.axis_index("dp"), lax.axis_size("dp")
    band, ext = 2 * rows, rows + 4
    above, below = (me + 1) * band, (me + 2) * band
    top_ok = (lax.rem(above, CROP) != 0) & (me > 0)
    bottom_ok = (lax.rem(below, CROP) != 0) & (me < devices - 1)
    valid = jnp.where(level == 0, top_ok.astype(jnp.int32), bottom_ok.astype(jnp.int32))
    bottom = level == 1

    def pair(start, size):
        a, b = mine[start : start + size], theirs[start : start + size]
        return jnp.where(bottom, a, b), jnp.where(bottom, b, a)

    for t in range(9):
        one, zero = pair(t * 128, 128)
        zero = jnp.concatenate([jnp.zeros((64, 128), BF), zero[0:64]], 0)
        dr, dc = t // 3, t % 3
        dn[dc * 128 : (dc + 1) * 128, dr * 256 : dr * 256 + 128] = one
        dn[dc * 128 : (dc + 1) * 128, dr * 256 + 128 : (dr + 1) * 256] = zero
        dt[0:128, t * 128 : (t + 1) * 128] = (0.5 * one.astype(F32)).T.astype(BF)
        dt[128:256, t * 128 : (t + 1) * 128] = (0.5 * zero.astype(F32)).T.astype(BF)
    one, zero = pair(R_ET, 128)
    et[0:128] = (0.5 * one.astype(F32)).astype(BF)
    et[128:256] = (0.5 * zero.astype(F32)).astype(BF)
    one, zero = pair(R_ZN, 128)
    zn[0:128] = (0.5 * one.astype(F32)).astype(BF)
    zn[128:256] = pltpu.roll(0.5 * zero.astype(F32), 64, 1).astype(BF)
    one, zero = pair(R_ZT, 64)
    blank = jnp.zeros((64, 128), BF)
    zt[0:64] = jnp.concatenate([one, blank], 1)
    zt[64:128] = jnp.concatenate([blank, zero], 1)
    one, zero = pair(R_OT, 16)
    blank = jnp.zeros((8, 128), F32)
    out_t = jnp.concatenate(
        [
            jnp.concatenate([one[0:8].astype(F32), blank], 1),
            jnp.concatenate([blank, zero[0:8].astype(F32)], 1),
        ],
        0,
    )
    ot[...] = out_t.astype(BF)
    on[...] = (0.5 * out_t).T.astype(BF)
    for half in range(2):
        one, zero = pair(R_BT + half * 128, 128)
        bt[0, :, half * 128 : (half + 1) * 128] = one
        bt[1, :, half * 128 : (half + 1) * 128] = zero

    fixed = [
        pltpu.make_async_copy(a, o, fixed_sems.at[n])
        for n, (a, o) in enumerate(((x_s, x_out), (dn, dn_out), (zn, zn_out)))
    ]
    fixed[1].start()
    fixed[2].start()

    far_s[0 : batches * band] = theirs[R_CODE : R_CODE + batches * band].astype(F32)
    far_s[batches * band : batches * band + across.shape[0]] = across[...].astype(F32)
    sub = lax.broadcasted_iota(jnp.int32, (8, W), 0)
    own_sub = jnp.where(bottom, 4, 5)

    def lay(b, e, shown, other):
        code = shown[4:5]
        t_s[b, e] = jnp.where(sub < 4, shown, jnp.where(sub == own_sub, code, other))

    def inner(i, _):
        b, e = i // (rows + 2), i % (rows + 2)
        row = b * band + level * (rows - 2) + e
        lay(
            b,
            e + jnp.where(bottom, 0, 2),
            tile[pl.ds(pl.multiple_of(row * 8, 8), 8), :],
            far_s[pl.ds(row, 1), :],
        )
        return 0

    lax.fori_loop(0, batches * (rows + 2), inner, 0, unroll=2)
    for b in range(batches):
        both = near[b * 16 : (b + 1) * 16].astype(F32)
        for r in range(2):
            row = batches * band + b * 2 + r
            shown = jnp.where(valid > 0, both[r * 8 : (r + 1) * 8], jnp.where(sub == 4, NOBODY, 0.0))
            other = jnp.where(valid > 0, far_s[row : row + 1], NOBODY)
            lay(b, jnp.where(bottom, rows + 2 + r, r), shown, other)

    for ref in (g_d, g_o, g_s, l_s):
        ref[...] = jnp.zeros_like(ref)

    def lookup(b, e, n):
        here = jnp.concatenate([t_s[b, e + i] for i in range(n)], 1)
        ids = lax.broadcasted_iota(jnp.int32, (256, n * W), 0).astype(F32)
        quants, onehots, highs = [], [], []
        for v in range(2):
            code = here[4 + v : 5 + v]
            high = code < 0.0
            low = jnp.where(high, code + 256.0, code)
            onehot = jnp.where(ids == low, 1.0, 0.0).astype(BF)
            both = dot(bt[v], onehot)
            quants.append(jnp.where(high, both[64:128], both[0:64]))
            onehots.append(onehot)
            highs.append(high)
        u = jnp.concatenate(quants, 0)
        for k, view in enumerate(sides(u)):
            u_s[k, :, at(b * ext + e, n)] = view.astype(BF)
        return here, u, onehots, highs

    pairs = ((h_s, h_out), (slope_s, slope_out), (gap_s, gap_out), (da_s, da_out))

    def leave(b, which=range(4)):
        return [pltpu.make_async_copy(pairs[n][0].at[b], pairs[n][1].at[b], sems.at[n, b]) for n in which]

    def encode(b, _):
        runs = [jnp.concatenate([t_s[b, e], t_s[b, e + 1]], 0) for e in range(1, rows + 3)]
        for dc, view in enumerate(sides(jnp.concatenate(runs, 1))):
            x_s[dc, :, at(b * (rows + 2), rows + 2)] = view.astype(BF)
        here, u, onehots, highs = lookup(b, 0, ext)
        inner = slice(2 * W, (2 + rows) * W)
        here, u = here[:, inner], u[:, inner]
        h, slope = silu_parts(dot(et[:, 0:PATCH], patches(x_s, b * (rows + 2), rows)))
        slope_s[b] = slope
        h = h.astype(BF)
        h_s[b] = h
        z = dot(zt[...], h)
        k = here[3:4]
        gap = z - u
        kept = k * gap
        l_s[0:128] += fold(kept * gap, 256)
        gap_s[b] = 0.5 * kept
        z = k * z.astype(BF).astype(F32)
        row = lax.broadcasted_iota(jnp.int32, (16, rows * W), 0)
        for v in range(2):
            part_z = z[v * 64 : v * 64 + 64]
            high = highs[v][:, inner]
            low_k = jnp.where(high, 0.0, k)
            high_k = jnp.where(high, k, 0.0)
            left = jnp.concatenate(
                [
                    jnp.where(high, 0.0, part_z),
                    jnp.where(high, part_z, 0.0),
                    jnp.where(row == 0, low_k, jnp.where(row == 1, high_k, 0.0)),
                ],
                0,
            ).astype(BF)
            g_s[v] += dot(left, onehots[v][:, inner], NT)
        for copy in leave(b, range(3)):
            copy.start()
        return 0

    lax.fori_loop(0, batches, encode, 0)
    fixed[0].start()

    def decode(b, _):
        u = jnp.concatenate(
            [u_s[dc, :, at(b * ext + dr, rows + 2)] for dr in range(3) for dc in range(3)], 0
        )
        inner = slice(W, (1 + rows) * W)
        g, slope = silu_parts(dot(dt[...], u))
        g = g.astype(BF)
        y = dot(ot[...], g)
        here = jnp.concatenate([t_s[b, e] for e in range(1, rows + 3)], 1)
        k = here[3:4]
        x = jnp.where(lax.broadcasted_iota(jnp.int32, here.shape, 0) < 3, here, 0.0)
        diff = y - jnp.concatenate([x, x], 0)
        kept = k * diff
        dy = (2.0 * kept).astype(BF)
        da = (dot(on[...], dy) * slope).astype(BF)
        da_s[b] = da
        l_s[128:144] += fold((kept * diff)[:, inner], 256)
        g_o[...] += dot(dy[:, inner], g[:, inner], NT)
        g_d[...] += dot(u[:, inner], da[:, inner], NT)
        leave(b, [3])[0].start()
        return 0

    lax.fori_loop(0, batches, decode, 0)
    give = giver(bottom, send)
    for t in range(9):
        top = jnp.concatenate([g_d[t * 128 + 64 : (t + 1) * 128, 128:256], jnp.zeros((64, 128), F32)], 0)
        give(t * 128, g_d[t * 128 : (t + 1) * 128, 0:128], top, keep_big, 0)
    for half in range(2):
        cols = slice(half * 128, (half + 1) * 128)
        give(TAPS + half * 128, g_s[0, 0:128, cols], g_s[1, 0:128, cols], keep_big, 0)
    pad = keep_big.shape[0]
    if pad > BIG:
        keep_big[BIG:pad] = jnp.zeros((pad - BIG, W), F32)
        send[BIG:pad] = jnp.zeros((pad - BIG, W), BF)
    blank = jnp.zeros((8, 128), F32)
    give(
        S_O,
        jnp.concatenate([g_o[0:8, 0:128], blank], 0),
        jnp.concatenate([g_o[8:16, 128:256], blank], 0),
        keep_small,
        pad,
        LATE,
    )
    valid_sum = jnp.sum(g_s[0, 128:130])
    loss = 0.25 * jnp.sum(l_s[0:128]) + jnp.sum(l_s[128:144])
    lane = lax.broadcasted_iota(jnp.int32, (1, W), 1)
    other = jnp.where(lane == 0, loss, jnp.where(lane == 1, valid_sum, 0.0))
    exact = []
    for v in range(2):
        runs = [g_s[v, 128 + hi : 129 + hi, half * 128 : (half + 1) * 128] for hi in range(2) for half in range(2)]
        pieces = part(jnp.concatenate(runs + [other], 0), 3)
        exact.append(jnp.concatenate([p.astype(F32) for p in pieces] + [jnp.zeros((1, 128), F32)], 0))
    give(S_X, exact[0], exact[1], keep_small, pad, LATE)
    for copy in fixed + [copy for b in range(batches) for copy in leave(b)]:
        copy.wait()


def back_kernel(
    h_in, slope_in, gap_in, da_in, x_in, dn_in, zn_in, _,
    keep, send, h_s, slope_s, gap_s, da_s, x_s, dn, zn, g_e, g_z, sems, fixed_sems,
    *, batches, rows,
):
    bottom = lax.axis_index("level") == 1
    pairs = ((h_in, h_s), (slope_in, slope_s), (gap_in, gap_s), (da_in, da_s))

    def fetch(b):
        return [pltpu.make_async_copy(a.at[b], o.at[b], sems.at[n, b]) for n, (a, o) in enumerate(pairs)]

    fixed = [
        pltpu.make_async_copy(a, o, fixed_sems.at[n])
        for n, (a, o) in enumerate(((dn_in, dn), (zn_in, zn), (x_in, x_s)))
    ]
    count = h_s.shape[0]
    copies = [fetch(b) for b in range(count)]
    for copy in [fixed[0], copies[0][3], copies[0][2], fixed[1], *copies[0][:2], fixed[2]]:
        copy.start()
    g_e[...] = jnp.zeros_like(g_e)
    g_z[...] = jnp.zeros_like(g_z)
    fixed[0].wait()
    copies[0][3].wait()
    for b in range(1, count):
        for n in (3, 2, 0, 1):
            copies[b][n].start()
    du = spread_back(dn, da_s[0])
    for copy in [fixed[1], fixed[2]]:
        copy.wait()
    for b in range(count):
        for copy in copies[b][:3]:
            copy.wait()
        if b + 1 < count:
            copies[b + 1][3].wait()
        row = b * (rows + 2)
        encoder_back(du, gap_s[b], h_s[b], slope_s[b], patches(x_s, row, rows), zn, g_z, g_e)
        if b + 1 < count:
            du = spread_back(dn, da_s[b + 1])
    give = giver(bottom, send)
    give(S_Z, g_z[0:64, 0:128], g_z[64:128, 128:256], keep, 0)
    enc = []
    for cols in (slice(0, 128), slice(128, 256)):
        runs = [g_e[patch_row(t) : patch_row(t) + 3, cols] for t in range(9)]
        enc.append(jnp.concatenate(runs + [jnp.zeros((5, 128), F32)], 0))
    give(S_E, enc[0], enc[1], keep, 0)


def update_kernel(
    *refs, stages, start
):
    (parts, refs) = refs[:stages], refs[stages:]
    (count, total, ew, e1, e2, zw, z1, z2, dw, d1, d2, ow, o1, o2,
     loss_out, valid_out, count_out, total_out,
     em, es, ep, ec, zm, zs, zp, zc, dm, ds, dp, dc, om, os, op, oc, big, rows) = refs
    share = big.shape[0] // stages
    index = (lax.axis_index("dp") >> start) & (stages - 1)
    size = big.shape[0] // lax.axis_size("dp")
    small = jnp.zeros((SMALL, W), F32)
    for n, ref in enumerate(parts):
        value = ref[0:share].astype(F32)
        for h in range(share // size):
            row = pl.multiple_of((h * stages + (index ^ n)) * size, 8)
            big[pl.ds(row, size), :] = value[h * size : (h + 1) * size]
        small = small + ref[share : share + SMALL].astype(F32)
    exact = sum(small[S_X + EXACT * i : S_X + EXACT * (i + 1)] for i in range(3))
    loss = jnp.sum(exact[4:5, 0:1])
    valid = jnp.sum(exact[4:5, 1:2])
    loss_out[0, 0] = loss
    valid_out[0, 0] = valid
    counts = jnp.concatenate([exact[i : i + 1] for i in range(4)], 1)
    count_out[...] = 0.99 * count[...] + 0.01 * counts
    for quarter in range(4):
        row = TAPS + (quarter % 2) * 128 + (quarter // 2) * 64
        cols = slice(quarter * 128, (quarter + 1) * 128)
        total_out[0, :, cols] = 0.99 * total[0, :, cols] + 0.01 * big[row : row + 64]

    scale = 1.0 - 0.5**STEP

    def adamw(grad, weight, first, second, rate):
        grad = grad / valid
        moment = 0.5 * first + 0.5 * grad
        square = 0.5 * second + 0.5 * grad * grad
        master = weight - rate * (moment / scale / (jnp.sqrt(square / scale) + 1e-08) + 0.01 * weight)
        return moment, square, master

    def whole(grad, w, first, second, rate, outs):
        outs[0][0], outs[1][0], master = adamw(grad, w[0], first[0], second[0], rate)
        outs[2][0] = master
        outs[3][0] = master.astype(BF)

    def by_row(grad, w, first, second, rate, outs):
        n = w.shape[0]
        for i in range(n):
            outs[0][i], outs[1][i], master = adamw(grad[i : i + 1], w[i], first[i], second[i], rate)
            outs[2][i] = master
            rows[i : i + 1] = master
        outs[3][0] = rows[0:n].astype(BF)

    by_row(small[S_E : S_E + 27], ew, e1, e2, RATES[0], (em, es, ep, ec))
    whole(small[S_Z : S_Z + 64], zw, z1, z2, RATES[1], (zm, zs, zp, zc))
    whole(big[0:TAPS], dw, d1, d2, RATES[2], (dm, ds, dp, dc))
    by_row(small[S_O : S_O + 3], ow, o1, o2, RATES[3], (om, os, op, oc))


def radices(devices):
    bits = devices.bit_length() - 1
    return [(start, min(2, bits - start)) for start in range(0, bits, 2)]


def partners(start, width):
    return [k << start for k in range(1, 1 << width)]


def xor_pairs(devices, by):
    return [(i, i ^ by) for i in range(devices)]


def lowered(value):
    return lax.reduce_precision(value, 8, 7)


def sum_small(parts, first):
    total = sum(item.astype(F32) for item in parts)
    value = sum(total[first + EXACT * i : first + EXACT * (i + 1)] for i in range(3))
    high = lowered(value)
    middle = lowered(value - high)
    low = value - high - middle
    rest = total[first + 3 * EXACT :]
    return jnp.concatenate([total[:first], high, middle, low, rest], 0).astype(BF)


def local(
    image, mask, codes, ema_count, ema_sum,
    encoder_weight, encoder_first, encoder_second,
    latent_weight, latent_first, latent_second,
    decoder_weight, decoder_first, decoder_second,
    readout_weight, readout_first, readout_second,
):
    batches, _, band, width = image.shape
    rows = band // 2
    me, devices = lax.axis_index("dp"), lax.axis_size("dp")
    ema_sum = jnp.swapaxes(ema_sum, 1, 2)
    encoder_weight, encoder_first, encoder_second = (
        jnp.swapaxes(item, 0, 1) for item in (encoder_weight, encoder_first, encoder_second)
    )
    latent_weight, latent_first, latent_second = (
        jnp.swapaxes(item, 1, 2) for item in (latent_weight, latent_first, latent_second)
    )
    readout_weight, readout_first, readout_second = (
        jnp.transpose(item, (2, 0, 1)) for item in (readout_weight, readout_first, readout_second)
    )

    def limit(mib):
        return pltpu.CompilerParams(vmem_limit_bytes=mib * 1024 * 1024)

    def outside(*items):
        return [pltpu.with_memory_space_constraint(item, pltpu.HBM) for item in items]

    packed = R_CODE + batches * band
    tile, near, across, pack = pl.pallas_call(
        pack_kernel,
        out_shape=[
            pltpu.VMEM((batches * band * 8, W), F32),
            pltpu.VMEM((batches * 16, W), BF),
            pltpu.VMEM((16, W), BF),
            pltpu.VMEM((packed, W), BF),
        ],
        in_specs=[VMEM] * 9,
        out_specs=[VMEM] * 4,
        scratch_shapes=[pltpu.VMEM((batches * band, W), F32), pltpu.VMEM((128, 128), F32)],
        compiler_params=limit(56),
    )(*outside(image, mask, codes, ema_count, ema_sum, encoder_weight, latent_weight, decoder_weight, readout_weight))

    both = ("level", "dp")
    same = [(d - 1, d) for d in range(1, devices)] + [(devices + d + 1, devices + d) for d in range(devices - 1)]
    cross = [(devices + d - 1, d) for d in range(1, devices)] + [(d + 1, devices + d) for d in range(devices - 1)]
    near = lax.ppermute(near, both, same)
    across = lax.ppermute(across, both, cross)
    theirs = lax.ppermute(pack, "level", [(0, 1), (1, 0)])

    ext = rows + 4
    pixels = batches * rows * W
    framed = batches * (rows + 2) * W
    held = [
        ((batches, 256, rows * W), BF),
        ((batches, 256, rows * W), F32),
        ((batches, 128, rows * W), F32),
        ((batches, 256, (rows + 2) * W), BF),
    ]
    fixed = [((3, 16, framed), BF), ((384, 768), BF), ((256, 128), BF)]
    size = -(-BIG // (8 * devices)) * 8
    padded = size * devices
    shape = jax.ShapeDtypeStruct
    keep, early, send, *kept = pl.pallas_call(
        functools.partial(step_kernel, batches=batches, rows=rows),
        out_shape=[
            pltpu.VMEM((padded, W), F32),
            pltpu.VMEM((SMALL - LATE, W), BF),
            pltpu.VMEM((padded + SMALL - LATE, W), BF),
            *[shape(*item) for item in held + fixed],
        ],
        in_specs=[VMEM] * 5,
        out_specs=[VMEM] * 3 + [AWAY] * 7,
        scratch_shapes=[
            pltpu.VMEM((batches, ext, 8, W), F32),
            pltpu.VMEM((batches * band + 16, W), F32),
            pltpu.VMEM((256, TAPS), BF),
            pltpu.VMEM((256, 128), BF),
            pltpu.VMEM((128, 256), BF),
            pltpu.VMEM((16, 256), BF),
            pltpu.VMEM((256, 16), BF),
            pltpu.VMEM((2, 128, 256), BF),
            pltpu.VMEM((3, 128, batches * ext * W), BF),
            *[pltpu.VMEM(*item) for item in held + fixed],
            pltpu.VMEM((TAPS, 256), F32),
            pltpu.VMEM((16, 256), F32),
            pltpu.VMEM((2, 144, 256), F32),
            pltpu.VMEM((144, 256), F32),
            pltpu.SemaphoreType.DMA((4, batches)),
            pltpu.SemaphoreType.DMA((3,)),
        ],
        compiler_params=limit(STEP_MIB),
    )(*[pltpu.with_memory_space_constraint(item, pltpu.VMEM) for item in (tile, near, across, pack, theirs)])

    swap = [(0, 1), (1, 0)]
    got = lax.ppermute(send, "level", swap)
    early = sum_small([early, got[padded:]], S_X - LATE)
    big = (keep + got[:padded].astype(F32)).astype(BF)
    big = lax.all_to_all(big.reshape(devices, size, W), "dp", 0, 0)

    late, send = pl.pallas_call(
        functools.partial(back_kernel, batches=batches, rows=rows),
        out_shape=[pltpu.VMEM((LATE, W), BF), pltpu.VMEM((LATE, W), BF)],
        in_specs=[AWAY] * 8,
        out_specs=[VMEM] * 2,
        scratch_shapes=[
            *[pltpu.VMEM(*item) for item in held + fixed],
            pltpu.VMEM((PATCH, 256), F32),
            pltpu.VMEM((128, 256), F32),
            pltpu.SemaphoreType.DMA((4, batches)),
            pltpu.SemaphoreType.DMA((3,)),
        ],
        compiler_params=limit(BACK_MIB),
        cost_estimate=pl.CostEstimate(flops=2 * pixels * 98304 * 4, bytes_accessed=1 << 20, transcendentals=0),
    )(*outside(*kept), got)
    big, send = lax.optimization_barrier((big, send))
    got = lax.ppermute(send, "level", swap)
    late = (late.astype(F32) + got.astype(F32)).astype(BF)
    small = jnp.concatenate([late, early], 0)

    big = jnp.sum(big.astype(F32), 0).astype(BF)[None]
    stages = radices(devices)
    for number, (start, width_bits) in enumerate(reversed(stages)):
        count = 1 << width_bits
        index = (me >> start) & (count - 1)
        payload = jnp.concatenate([big.reshape(-1, W), small], 0)
        parts = [payload] + [lax.ppermute(payload, "dp", xor_pairs(devices, k << start)) for k in range(1, count)]
        if number == len(stages) - 1:
            break
        high = big.shape[0]
        stacked = jnp.zeros((high, count, size, W), BF)
        for k in range(count):
            piece = parts[k][: high * size].reshape(high, size, W)
            stacked = lax.dynamic_update_index_in_dim(stacked, piece, index ^ k, 1)
        small = sum_small([item[high * size :] for item in parts], S_X)
        big = stacked.reshape(high * count, size, W)

    state = (
        ema_count, ema_sum,
        encoder_weight, encoder_first, encoder_second, latent_weight, latent_first, latent_second,
        decoder_weight, decoder_first, decoder_second, readout_weight, readout_first, readout_second,
    )
    outs = [jax.ShapeDtypeStruct((1, 1), F32)] * 2
    outs += [jax.ShapeDtypeStruct(ema_count.shape, F32), jax.ShapeDtypeStruct(ema_sum.shape, F32)]
    for item in (encoder_weight, latent_weight, decoder_weight, readout_weight):
        copy = item.shape if item.shape[0] == 1 else (1, item.shape[0], item.shape[2])
        outs += [jax.ShapeDtypeStruct(item.shape, F32)] * 3 + [jax.ShapeDtypeStruct(copy, BF)]
    result = pl.pallas_call(
        functools.partial(update_kernel, stages=len(parts), start=start),
        out_shape=outs,
        in_specs=[VMEM] * (len(parts) + len(state)),
        out_specs=[SMEM] * 2 + [VMEM] * (len(outs) - 2),
        scratch_shapes=[pltpu.VMEM((padded, W), F32), pltpu.VMEM((32, W), F32)],
        compiler_params=limit(16),
    )(*parts, *state)
    loss, valid, count_new, total_new = result[:4]
    enc, lat, dec, read = (list(result[4 * n : 4 * n + 4]) for n in range(1, 5))
    enc[:3] = [jnp.swapaxes(item, 0, 1) for item in enc[:3]]
    lat = [jnp.swapaxes(item, 1, 2) for item in lat]
    read = [jnp.transpose(item, (1, 2, 0)) for item in read[:3]] + [jnp.swapaxes(read[3], 1, 2)]
    return (loss.reshape(()), valid.reshape(()), count_new, jnp.swapaxes(total_new, 1, 2), *enc, *lat, *dec, *read)


def solution(mesh):
    rank = (0, 0, 2, 3) + (3,) * 16
    in_specs = (P(None, None, "dp", None), P(None, "dp", None), P("level", None, "dp", None), P("level", None))
    in_specs += (P("level", None, None),) * 13
    out_specs = tuple(P(*(("level",) + (None,) * (n - 1) if n else ())) for n in rank)
    return jax.shard_map(local, mesh=mesh, in_specs=in_specs, out_specs=out_specs, check_vma=False)
```

```python
import functools

import jax
import jax.numpy as jnp
from jax import lax
from jax.experimental import pallas as pl
from jax.experimental.pallas import tpu as pltpu
from jax.sharding import PartitionSpec as P

CROP = 128
STEP = 5
RATES = (0.05, 0.03, 0.01, 0.03)

F32 = jnp.float32
BF = jnp.bfloat16
W = 128
STEP_MIB, BACK_MIB = 56, 56
NOBODY = 300.0

TAPS = 9 * 128
R_ET = TAPS
R_ZN = R_ET + 128
R_ZT = R_ZN + 128
R_OT = R_ZT + 64
R_BT = R_OT + 16
PACKED = R_BT + 256
BIG = TAPS + 256
S_Z, S_E, S_O, S_X = 0, 64, 96, 112
LATE, SMALL = 96, 128
EXACT = 5
PATCH = 96

NN = (((1,), (0,)), ((), ()))
NT = (((1,), (1,)), ((), ()))
VMEM = pl.BlockSpec(memory_space=pltpu.VMEM)
SMEM = pl.BlockSpec(memory_space=pltpu.SMEM)
AWAY = pl.BlockSpec(memory_space=pl.ANY)


def dot(a, b, dims=NN):
    return lax.dot_general(a, b, dims, preferred_element_type=F32)


def part(value, count):
    out = []
    for _ in range(count):
        piece = value.astype(BF)
        out.append(piece)
        value = value - piece.astype(F32)
    return out


def patch_row(t):
    dr, dc = t // 3, t % 3
    return ((dr // 2) * 3 + dc) * 16 + (dr % 2) * 8


def rows_kernel(image, mask, codes, others, tile, near):
    level = lax.axis_index("level")
    batches, _, band, _ = image.shape

    def fitted(code):
        return jnp.where(code < 256, code, code - 512).astype(F32)

    for b in range(batches):
        base = b * band * 8
        shown = image[b].astype(F32)
        for c in range(3):
            tile[pl.ds(base + c, band, stride=8), :] = shown[c]
        tile[pl.ds(base + 3, band, stride=8), :] = mask[b].astype(F32)
        mine, theirs = fitted(codes[0, b]), fitted(others[0, b])
        tile[pl.ds(base + 4, band, stride=8), :] = jnp.where(level == 1, mine, theirs)
        tile[pl.ds(base + 5, band, stride=8), :] = jnp.where(level == 1, theirs, mine)
        for c in range(6, 8):
            tile[pl.ds(base + c, band, stride=8), :] = jnp.zeros((band, W), F32)
    for b in range(batches):
        row = jnp.where(level == 0, band - 2, 0)
        start = pl.multiple_of((b * band + row) * 8, 8)
        near[b * 16 : (b + 1) * 16] = tile[pl.ds(start, 16), :].astype(BF)


def pack_kernel(count, total, enc, lat, dec, read, pack, flat):
    pack[0:TAPS] = dec[0].astype(BF)
    flat[...] = jnp.zeros_like(flat)
    for t in range(9):
        for c in range(3):
            row = patch_row(t) + c
            flat[row : row + 1] = enc[3 * t + c]
    pack[R_ET : R_ET + 128] = flat[...].T.astype(BF)
    flat[...] = jnp.zeros_like(flat)
    flat[0:64] = lat[0]
    pack[R_ZT : R_ZT + 64] = lat[0].astype(BF)
    pack[R_ZN : R_ZN + 128] = flat[...].T.astype(BF)
    blank = jnp.zeros((13, 128), F32)
    pack[R_OT : R_OT + 16] = jnp.concatenate([read[0], read[1], read[2], blank], 0).astype(BF)
    book = total[0] / count[...]
    for quarter in range(4):
        row = R_BT + (quarter % 2) * 128 + (quarter // 2) * 64
        pack[row : row + 64] = book[:, quarter * 128 : (quarter + 1) * 128].astype(BF)


def sides(v):
    lane = lax.broadcasted_iota(jnp.int32, (v.shape[0], W), 1)
    before, after = [], []
    for i in range(v.shape[1] // W):
        row = v[:, i * W : (i + 1) * W]
        before.append(jnp.where(lane == 0, 0.0, pltpu.roll(row, 1, 1)))
        after.append(jnp.where(lane == W - 1, 0.0, pltpu.roll(row, W - 1, 1)))
    if len(before) == 1:
        return before[0], v, after[0]
    return jnp.concatenate(before, 1), v, jnp.concatenate(after, 1)


def at(row, rows):
    return pl.ds(pl.multiple_of(row * W, W), rows * W)


def fold(v, width):
    return sum(v[:, i : i + width] for i in range(0, v.shape[1], width))


def silu_parts(half):
    p = jnp.tanh(half) + 1.0
    out = half * p
    return out, p + out * (2.0 - p)


def one_hots(here):
    ids = lax.broadcasted_iota(jnp.int32, (256, here.shape[1]), 0).astype(F32)
    onehots, highs = [], []
    for v in range(2):
        code = here[4 + v : 5 + v]
        high = code < 0.0
        low = jnp.where(high, code + 256.0, code)
        onehots.append(jnp.where(ids == low, 1.0, 0.0).astype(BF))
        highs.append(high)
    return onehots, highs


def quantized(here, bt):
    quants = []
    for onehot, high, book in zip(*one_hots(here), bt):
        both = dot(book, onehot)
        quants.append(jnp.where(high, both[64:128], both[0:64]))
    return jnp.concatenate(quants, 0)


def books(mine, theirs, bottom):
    a, b = (jnp.concatenate([pack[R_BT : R_BT + 128], pack[R_BT + 128 : R_BT + 256]], 1) for pack in (mine, theirs))
    return jnp.where(bottom, a, b), jnp.where(bottom, b, a)


def lookup_kernel(tile, mine, theirs, u_c, *, batches, rows):
    level = lax.axis_index("level")
    bt = books(mine, theirs, level == 1)

    def batch(b, _):
        first = b * 2 * rows + level * (rows - 2)
        runs = [tile[pl.ds(pl.multiple_of((first + i) * 8, 8), 8), :] for i in range(rows + 2)]
        u_c[:, at(b * (rows + 2), rows + 2)] = quantized(jnp.concatenate(runs, 1), bt).astype(BF)
        return 0

    lax.fori_loop(0, batches, batch, 0)


def patches(x_s, row, n):
    return jnp.concatenate([x_s[dc, :, at(row + pair, n)] for pair in (0, 2) for dc in range(3)], 0)


def giver(bottom, send):
    def give(start, one, zero, keep, offset, shift=0):
        n = one.shape[0]
        keep[start - shift : start - shift + n] = jnp.where(bottom, one, zero).astype(keep.dtype)
        start = offset + start - shift
        send[start : start + n] = jnp.where(bottom, zero, one).astype(BF)

    return give


def spread_back(dn, da):
    rows = da.shape[1] // W - 2
    near = jnp.concatenate([da[:, (2 - dr) * W : (2 - dr + rows) * W] for dr in range(3)], 0)
    spread = dot(dn[...], near)
    _, _, after = sides(spread[0:128])
    before, _, _ = sides(spread[256:384])
    return after + spread[128:256] + before


def encoder_back(du, gap, h, slope, x, zn, g_z, g_e):
    dz = (du + gap).astype(BF)
    g_z[...] += dot(dz, h, NT)
    dpre = (dot(zn[...], dz) * slope).astype(BF)
    g_e[...] += dot(x, dpre, NT)


def step_kernel(
    tile, near, mine, theirs, u_c,
    keep_big, keep_small, send, h_out, slope_out, gap_out, da_out, x_out, dn_out, zn_out,
    t_s, dt, et, zt, ot, on, u_s, h_s, slope_s, gap_s, da_s, x_s, dn, zn, g_d, g_o, g_s, l_s, sems, fixed_sems,
    *, batches, rows,
):
    level, me, devices = lax.axis_index("level"), lax.axis_index("dp"), lax.axis_size("dp")
    band, ext = 2 * rows, rows + 4
    above, below = (me + 1) * band, (me + 2) * band
    top_ok = (lax.rem(above, CROP) != 0) & (me > 0)
    bottom_ok = (lax.rem(below, CROP) != 0) & (me < devices - 1)
    valid = jnp.where(level == 0, top_ok.astype(jnp.int32), bottom_ok.astype(jnp.int32))
    bottom = level == 1

    def pair(start, size):
        a, b = mine[start : start + size], theirs[start : start + size]
        return jnp.where(bottom, a, b), jnp.where(bottom, b, a)

    for t in range(9):
        one, zero = pair(t * 128, 128)
        zero = jnp.concatenate([jnp.zeros((64, 128), BF), zero[0:64]], 0)
        dr, dc = t // 3, t % 3
        dn[dc * 128 : (dc + 1) * 128, dr * 256 : dr * 256 + 128] = one
        dn[dc * 128 : (dc + 1) * 128, dr * 256 + 128 : (dr + 1) * 256] = zero
        dt[0:128, t * 128 : (t + 1) * 128] = (0.5 * one.astype(F32)).T.astype(BF)
        dt[128:256, t * 128 : (t + 1) * 128] = (0.5 * zero.astype(F32)).T.astype(BF)
    one, zero = pair(R_ET, 128)
    et[0:128] = (0.5 * one.astype(F32)).astype(BF)
    et[128:256] = (0.5 * zero.astype(F32)).astype(BF)
    one, zero = pair(R_ZN, 128)
    zn[0:128] = (0.5 * one.astype(F32)).astype(BF)
    zn[128:256] = pltpu.roll(0.5 * zero.astype(F32), 64, 1).astype(BF)
    one, zero = pair(R_ZT, 64)
    blank = jnp.zeros((64, 128), BF)
    zt[0:64] = jnp.concatenate([one, blank], 1)
    zt[64:128] = jnp.concatenate([blank, zero], 1)
    one, zero = pair(R_OT, 16)
    blank = jnp.zeros((8, 128), F32)
    out_t = jnp.concatenate(
        [
            jnp.concatenate([one[0:8].astype(F32), blank], 1),
            jnp.concatenate([blank, zero[0:8].astype(F32)], 1),
        ],
        0,
    )
    ot[...] = out_t.astype(BF)
    on[...] = (0.5 * out_t).T.astype(BF)
    bt = books(mine, theirs, bottom)
    fixed = [
        pltpu.make_async_copy(a, o, fixed_sems.at[n])
        for n, (a, o) in enumerate(((x_s, x_out), (dn, dn_out), (zn, zn_out)))
    ]
    fixed[1].start()
    fixed[2].start()

    sub = lax.broadcasted_iota(jnp.int32, (8, W), 0)
    nothing = jnp.where((sub == 4) | (sub == 5), NOBODY, 0.0)

    def inner(i, _):
        b, e = i // (rows + 2), i % (rows + 2)
        row = b * band + level * (rows - 2) + e
        t_s[b, e + jnp.where(bottom, 0, 2)] = tile[pl.ds(pl.multiple_of(row * 8, 8), 8), :]
        return 0

    lax.fori_loop(0, batches * (rows + 2), inner, 0, unroll=6)
    for b in range(batches):
        both = near[b * 16 : (b + 1) * 16].astype(F32)
        for r in range(2):
            shown = jnp.where(valid > 0, both[r * 8 : (r + 1) * 8], nothing)
            t_s[b, jnp.where(bottom, rows + 2 + r, r)] = shown

    for ref in (g_d, g_o, g_s, l_s):
        ref[...] = jnp.zeros_like(ref)

    def spread_rows(u, b, e, n):
        for k, view in enumerate(sides(u)):
            u_s[k, :, at(b * ext + e, n)] = view.astype(BF)

    outer = jnp.where(bottom, rows + 2, 0)
    here = jnp.concatenate([t_s[b, outer + r] for b in range(batches) for r in range(2)], 1)
    u = quantized(here, bt)
    for b in range(batches):
        spread_rows(u[:, b * 2 * W : (b + 1) * 2 * W], b, outer, 2)

    pairs = ((h_s, h_out), (slope_s, slope_out), (gap_s, gap_out), (da_s, da_out))

    def leave(b, which=range(4)):
        return [pltpu.make_async_copy(pairs[n][0].at[b], pairs[n][1].at[b], sems.at[n, b]) for n in which]

    def encode(b, _):
        runs = [jnp.concatenate([t_s[b, e], t_s[b, e + 1]], 0) for e in range(1, rows + 3)]
        for dc, view in enumerate(sides(jnp.concatenate(runs, 1))):
            x_s[dc, :, at(b * (rows + 2), rows + 2)] = view.astype(BF)
        spread_rows(u_c[:, at(b * (rows + 2), rows + 2)].astype(F32), b, jnp.where(bottom, 0, 2), rows + 2)
        u = u_c[:, at(b * (rows + 2) + 2 * level, rows)].astype(F32)
        here = jnp.concatenate([t_s[b, 2 + i] for i in range(rows)], 1)
        onehots, highs = one_hots(here)
        h, slope = silu_parts(dot(et[:, 0:PATCH], patches(x_s, b * (rows + 2), rows)))
        slope_s[b] = slope
        h = h.astype(BF)
        h_s[b] = h
        z = dot(zt[...], h)
        k = here[3:4]
        gap = z - u
        kept = k * gap
        l_s[0:128] += fold(kept * gap, 256)
        gap_s[b] = 0.5 * kept
        z = k * z.astype(BF).astype(F32)
        row = lax.broadcasted_iota(jnp.int32, (16, rows * W), 0)
        for v in range(2):
            part_z = z[v * 64 : v * 64 + 64]
            high = highs[v]
            low_k = jnp.where(high, 0.0, k)
            high_k = jnp.where(high, k, 0.0)
            left = jnp.concatenate(
                [
                    jnp.where(high, 0.0, part_z),
                    jnp.where(high, part_z, 0.0),
                    jnp.where(row == 0, low_k, jnp.where(row == 1, high_k, 0.0)),
                ],
                0,
            ).astype(BF)
            g_s[v] += dot(left, onehots[v], NT)
        for copy in leave(b, range(3)):
            copy.start()
        return 0

    lax.fori_loop(0, batches, encode, 0)
    fixed[0].start()

    def decode(b, _):
        u = jnp.concatenate(
            [u_s[dc, :, at(b * ext + dr, rows + 2)] for dr in range(3) for dc in range(3)], 0
        )
        inner = slice(W, (1 + rows) * W)
        g, slope = silu_parts(dot(dt[...], u))
        g = g.astype(BF)
        y = dot(ot[...], g)
        here = jnp.concatenate([t_s[b, e] for e in range(1, rows + 3)], 1)
        k = here[3:4]
        x = jnp.where(lax.broadcasted_iota(jnp.int32, here.shape, 0) < 3, here, 0.0)
        diff = y - jnp.concatenate([x, x], 0)
        kept = k * diff
        dy = (2.0 * kept).astype(BF)
        da = (dot(on[...], dy) * slope).astype(BF)
        da_s[b] = da
        leave(b, [3])[0].start()
        l_s[128:144] += fold((kept * diff)[:, inner], 256)
        g_o[...] += dot(g[:, inner], dy[:, inner], NT)
        g_d[...] += dot(u[:, inner], da[:, inner], NT)
        return 0

    lax.fori_loop(0, batches, decode, 0)
    give = giver(bottom, send)
    for t in range(9):
        top = jnp.concatenate([g_d[t * 128 + 64 : (t + 1) * 128, 128:256], jnp.zeros((64, 128), F32)], 0)
        give(t * 128, g_d[t * 128 : (t + 1) * 128, 0:128], top, keep_big, 0)
    for half in range(2):
        cols = slice(half * 128, (half + 1) * 128)
        give(TAPS + half * 128, g_s[0, 0:128, cols], g_s[1, 0:128, cols], keep_big, 0)
    pad = keep_big.shape[0]
    if pad > BIG:
        keep_big[BIG:pad] = jnp.zeros((pad - BIG, W), F32)
        send[BIG:pad] = jnp.zeros((pad - BIG, W), BF)
    readouts = g_o[...].T
    blank = jnp.zeros((8, 128), F32)
    give(
        S_O,
        jnp.concatenate([readouts[0:8, 0:128], blank], 0),
        jnp.concatenate([readouts[8:16, 128:256], blank], 0),
        keep_small,
        pad,
        LATE,
    )
    valid_sum = jnp.sum(g_s[0, 128:130])
    loss = 0.25 * jnp.sum(l_s[0:128]) + jnp.sum(l_s[128:144])
    lane = lax.broadcasted_iota(jnp.int32, (1, W), 1)
    other = jnp.where(lane == 0, loss, jnp.where(lane == 1, valid_sum, 0.0))
    exact = []
    for v in range(2):
        runs = [g_s[v, 128 + hi : 129 + hi, half * 128 : (half + 1) * 128] for hi in range(2) for half in range(2)]
        pieces = part(jnp.concatenate(runs + [other], 0), 3)
        exact.append(jnp.concatenate([p.astype(F32) for p in pieces] + [jnp.zeros((1, 128), F32)], 0))
    give(S_X, exact[0], exact[1], keep_small, pad, LATE)
    for copy in fixed + [copy for b in range(batches) for copy in leave(b)]:
        copy.wait()


def back_kernel(
    h_in, slope_in, gap_in, da_in, x_in, dn_in, zn_in, _,
    keep, send, h_s, slope_s, gap_s, da_s, x_s, dn, zn, g_e, g_z, sems, fixed_sems,
    *, batches, rows,
):
    bottom = lax.axis_index("level") == 1
    pairs = ((h_in, h_s), (slope_in, slope_s), (gap_in, gap_s), (da_in, da_s))

    def fetch(b):
        return [pltpu.make_async_copy(a.at[b], o.at[b], sems.at[n, b]) for n, (a, o) in enumerate(pairs)]

    fixed = [
        pltpu.make_async_copy(a, o, fixed_sems.at[n])
        for n, (a, o) in enumerate(((dn_in, dn), (zn_in, zn), (x_in, x_s)))
    ]
    count = h_s.shape[0]
    copies = [fetch(b) for b in range(count)]
    for copy in [fixed[0], copies[0][3], copies[0][2], fixed[1], *copies[0][:2], fixed[2]]:
        copy.start()
    g_e[...] = jnp.zeros_like(g_e)
    g_z[...] = jnp.zeros_like(g_z)
    fixed[0].wait()
    copies[0][3].wait()
    for b in range(1, count):
        for n in (3, 2, 0, 1):
            copies[b][n].start()
    du = spread_back(dn, da_s[0])
    for copy in [fixed[1], fixed[2]]:
        copy.wait()
    for b in range(count):
        for copy in copies[b][:3]:
            copy.wait()
        if b + 1 < count:
            copies[b + 1][3].wait()
        row = b * (rows + 2)
        encoder_back(du, gap_s[b], h_s[b], slope_s[b], patches(x_s, row, rows), zn, g_z, g_e)
        if b + 1 < count:
            du = spread_back(dn, da_s[b + 1])
    give = giver(bottom, send)
    give(S_Z, g_z[0:64, 0:128], g_z[64:128, 128:256], keep, 0)
    enc = []
    for cols in (slice(0, 128), slice(128, 256)):
        runs = [g_e[patch_row(t) : patch_row(t) + 3, cols] for t in range(9)]
        enc.append(jnp.concatenate(runs + [jnp.zeros((5, 128), F32)], 0))
    give(S_E, enc[0], enc[1], keep, 0)


def update_kernel(
    *refs, stages, start, other
):
    (parts, refs) = refs[:stages], refs[stages:]
    (count, total, ew, e1, e2, zw, z1, z2, dw, d1, d2, ow, o1, o2,
     loss_out, valid_out, count_out, total_out,
     em, es, ep, ec, zm, zs, zp, zc, dm, ds, dp, dc, om, os, op, oc, big, rows) = refs
    share = big.shape[0] // stages
    top = lax.axis_index("level") == 0
    index = (lax.axis_index("dp") >> jnp.where(top, start, other)) & (stages - 1)
    size = big.shape[0] // lax.axis_size("dp")
    small = jnp.zeros((SMALL, W), F32)
    for n, ref in enumerate(parts):
        value = ref[0:share].astype(F32)
        for h in range(share // size):
            place = h * stages + (index ^ n)
            if other != start:
                place = jnp.where(top, place, (index ^ n) * (share // size) + h)
            row = pl.multiple_of(place * size, 8)
            big[pl.ds(row, size), :] = value[h * size : (h + 1) * size]
        small = small + ref[share : share + SMALL].astype(F32)
    exact = sum(small[S_X + EXACT * i : S_X + EXACT * (i + 1)] for i in range(3))
    loss = jnp.sum(exact[4:5, 0:1])
    valid = jnp.sum(exact[4:5, 1:2])
    loss_out[0, 0] = loss
    valid_out[0, 0] = valid
    counts = jnp.concatenate([exact[i : i + 1] for i in range(4)], 1)
    count_out[...] = 0.99 * count[...] + 0.01 * counts
    for quarter in range(4):
        row = TAPS + (quarter % 2) * 128 + (quarter // 2) * 64
        cols = slice(quarter * 128, (quarter + 1) * 128)
        total_out[0, :, cols] = 0.99 * total[0, :, cols] + 0.01 * big[row : row + 64]

    scale = 1.0 - 0.5**STEP

    def adamw(grad, weight, first, second, rate):
        grad = grad / valid
        moment = 0.5 * first + 0.5 * grad
        square = 0.5 * second + 0.5 * grad * grad
        master = weight - rate * (moment / scale / (jnp.sqrt(square / scale) + 1e-08) + 0.01 * weight)
        return moment, square, master

    def whole(grad, w, first, second, rate, outs):
        outs[0][0], outs[1][0], master = adamw(grad, w[0], first[0], second[0], rate)
        outs[2][0] = master
        outs[3][0] = master.astype(BF)

    def by_row(grad, w, first, second, rate, outs):
        n = w.shape[0]
        for i in range(n):
            outs[0][i], outs[1][i], master = adamw(grad[i : i + 1], w[i], first[i], second[i], rate)
            outs[2][i] = master
            rows[i : i + 1] = master
        outs[3][0] = rows[0:n].astype(BF)

    by_row(small[S_E : S_E + 27], ew, e1, e2, RATES[0], (em, es, ep, ec))
    whole(small[S_Z : S_Z + 64], zw, z1, z2, RATES[1], (zm, zs, zp, zc))
    whole(big[0:TAPS], dw, d1, d2, RATES[2], (dm, ds, dp, dc))
    by_row(small[S_O : S_O + 3], ow, o1, o2, RATES[3], (om, os, op, oc))


def radices(devices):
    bits = devices.bit_length() - 1
    return [(start, min(2, bits - start)) for start in range(0, bits, 2)]


def partners(start, width):
    return [k << start for k in range(1, 1 << width)]


def xor_pairs(devices, by, other):
    return [(i, i ^ by) for i in range(devices)] + [(devices + i, devices + (i ^ other)) for i in range(devices)]


def lowered(value):
    return lax.reduce_precision(value, 8, 7)


def sum_small(parts, first):
    total = sum(item.astype(F32) for item in parts)
    value = sum(total[first + EXACT * i : first + EXACT * (i + 1)] for i in range(3))
    high = lowered(value)
    middle = lowered(value - high)
    low = value - high - middle
    rest = total[first + 3 * EXACT :]
    return jnp.concatenate([total[:first], high, middle, low, rest], 0).astype(BF)


def local(
    image, mask, codes, ema_count, ema_sum,
    encoder_weight, encoder_first, encoder_second,
    latent_weight, latent_first, latent_second,
    decoder_weight, decoder_first, decoder_second,
    readout_weight, readout_first, readout_second,
):
    batches, _, band, width = image.shape
    rows = band // 2
    me, devices = lax.axis_index("dp"), lax.axis_size("dp")
    ema_sum = jnp.swapaxes(ema_sum, 1, 2)
    encoder_weight, encoder_first, encoder_second = (
        jnp.swapaxes(item, 0, 1) for item in (encoder_weight, encoder_first, encoder_second)
    )
    latent_weight, latent_first, latent_second = (
        jnp.swapaxes(item, 1, 2) for item in (latent_weight, latent_first, latent_second)
    )
    readout_weight, readout_first, readout_second = (
        jnp.transpose(item, (2, 0, 1)) for item in (readout_weight, readout_first, readout_second)
    )

    def limit(mib):
        return pltpu.CompilerParams(vmem_limit_bytes=mib * 1024 * 1024)

    def outside(*items):
        return [pltpu.with_memory_space_constraint(item, pltpu.HBM) for item in items]

    def inside_vmem(item):
        return pltpu.with_memory_space_constraint(item, pltpu.VMEM)

    swap = [(0, 1), (1, 0)]
    others = lax.ppermute(codes, "level", swap)
    weights = outside(ema_count, ema_sum, encoder_weight, latent_weight, decoder_weight, readout_weight)
    pack = pl.pallas_call(
        pack_kernel,
        out_shape=pltpu.VMEM((PACKED, W), BF),
        in_specs=[VMEM] * 6,
        out_specs=VMEM,
        scratch_shapes=[pltpu.VMEM((128, 128), F32)],
        compiler_params=limit(56),
    )(*weights)
    others, pack = lax.optimization_barrier((others, pack))
    tile, near = pl.pallas_call(
        rows_kernel,
        out_shape=[pltpu.VMEM((batches * band * 8, W), F32), pltpu.VMEM((batches * 16, W), BF)],
        in_specs=[VMEM] * 4,
        out_specs=[VMEM] * 2,
        compiler_params=limit(56),
    )(*outside(image, mask, codes), others)

    both = ("level", "dp")
    inside = [d for d in range(1, devices) if (d + 1) * band % CROP != 0]
    pairs = [(d - 1, d) for d in inside] + [(devices + d, devices + d - 1) for d in inside]
    near = lax.ppermute(near, both, pairs)
    theirs = lax.ppermute(pack, "level", swap)

    u_c = pl.pallas_call(
        functools.partial(lookup_kernel, batches=batches, rows=rows),
        out_shape=pltpu.VMEM((128, batches * (rows + 2) * W), BF),
        in_specs=[VMEM] * 3,
        out_specs=VMEM,
        compiler_params=limit(40),
        cost_estimate=pl.CostEstimate(flops=3 << 30, bytes_accessed=1 << 20, transcendentals=0),
    )(*[inside_vmem(item) for item in (tile, pack, theirs)])
    ext = rows + 4
    pixels = batches * rows * W
    framed = batches * (rows + 2) * W
    held = [
        ((batches, 256, rows * W), BF),
        ((batches, 256, rows * W), F32),
        ((batches, 128, rows * W), F32),
        ((batches, 256, (rows + 2) * W), BF),
    ]
    fixed = [((3, 16, framed), BF), ((384, 768), BF), ((256, 128), BF)]
    size = -(-BIG // (8 * devices)) * 8
    padded = size * devices
    shape = jax.ShapeDtypeStruct
    keep, early, send, *kept = pl.pallas_call(
        functools.partial(step_kernel, batches=batches, rows=rows),
        out_shape=[
            pltpu.VMEM((padded, W), F32),
            pltpu.VMEM((SMALL - LATE, W), BF),
            pltpu.VMEM((padded + SMALL - LATE, W), BF),
            *[shape(*item) for item in held + fixed],
        ],
        in_specs=[VMEM] * 5,
        out_specs=[VMEM] * 3 + [AWAY] * 7,
        scratch_shapes=[
            pltpu.VMEM((batches, ext, 8, W), F32),
            pltpu.VMEM((256, TAPS), BF),
            pltpu.VMEM((256, 128), BF),
            pltpu.VMEM((128, 256), BF),
            pltpu.VMEM((16, 256), BF),
            pltpu.VMEM((256, 16), BF),
            pltpu.VMEM((3, 128, batches * ext * W), BF),
            *[pltpu.VMEM(*item) for item in held + fixed],
            pltpu.VMEM((TAPS, 256), F32),
            pltpu.VMEM((256, 16), F32),
            pltpu.VMEM((2, 144, 256), F32),
            pltpu.VMEM((144, 256), F32),
            pltpu.SemaphoreType.DMA((4, batches)),
            pltpu.SemaphoreType.DMA((3,)),
        ],
        compiler_params=limit(STEP_MIB),
    )(*[inside_vmem(item) for item in (tile, near, pack, theirs, u_c)])

    got = lax.ppermute(send, "level", swap)
    early = sum_small([early, got[padded:]], S_X - LATE)
    big = (keep + got[:padded].astype(F32)).astype(BF)
    big = lax.all_to_all(big.reshape(devices, size, W), "dp", 0, 0)

    late, send = pl.pallas_call(
        functools.partial(back_kernel, batches=batches, rows=rows),
        out_shape=[pltpu.VMEM((LATE, W), BF), pltpu.VMEM((LATE, W), BF)],
        in_specs=[AWAY] * 8,
        out_specs=[VMEM] * 2,
        scratch_shapes=[
            *[pltpu.VMEM(*item) for item in held + fixed],
            pltpu.VMEM((PATCH, 256), F32),
            pltpu.VMEM((128, 256), F32),
            pltpu.SemaphoreType.DMA((4, batches)),
            pltpu.SemaphoreType.DMA((3,)),
        ],
        compiler_params=limit(BACK_MIB),
        cost_estimate=pl.CostEstimate(flops=2 * pixels * 98304 * 4, bytes_accessed=1 << 20, transcendentals=0),
    )(*outside(*kept), got)
    big, send = lax.optimization_barrier((big, send))
    got = lax.ppermute(send, "level", swap)
    late = (late.astype(F32) + got.astype(F32)).astype(BF)
    small = jnp.concatenate([late, early], 0)

    big = jnp.sum(big.astype(F32), 0).astype(BF)[None]
    stages = radices(devices)
    crossed = len(stages) == 2 and stages[0][1] == stages[1][1]
    for number, (start, width_bits) in enumerate(reversed(stages)):
        count = 1 << width_bits
        other = stages[number][0] if crossed else start
        index = (me >> jnp.where(lax.axis_index("level") == 0, start, other)) & (count - 1)
        payload = jnp.concatenate([big.reshape(-1, W), small], 0)
        parts = [payload] + [
            lax.ppermute(payload, both, xor_pairs(devices, k << start, k << other)) for k in range(1, count)
        ]
        if number == len(stages) - 1:
            break
        high = big.shape[0]
        stacked = jnp.zeros((high, count, size, W), BF)
        for k in range(count):
            piece = parts[k][: high * size].reshape(high, size, W)
            stacked = lax.dynamic_update_index_in_dim(stacked, piece, index ^ k, 1)
        small = sum_small([item[high * size :] for item in parts], S_X)
        big = stacked.reshape(high * count, size, W)

    state = (
        ema_count, ema_sum,
        encoder_weight, encoder_first, encoder_second, latent_weight, latent_first, latent_second,
        decoder_weight, decoder_first, decoder_second, readout_weight, readout_first, readout_second,
    )
    outs = [jax.ShapeDtypeStruct((1, 1), F32)] * 2
    outs += [jax.ShapeDtypeStruct(ema_count.shape, F32), jax.ShapeDtypeStruct(ema_sum.shape, F32)]
    for item in (encoder_weight, latent_weight, decoder_weight, readout_weight):
        copy = item.shape if item.shape[0] == 1 else (1, item.shape[0], item.shape[2])
        outs += [jax.ShapeDtypeStruct(item.shape, F32)] * 3 + [jax.ShapeDtypeStruct(copy, BF)]
    result = pl.pallas_call(
        functools.partial(update_kernel, stages=len(parts), start=start, other=other),
        out_shape=outs,
        in_specs=[VMEM] * (len(parts) + len(state)),
        out_specs=[SMEM] * 2 + [VMEM] * (len(outs) - 2),
        scratch_shapes=[pltpu.VMEM((padded, W), F32), pltpu.VMEM((32, W), F32)],
        compiler_params=limit(16),
    )(*parts, *state)
    loss, valid, count_new, total_new = result[:4]
    enc, lat, dec, read = (list(result[4 * n : 4 * n + 4]) for n in range(1, 5))
    enc[:3] = [jnp.swapaxes(item, 0, 1) for item in enc[:3]]
    lat = [jnp.swapaxes(item, 1, 2) for item in lat]
    read = [jnp.transpose(item, (1, 2, 0)) for item in read[:3]] + [jnp.swapaxes(read[3], 1, 2)]
    return (loss.reshape(()), valid.reshape(()), count_new, jnp.swapaxes(total_new, 1, 2), *enc, *lat, *dec, *read)


def solution(mesh):
    rank = (0, 0, 2, 3) + (3,) * 16
    in_specs = (P(None, None, "dp", None), P(None, "dp", None), P("level", None, "dp", None), P("level", None))
    in_specs += (P("level", None, None),) * 13
    out_specs = tuple(P(*(("level",) + (None,) * (n - 1) if n else ())) for n in rank)
    return jax.shard_map(local, mesh=mesh, in_specs=in_specs, out_specs=out_specs, check_vma=False)
```

```python
import functools

import jax
import jax.numpy as jnp
from jax import lax
from jax.experimental import pallas as pl
from jax.experimental.pallas import tpu as pltpu
from jax.sharding import PartitionSpec as P

CROP = 128
STEP = 5
RATES = (0.05, 0.03, 0.01, 0.03)

F32 = jnp.float32
BF = jnp.bfloat16
W = 128
STEP_MIB, BACK_MIB = 56, 56
NOBODY = 300.0

TAPS = 9 * 128
R_ET = TAPS
R_ZN = R_ET + 128
R_ZT = R_ZN + 128
R_OT = R_ZT + 64
R_BT = R_OT + 16
PACKED = R_BT + 256
BIG = TAPS + 256
S_Z, S_E, S_O, S_X = 0, 64, 96, 112
LATE, SMALL = 96, 128
EXACT = 5
PATCH = 96

NN = (((1,), (0,)), ((), ()))
NT = (((1,), (1,)), ((), ()))
VMEM = pl.BlockSpec(memory_space=pltpu.VMEM)
SMEM = pl.BlockSpec(memory_space=pltpu.SMEM)
AWAY = pl.BlockSpec(memory_space=pl.ANY)


def dot(a, b, dims=NN):
    return lax.dot_general(a, b, dims, preferred_element_type=F32)


def part(value, count):
    out = []
    for _ in range(count):
        piece = value.astype(BF)
        out.append(piece)
        value = value - piece.astype(F32)
    return out


def patch_row(t):
    dr, dc = t // 3, t % 3
    return ((dr // 2) * 3 + dc) * 16 + (dr % 2) * 8


def rows_kernel(image, mask, codes, others, tile, near):
    level = lax.axis_index("level")
    batches, _, band, _ = image.shape

    def fitted(code):
        return jnp.where(code < 256, code, code - 512).astype(F32)

    for b in range(batches):
        base = b * band * 8
        shown = image[b].astype(F32)
        for c in range(3):
            tile[pl.ds(base + c, band, stride=8), :] = shown[c]
        tile[pl.ds(base + 3, band, stride=8), :] = mask[b].astype(F32)
        mine, theirs = fitted(codes[0, b]), fitted(others[0, b])
        tile[pl.ds(base + 4, band, stride=8), :] = jnp.where(level == 1, mine, theirs)
        tile[pl.ds(base + 5, band, stride=8), :] = jnp.where(level == 1, theirs, mine)
        for c in range(6, 8):
            tile[pl.ds(base + c, band, stride=8), :] = jnp.zeros((band, W), F32)
    for b in range(batches):
        row = jnp.where(level == 0, band - 2, 0)
        start = pl.multiple_of((b * band + row) * 8, 8)
        near[b * 16 : (b + 1) * 16] = tile[pl.ds(start, 16), :].astype(BF)


def pack_kernel(count, total, enc, lat, dec, read, pack, flat):
    pack[0:TAPS] = dec[0].astype(BF)
    flat[...] = jnp.zeros_like(flat)
    for t in range(9):
        for c in range(3):
            row = patch_row(t) + c
            flat[row : row + 1] = enc[3 * t + c]
    pack[R_ET : R_ET + 128] = flat[...].T.astype(BF)
    flat[...] = jnp.zeros_like(flat)
    flat[0:64] = lat[0]
    pack[R_ZT : R_ZT + 64] = lat[0].astype(BF)
    pack[R_ZN : R_ZN + 128] = flat[...].T.astype(BF)
    blank = jnp.zeros((13, 128), F32)
    pack[R_OT : R_OT + 16] = jnp.concatenate([read[0], read[1], read[2], blank], 0).astype(BF)
    book = total[0] / count[...]
    for quarter in range(4):
        row = R_BT + (quarter % 2) * 128 + (quarter // 2) * 64
        pack[row : row + 64] = book[:, quarter * 128 : (quarter + 1) * 128].astype(BF)


def sides(v):
    lane = lax.broadcasted_iota(jnp.int32, (v.shape[0], W), 1)
    before, after = [], []
    for i in range(v.shape[1] // W):
        row = v[:, i * W : (i + 1) * W]
        before.append(jnp.where(lane == 0, 0.0, pltpu.roll(row, 1, 1)))
        after.append(jnp.where(lane == W - 1, 0.0, pltpu.roll(row, W - 1, 1)))
    if len(before) == 1:
        return before[0], v, after[0]
    return jnp.concatenate(before, 1), v, jnp.concatenate(after, 1)


def at(row, rows):
    return pl.ds(pl.multiple_of(row * W, W), rows * W)


def fold(v, width):
    return sum(v[:, i : i + width] for i in range(0, v.shape[1], width))


def silu_parts(half):
    p = jnp.tanh(half) + 1.0
    out = half * p
    return out, p + out * (2.0 - p)


def one_hots(here):
    ids = lax.broadcasted_iota(jnp.int32, (256, here.shape[1]), 0).astype(F32)
    onehots, highs = [], []
    for v in range(2):
        code = here[4 + v : 5 + v]
        high = code < 0.0
        low = jnp.where(high, code + 256.0, code)
        onehots.append(jnp.where(ids == low, 1.0, 0.0).astype(BF))
        highs.append(high)
    return onehots, highs


def quantized(here, bt):
    quants = []
    for onehot, high, book in zip(*one_hots(here), bt):
        both = dot(book, onehot)
        quants.append(jnp.where(high, both[64:128], both[0:64]))
    return jnp.concatenate(quants, 0)


def books(mine, theirs, bottom):
    a, b = (jnp.concatenate([pack[R_BT : R_BT + 128], pack[R_BT + 128 : R_BT + 256]], 1) for pack in (mine, theirs))
    return jnp.where(bottom, a, b), jnp.where(bottom, b, a)


def lookup_kernel(tile, mine, theirs, u_c, *, batches, rows):
    level = lax.axis_index("level")
    bt = books(mine, theirs, level == 1)

    def batch(b, _):
        first = b * 2 * rows + level * (rows - 2)
        runs = [tile[pl.ds(pl.multiple_of((first + i) * 8, 8), 8), :] for i in range(rows + 2)]
        u_c[:, at(b * (rows + 2), rows + 2)] = quantized(jnp.concatenate(runs, 1), bt).astype(BF)
        return 0

    lax.fori_loop(0, batches, batch, 0)


def patches(x_s, row, n):
    return jnp.concatenate([x_s[dc, :, at(row + pair, n)] for pair in (0, 2) for dc in range(3)], 0)


def giver(bottom, send):
    def give(start, one, zero, keep, offset, shift=0):
        n = one.shape[0]
        keep[start - shift : start - shift + n] = jnp.where(bottom, one, zero).astype(keep.dtype)
        start = offset + start - shift
        send[start : start + n] = jnp.where(bottom, zero, one).astype(BF)

    return give


def spread_back(dn, da):
    rows = da.shape[1] // W - 2
    near = jnp.concatenate([da[:, (2 - dr) * W : (2 - dr + rows) * W] for dr in range(3)], 0)
    spread = dot(dn[...], near)
    _, _, after = sides(spread[0:128])
    before, _, _ = sides(spread[256:384])
    return after + spread[128:256] + before


def encoder_back(du, gap, h, slope, x, zn, g_z, g_e):
    dz = (du + gap).astype(BF)
    g_z[...] += dot(dz, h, NT)
    dpre = (dot(zn[...], dz) * slope).astype(BF)
    g_e[...] += dot(x, dpre, NT)


def step_kernel(
    tile, near, mine, theirs, u_c,
    keep_big, keep_small, send, h_out, slope_out, gap_out, da_out, x_out, dn_out, zn_out,
    t_s, dt, et, zt, ot, on, u_s, h_s, slope_s, gap_s, da_s, x_s, dn, zn, g_d, g_o, g_s, l_s, sems, fixed_sems,
    *, batches, rows,
):
    level, me, devices = lax.axis_index("level"), lax.axis_index("dp"), lax.axis_size("dp")
    band, ext = 2 * rows, rows + 4
    above, below = (me + 1) * band, (me + 2) * band
    top_ok = (lax.rem(above, CROP) != 0) & (me > 0)
    bottom_ok = (lax.rem(below, CROP) != 0) & (me < devices - 1)
    valid = jnp.where(level == 0, top_ok.astype(jnp.int32), bottom_ok.astype(jnp.int32))
    bottom = level == 1

    def pair(start, size):
        a, b = mine[start : start + size], theirs[start : start + size]
        return jnp.where(bottom, a, b), jnp.where(bottom, b, a)

    for t in range(9):
        one, zero = pair(t * 128, 128)
        zero = jnp.concatenate([jnp.zeros((64, 128), BF), zero[0:64]], 0)
        dr, dc = t // 3, t % 3
        dn[dc * 128 : (dc + 1) * 128, dr * 256 : dr * 256 + 128] = one
        dn[dc * 128 : (dc + 1) * 128, dr * 256 + 128 : (dr + 1) * 256] = zero
        dt[0:128, t * 128 : (t + 1) * 128] = (0.5 * one.astype(F32)).T.astype(BF)
        dt[128:256, t * 128 : (t + 1) * 128] = (0.5 * zero.astype(F32)).T.astype(BF)
    one, zero = pair(R_ET, 128)
    et[0:128] = (0.5 * one.astype(F32)).astype(BF)
    et[128:256] = (0.5 * zero.astype(F32)).astype(BF)
    one, zero = pair(R_ZN, 128)
    zn[0:128] = (0.5 * one.astype(F32)).astype(BF)
    zn[128:256] = pltpu.roll(0.5 * zero.astype(F32), 64, 1).astype(BF)
    one, zero = pair(R_ZT, 64)
    blank = jnp.zeros((64, 128), BF)
    zt[0:64] = jnp.concatenate([one, blank], 1)
    zt[64:128] = jnp.concatenate([blank, zero], 1)
    one, zero = pair(R_OT, 16)
    blank = jnp.zeros((8, 128), F32)
    out_t = jnp.concatenate(
        [
            jnp.concatenate([one[0:8].astype(F32), blank], 1),
            jnp.concatenate([blank, zero[0:8].astype(F32)], 1),
        ],
        0,
    )
    ot[...] = out_t.astype(BF)
    on[...] = (0.5 * out_t).T.astype(BF)
    bt = books(mine, theirs, bottom)
    fixed = [
        pltpu.make_async_copy(a, o, fixed_sems.at[n])
        for n, (a, o) in enumerate(((x_s, x_out), (dn, dn_out), (zn, zn_out)))
    ]
    fixed[1].start()
    fixed[2].start()

    sub = lax.broadcasted_iota(jnp.int32, (8, W), 0)
    nothing = jnp.where((sub == 4) | (sub == 5), NOBODY, 0.0)

    def inner(i, _):
        b, e = i // (rows + 2), i % (rows + 2)
        row = b * band + level * (rows - 2) + e
        t_s[b, e + jnp.where(bottom, 0, 2)] = tile[pl.ds(pl.multiple_of(row * 8, 8), 8), :]
        return 0

    lax.fori_loop(0, batches * (rows + 2), inner, 0, unroll=6)
    for b in range(batches):
        both = near[b * 16 : (b + 1) * 16].astype(F32)
        for r in range(2):
            shown = jnp.where(valid > 0, both[r * 8 : (r + 1) * 8], nothing)
            t_s[b, jnp.where(bottom, rows + 2 + r, r)] = shown

    for ref in (g_d, g_o, g_s, l_s):
        ref[...] = jnp.zeros_like(ref)

    def spread_rows(u, b, e, n):
        for k, view in enumerate(sides(u)):
            u_s[k, :, at(b * ext + e, n)] = view.astype(BF)

    outer = jnp.where(bottom, rows + 2, 0)
    here = jnp.concatenate([t_s[b, outer + r] for b in range(batches) for r in range(2)], 1)
    u = quantized(here, bt)
    for b in range(batches):
        spread_rows(u[:, b * 2 * W : (b + 1) * 2 * W], b, outer, 2)

    pairs = ((h_s, h_out), (slope_s, slope_out), (gap_s, gap_out), (da_s, da_out))

    def leave(b, which=range(4)):
        return [pltpu.make_async_copy(pairs[n][0].at[b], pairs[n][1].at[b], sems.at[n, b]) for n in which]

    def encode(b, _):
        runs = [jnp.concatenate([t_s[b, e], t_s[b, e + 1]], 0) for e in range(1, rows + 3)]
        for dc, view in enumerate(sides(jnp.concatenate(runs, 1))):
            x_s[dc, :, at(b * (rows + 2), rows + 2)] = view.astype(BF)
        spread_rows(u_c[:, at(b * (rows + 2), rows + 2)].astype(F32), b, jnp.where(bottom, 0, 2), rows + 2)
        u = u_c[:, at(b * (rows + 2) + 2 * level, rows)].astype(F32)
        here = jnp.concatenate([t_s[b, 2 + i] for i in range(rows)], 1)
        onehots, highs = one_hots(here)
        h, slope = silu_parts(dot(et[:, 0:PATCH], patches(x_s, b * (rows + 2), rows)))
        slope_s[b] = slope
        h = h.astype(BF)
        h_s[b] = h
        z = dot(zt[...], h)
        k = here[3:4]
        gap = z - u
        kept = k * gap
        l_s[0:128] += fold(kept * gap, 256)
        gap_s[b] = 0.5 * kept
        z = k * z.astype(BF).astype(F32)
        row = lax.broadcasted_iota(jnp.int32, (16, rows * W), 0)
        for v in range(2):
            part_z = z[v * 64 : v * 64 + 64]
            high = highs[v]
            low_k = jnp.where(high, 0.0, k)
            high_k = jnp.where(high, k, 0.0)
            left = jnp.concatenate(
                [
                    jnp.where(high, 0.0, part_z),
                    jnp.where(high, part_z, 0.0),
                    jnp.where(row == 0, low_k, jnp.where(row == 1, high_k, 0.0)),
                ],
                0,
            ).astype(BF)
            g_s[v] += dot(left, onehots[v], NT)
        for copy in leave(b, range(3)):
            copy.start()
        return 0

    lax.fori_loop(0, batches, encode, 0)
    fixed[0].start()

    def decode(b, _):
        u = jnp.concatenate(
            [u_s[dc, :, at(b * ext + dr, rows + 2)] for dr in range(3) for dc in range(3)], 0
        )
        inner = slice(W, (1 + rows) * W)
        g, slope = silu_parts(dot(dt[...], u))
        g = g.astype(BF)
        y = dot(ot[...], g)
        here = jnp.concatenate([t_s[b, e] for e in range(1, rows + 3)], 1)
        k = here[3:4]
        x = jnp.where(lax.broadcasted_iota(jnp.int32, here.shape, 0) < 3, here, 0.0)
        diff = y - jnp.concatenate([x, x], 0)
        kept = k * diff
        dy = (2.0 * kept).astype(BF)
        da = (dot(on[...], dy) * slope).astype(BF)
        da_s[b] = da
        leave(b, [3])[0].start()
        l_s[128:144] += fold((kept * diff)[:, inner], 256)
        g_o[...] += dot(g[:, inner], dy[:, inner], NT)
        g_d[...] += dot(u[:, inner], da[:, inner], NT)
        return 0

    lax.fori_loop(0, batches, decode, 0)
    give = giver(bottom, send)
    for t in range(9):
        top = jnp.concatenate([g_d[t * 128 + 64 : (t + 1) * 128, 128:256], jnp.zeros((64, 128), F32)], 0)
        give(t * 128, g_d[t * 128 : (t + 1) * 128, 0:128], top, keep_big, 0)
    for half in range(2):
        cols = slice(half * 128, (half + 1) * 128)
        give(TAPS + half * 128, g_s[0, 0:128, cols], g_s[1, 0:128, cols], keep_big, 0)
    pad = keep_big.shape[0]
    if pad > BIG:
        keep_big[BIG:pad] = jnp.zeros((pad - BIG, W), F32)
        send[BIG:pad] = jnp.zeros((pad - BIG, W), BF)
    readouts = g_o[...].T
    blank = jnp.zeros((8, 128), F32)
    give(
        S_O,
        jnp.concatenate([readouts[0:8, 0:128], blank], 0),
        jnp.concatenate([readouts[8:16, 128:256], blank], 0),
        keep_small,
        pad,
        LATE,
    )
    valid_sum = jnp.sum(g_s[0, 128:130])
    loss = 0.25 * jnp.sum(l_s[0:128]) + jnp.sum(l_s[128:144])
    lane = lax.broadcasted_iota(jnp.int32, (1, W), 1)
    other = jnp.where(lane == 0, loss, jnp.where(lane == 1, valid_sum, 0.0))
    exact = []
    for v in range(2):
        runs = [g_s[v, 128 + hi : 129 + hi, half * 128 : (half + 1) * 128] for hi in range(2) for half in range(2)]
        pieces = part(jnp.concatenate(runs + [other], 0), 3)
        exact.append(jnp.concatenate([p.astype(F32) for p in pieces] + [jnp.zeros((1, 128), F32)], 0))
    give(S_X, exact[0], exact[1], keep_small, pad, LATE)
    for copy in fixed + [copy for b in range(batches) for copy in leave(b)]:
        copy.wait()


def back_kernel(
    h_in, slope_in, gap_in, da_in, x_in, dn_in, zn_in, _,
    keep, send, h_s, slope_s, gap_s, da_s, x_s, dn, zn, g_e, g_z, sems, fixed_sems,
    *, batches, rows,
):
    bottom = lax.axis_index("level") == 1
    pairs = ((h_in, h_s), (slope_in, slope_s), (gap_in, gap_s), (da_in, da_s))

    def fetch(b):
        return [pltpu.make_async_copy(a.at[b], o.at[b], sems.at[n, b]) for n, (a, o) in enumerate(pairs)]

    fixed = [
        pltpu.make_async_copy(a, o, fixed_sems.at[n])
        for n, (a, o) in enumerate(((dn_in, dn), (zn_in, zn), (x_in, x_s)))
    ]
    count = h_s.shape[0]
    copies = [fetch(b) for b in range(count)]
    for copy in [fixed[0], copies[0][3], copies[0][2], fixed[1], *copies[0][:2], fixed[2]]:
        copy.start()
    g_e[...] = jnp.zeros_like(g_e)
    g_z[...] = jnp.zeros_like(g_z)
    fixed[0].wait()
    copies[0][3].wait()
    for b in range(1, count):
        for n in (3, 2, 0, 1):
            copies[b][n].start()
    du = spread_back(dn, da_s[0])
    for copy in [fixed[1], fixed[2]]:
        copy.wait()
    for b in range(count):
        for copy in copies[b][:3]:
            copy.wait()
        if b + 1 < count:
            copies[b + 1][3].wait()
        row = b * (rows + 2)
        encoder_back(du, gap_s[b], h_s[b], slope_s[b], patches(x_s, row, rows), zn, g_z, g_e)
        if b + 1 < count:
            du = spread_back(dn, da_s[b + 1])
    give = giver(bottom, send)
    give(S_Z, g_z[0:64, 0:128], g_z[64:128, 128:256], keep, 0)
    enc = []
    for cols in (slice(0, 128), slice(128, 256)):
        runs = [g_e[patch_row(t) : patch_row(t) + 3, cols] for t in range(9)]
        enc.append(jnp.concatenate(runs + [jnp.zeros((5, 128), F32)], 0))
    give(S_E, enc[0], enc[1], keep, 0)


def exact_sum(total, first):
    value = sum(total[first + EXACT * i : first + EXACT * (i + 1)] for i in range(3))
    pieces = [piece.astype(F32) for piece in part(value, 3)]
    return jnp.concatenate([total[:first], *pieces, total[first + 3 * EXACT :]], 0).astype(BF)


def merge_kernel(keep, early, got, big, early_out):
    size = keep.shape[0]
    big[...] = (keep[...] + got[0:size].astype(F32)).astype(BF)
    total = early[...].astype(F32) + got[size : size + SMALL - LATE].astype(F32)
    early_out[...] = exact_sum(total, S_X - LATE)


def sum_kernel(parts, out):
    total = parts[0].astype(F32)
    for i in range(1, parts.shape[0]):
        total = total + parts[i].astype(F32)
    out[...] = total.astype(BF)


def update_kernel(
    *refs, stages, start, other
):
    (parts, refs) = refs[:stages], refs[stages:]
    (count, total, ew, e1, e2, zw, z1, z2, dw, d1, d2, ow, o1, o2,
     loss_out, valid_out, count_out, total_out,
     em, es, ep, ec, zm, zs, zp, zc, dm, ds, dp, dc, om, os, op, oc, big, rows) = refs
    share = big.shape[0] // stages
    top = lax.axis_index("level") == 0
    index = (lax.axis_index("dp") >> jnp.where(top, start, other)) & (stages - 1)
    size = big.shape[0] // lax.axis_size("dp")
    small = jnp.zeros((SMALL, W), F32)
    for n, ref in enumerate(parts):
        value = ref[0:share].astype(F32)
        for h in range(share // size):
            place = h * stages + (index ^ n)
            if other != start:
                place = jnp.where(top, place, (index ^ n) * (share // size) + h)
            row = pl.multiple_of(place * size, 8)
            big[pl.ds(row, size), :] = value[h * size : (h + 1) * size]
        small = small + ref[share : share + SMALL].astype(F32)
    exact = sum(small[S_X + EXACT * i : S_X + EXACT * (i + 1)] for i in range(3))
    loss = jnp.sum(exact[4:5, 0:1])
    valid = jnp.sum(exact[4:5, 1:2])
    loss_out[0, 0] = loss
    valid_out[0, 0] = valid
    counts = jnp.concatenate([exact[i : i + 1] for i in range(4)], 1)
    count_out[...] = 0.99 * count[...] + 0.01 * counts
    for quarter in range(4):
        row = TAPS + (quarter % 2) * 128 + (quarter // 2) * 64
        cols = slice(quarter * 128, (quarter + 1) * 128)
        total_out[0, :, cols] = 0.99 * total[0, :, cols] + 0.01 * big[row : row + 64]

    scale = 1.0 - 0.5**STEP

    def adamw(grad, weight, first, second, rate):
        grad = grad / valid
        moment = 0.5 * first + 0.5 * grad
        square = 0.5 * second + 0.5 * grad * grad
        master = weight - rate * (moment / scale / (jnp.sqrt(square / scale) + 1e-08) + 0.01 * weight)
        return moment, square, master

    def whole(grad, w, first, second, rate, outs):
        outs[0][0], outs[1][0], master = adamw(grad, w[0], first[0], second[0], rate)
        outs[2][0] = master
        outs[3][0] = master.astype(BF)

    def by_row(grad, w, first, second, rate, outs):
        n = w.shape[0]
        for i in range(n):
            outs[0][i], outs[1][i], master = adamw(grad[i : i + 1], w[i], first[i], second[i], rate)
            outs[2][i] = master
            rows[i : i + 1] = master
        outs[3][0] = rows[0:n].astype(BF)

    by_row(small[S_E : S_E + 27], ew, e1, e2, RATES[0], (em, es, ep, ec))
    whole(small[S_Z : S_Z + 64], zw, z1, z2, RATES[1], (zm, zs, zp, zc))
    whole(big[0:TAPS], dw, d1, d2, RATES[2], (dm, ds, dp, dc))
    by_row(small[S_O : S_O + 3], ow, o1, o2, RATES[3], (om, os, op, oc))


def radices(devices):
    bits = devices.bit_length() - 1
    return [(start, min(2, bits - start)) for start in range(0, bits, 2)]


def partners(start, width):
    return [k << start for k in range(1, 1 << width)]


def xor_pairs(devices, by, other):
    return [(i, i ^ by) for i in range(devices)] + [(devices + i, devices + (i ^ other)) for i in range(devices)]


def lowered(value):
    return lax.reduce_precision(value, 8, 7)


def sum_small(parts, first):
    total = sum(item.astype(F32) for item in parts)
    value = sum(total[first + EXACT * i : first + EXACT * (i + 1)] for i in range(3))
    high = lowered(value)
    middle = lowered(value - high)
    low = value - high - middle
    rest = total[first + 3 * EXACT :]
    return jnp.concatenate([total[:first], high, middle, low, rest], 0).astype(BF)


def local(
    image, mask, codes, ema_count, ema_sum,
    encoder_weight, encoder_first, encoder_second,
    latent_weight, latent_first, latent_second,
    decoder_weight, decoder_first, decoder_second,
    readout_weight, readout_first, readout_second,
):
    batches, _, band, width = image.shape
    rows = band // 2
    me, devices = lax.axis_index("dp"), lax.axis_size("dp")
    ema_sum = jnp.swapaxes(ema_sum, 1, 2)
    encoder_weight, encoder_first, encoder_second = (
        jnp.swapaxes(item, 0, 1) for item in (encoder_weight, encoder_first, encoder_second)
    )
    latent_weight, latent_first, latent_second = (
        jnp.swapaxes(item, 1, 2) for item in (latent_weight, latent_first, latent_second)
    )
    readout_weight, readout_first, readout_second = (
        jnp.transpose(item, (2, 0, 1)) for item in (readout_weight, readout_first, readout_second)
    )

    def limit(mib):
        return pltpu.CompilerParams(vmem_limit_bytes=mib * 1024 * 1024)

    def outside(*items):
        return [pltpu.with_memory_space_constraint(item, pltpu.HBM) for item in items]

    def inside_vmem(item):
        return pltpu.with_memory_space_constraint(item, pltpu.VMEM)

    swap = [(0, 1), (1, 0)]
    others = lax.ppermute(codes, "level", swap)
    weights = outside(ema_count, ema_sum, encoder_weight, latent_weight, decoder_weight, readout_weight)
    pack = pl.pallas_call(
        pack_kernel,
        out_shape=pltpu.VMEM((PACKED, W), BF),
        in_specs=[VMEM] * 6,
        out_specs=VMEM,
        scratch_shapes=[pltpu.VMEM((128, 128), F32)],
        compiler_params=limit(56),
    )(*weights)
    others, pack = lax.optimization_barrier((others, pack))
    tile, near = pl.pallas_call(
        rows_kernel,
        out_shape=[pltpu.VMEM((batches * band * 8, W), F32), pltpu.VMEM((batches * 16, W), BF)],
        in_specs=[VMEM] * 4,
        out_specs=[VMEM] * 2,
        compiler_params=limit(56),
    )(*outside(image, mask, codes), others)

    both = ("level", "dp")
    inside = [d for d in range(1, devices) if (d + 1) * band % CROP != 0]
    pairs = [(d - 1, d) for d in inside] + [(devices + d, devices + d - 1) for d in inside]
    near = lax.ppermute(near, both, pairs)
    theirs = lax.ppermute(pack, "level", swap)

    u_c = pl.pallas_call(
        functools.partial(lookup_kernel, batches=batches, rows=rows),
        out_shape=pltpu.VMEM((128, batches * (rows + 2) * W), BF),
        in_specs=[VMEM] * 3,
        out_specs=VMEM,
        compiler_params=limit(40),
        cost_estimate=pl.CostEstimate(flops=3 << 30, bytes_accessed=1 << 20, transcendentals=0),
    )(*[inside_vmem(item) for item in (tile, pack, theirs)])
    ext = rows + 4
    pixels = batches * rows * W
    framed = batches * (rows + 2) * W
    held = [
        ((batches, 256, rows * W), BF),
        ((batches, 256, rows * W), F32),
        ((batches, 128, rows * W), F32),
        ((batches, 256, (rows + 2) * W), BF),
    ]
    fixed = [((3, 16, framed), BF), ((384, 768), BF), ((256, 128), BF)]
    size = -(-BIG // (8 * devices)) * 8
    padded = size * devices
    shape = jax.ShapeDtypeStruct
    keep, early, send, *kept = pl.pallas_call(
        functools.partial(step_kernel, batches=batches, rows=rows),
        out_shape=[
            pltpu.VMEM((padded, W), F32),
            pltpu.VMEM((SMALL - LATE, W), BF),
            pltpu.VMEM((padded + SMALL - LATE, W), BF),
            *[shape(*item) for item in held + fixed],
        ],
        in_specs=[VMEM] * 5,
        out_specs=[VMEM] * 3 + [AWAY] * 7,
        scratch_shapes=[
            pltpu.VMEM((batches, ext, 8, W), F32),
            pltpu.VMEM((256, TAPS), BF),
            pltpu.VMEM((256, 128), BF),
            pltpu.VMEM((128, 256), BF),
            pltpu.VMEM((16, 256), BF),
            pltpu.VMEM((256, 16), BF),
            pltpu.VMEM((3, 128, batches * ext * W), BF),
            *[pltpu.VMEM(*item) for item in held + fixed],
            pltpu.VMEM((TAPS, 256), F32),
            pltpu.VMEM((256, 16), F32),
            pltpu.VMEM((2, 144, 256), F32),
            pltpu.VMEM((144, 256), F32),
            pltpu.SemaphoreType.DMA((4, batches)),
            pltpu.SemaphoreType.DMA((3,)),
        ],
        compiler_params=limit(STEP_MIB),
    )(*[inside_vmem(item) for item in (tile, near, pack, theirs, u_c)])

    got = lax.ppermute(send, "level", swap)
    big, early = pl.pallas_call(
        merge_kernel,
        out_shape=[pltpu.VMEM((padded, W), BF), pltpu.VMEM((SMALL - LATE, W), BF)],
        in_specs=[VMEM] * 3,
        out_specs=[VMEM] * 2,
        compiler_params=limit(32),
    )(*[inside_vmem(item) for item in (keep, early, got)])
    big = lax.all_to_all(big.reshape(devices, size, W), "dp", 0, 0)

    late, send = pl.pallas_call(
        functools.partial(back_kernel, batches=batches, rows=rows),
        out_shape=[pltpu.VMEM((LATE, W), BF), pltpu.VMEM((LATE, W), BF)],
        in_specs=[AWAY] * 8,
        out_specs=[VMEM] * 2,
        scratch_shapes=[
            *[pltpu.VMEM(*item) for item in held + fixed],
            pltpu.VMEM((PATCH, 256), F32),
            pltpu.VMEM((128, 256), F32),
            pltpu.SemaphoreType.DMA((4, batches)),
            pltpu.SemaphoreType.DMA((3,)),
        ],
        compiler_params=limit(BACK_MIB),
        cost_estimate=pl.CostEstimate(flops=2 * pixels * 98304 * 4, bytes_accessed=1 << 20, transcendentals=0),
    )(*outside(*kept), got)
    got = lax.ppermute(send, "level", swap)
    late = (late.astype(F32) + got.astype(F32)).astype(BF)
    small = jnp.concatenate([late, early], 0)

    big = pl.pallas_call(
        sum_kernel,
        out_shape=pltpu.VMEM((size, W), BF),
        in_specs=[VMEM],
        out_specs=VMEM,
        compiler_params=limit(32),
        cost_estimate=pl.CostEstimate(flops=1 << 34, bytes_accessed=1 << 20, transcendentals=0),
    )(inside_vmem(big))[None]
    stages = radices(devices)
    crossed = len(stages) == 2 and stages[0][1] == stages[1][1]
    for number, (start, width_bits) in enumerate(reversed(stages)):
        count = 1 << width_bits
        other = stages[number][0] if crossed else start
        index = (me >> jnp.where(lax.axis_index("level") == 0, start, other)) & (count - 1)
        payload = jnp.concatenate([big.reshape(-1, W), small], 0)
        parts = [payload] + [
            lax.ppermute(payload, both, xor_pairs(devices, k << start, k << other)) for k in range(1, count)
        ]
        if number == len(stages) - 1:
            break
        high = big.shape[0]
        stacked = jnp.zeros((high, count, size, W), BF)
        far_first = [0, *range(count - 1, 0, -1)]
        for k in far_first:
            piece = parts[k][: high * size].reshape(high, size, W)
            stacked = lax.dynamic_update_index_in_dim(stacked, piece, index ^ k, 1)
        small = sum_small([parts[k][high * size :] for k in far_first], S_X)
        big = stacked.reshape(high * count, size, W)

    state = (
        ema_count, ema_sum,
        encoder_weight, encoder_first, encoder_second, latent_weight, latent_first, latent_second,
        decoder_weight, decoder_first, decoder_second, readout_weight, readout_first, readout_second,
    )
    outs = [jax.ShapeDtypeStruct((1, 1), F32)] * 2
    outs += [jax.ShapeDtypeStruct(ema_count.shape, F32), jax.ShapeDtypeStruct(ema_sum.shape, F32)]
    for item in (encoder_weight, latent_weight, decoder_weight, readout_weight):
        copy = item.shape if item.shape[0] == 1 else (1, item.shape[0], item.shape[2])
        outs += [jax.ShapeDtypeStruct(item.shape, F32)] * 3 + [jax.ShapeDtypeStruct(copy, BF)]
    result = pl.pallas_call(
        functools.partial(update_kernel, stages=len(parts), start=start, other=other),
        out_shape=outs,
        in_specs=[VMEM] * (len(parts) + len(state)),
        out_specs=[SMEM] * 2 + [VMEM] * (len(outs) - 2),
        scratch_shapes=[pltpu.VMEM((padded, W), F32), pltpu.VMEM((32, W), F32)],
        compiler_params=limit(16),
    )(*parts, *state)
    loss, valid, count_new, total_new = result[:4]
    enc, lat, dec, read = (list(result[4 * n : 4 * n + 4]) for n in range(1, 5))
    enc[:3] = [jnp.swapaxes(item, 0, 1) for item in enc[:3]]
    lat = [jnp.swapaxes(item, 1, 2) for item in lat]
    read = [jnp.transpose(item, (1, 2, 0)) for item in read[:3]] + [jnp.swapaxes(read[3], 1, 2)]
    return (loss.reshape(()), valid.reshape(()), count_new, jnp.swapaxes(total_new, 1, 2), *enc, *lat, *dec, *read)


def solution(mesh):
    rank = (0, 0, 2, 3) + (3,) * 16
    in_specs = (P(None, None, "dp", None), P(None, "dp", None), P("level", None, "dp", None), P("level", None))
    in_specs += (P("level", None, None),) * 13
    out_specs = tuple(P(*(("level",) + (None,) * (n - 1) if n else ())) for n in rank)
    return jax.shard_map(local, mesh=mesh, in_specs=in_specs, out_specs=out_specs, check_vma=False)
```

```python
import functools

import jax
import jax.numpy as jnp
from jax import lax
from jax.experimental import pallas as pl
from jax.experimental.pallas import tpu as pltpu
from jax.sharding import PartitionSpec as P

CROP = 128
STEP = 5
RATES = (0.05, 0.03, 0.01, 0.03)

F32 = jnp.float32
BF = jnp.bfloat16
W = 128
EARLY_MIB, STEP_MIB, BACK_MIB = 36, 36, 56
NOBODY = 300.0

TAPS = 9 * 128
R_ET = TAPS
R_ZN = R_ET + 128
R_ZT = R_ZN + 128
R_OT = R_ZT + 64
R_BT = R_OT + 16
PACKED = R_BT + 256
BIG = TAPS + 256
S_Z, S_E, S_O, S_X = 0, 64, 96, 112
LATE, SMALL = 96, 128
EXACT = 5
PATCH = 96

NN = (((1,), (0,)), ((), ()))
NT = (((1,), (1,)), ((), ()))
VMEM = pl.BlockSpec(memory_space=pltpu.VMEM)
SMEM = pl.BlockSpec(memory_space=pltpu.SMEM)
AWAY = pl.BlockSpec(memory_space=pl.ANY)


def dot(a, b, dims=NN):
    return lax.dot_general(a, b, dims, preferred_element_type=F32)


def part(value, count):
    out = []
    for _ in range(count):
        piece = value.astype(BF)
        out.append(piece)
        value = value - piece.astype(F32)
    return out


def patch_row(t):
    dr, dc = t // 3, t % 3
    return ((dr // 2) * 3 + dc) * 16 + (dr % 2) * 8


def rows_kernel(image, mask, codes, others, tile, near):
    level = lax.axis_index("level")
    batches, _, band, _ = image.shape

    def fitted(code):
        return jnp.where(code < 256, code, code - 512).astype(F32)

    for b in range(batches):
        base = b * band * 8
        shown = image[b].astype(F32)
        for c in range(3):
            tile[pl.ds(base + c, band, stride=8), :] = shown[c]
        tile[pl.ds(base + 3, band, stride=8), :] = mask[b].astype(F32)
        mine, theirs = fitted(codes[0, b]), fitted(others[0, b])
        tile[pl.ds(base + 4, band, stride=8), :] = jnp.where(level == 1, mine, theirs)
        tile[pl.ds(base + 5, band, stride=8), :] = jnp.where(level == 1, theirs, mine)
        for c in range(6, 8):
            tile[pl.ds(base + c, band, stride=8), :] = jnp.zeros((band, W), F32)
    for b in range(batches):
        row = jnp.where(level == 0, band - 2, 0)
        start = pl.multiple_of((b * band + row) * 8, 8)
        near[b * 16 : (b + 1) * 16] = tile[pl.ds(start, 16), :].astype(BF)


def pack_kernel(count, total, enc, lat, dec, read, pack, flat):
    pack[0:TAPS] = dec[0].astype(BF)
    flat[...] = jnp.zeros_like(flat)
    for t in range(9):
        for c in range(3):
            row = patch_row(t) + c
            flat[row : row + 1] = enc[3 * t + c]
    pack[R_ET : R_ET + 128] = flat[...].T.astype(BF)
    flat[...] = jnp.zeros_like(flat)
    flat[0:64] = lat[0]
    pack[R_ZT : R_ZT + 64] = lat[0].astype(BF)
    pack[R_ZN : R_ZN + 128] = flat[...].T.astype(BF)
    blank = jnp.zeros((13, 128), F32)
    pack[R_OT : R_OT + 16] = jnp.concatenate([read[0], read[1], read[2], blank], 0).astype(BF)
    book = total[0] / count[...]
    for quarter in range(4):
        row = R_BT + (quarter % 2) * 128 + (quarter // 2) * 64
        pack[row : row + 64] = book[:, quarter * 128 : (quarter + 1) * 128].astype(BF)


def sides(v):
    lane = lax.broadcasted_iota(jnp.int32, (v.shape[0], W), 1)
    before, after = [], []
    for i in range(v.shape[1] // W):
        row = v[:, i * W : (i + 1) * W]
        before.append(jnp.where(lane == 0, 0.0, pltpu.roll(row, 1, 1)))
        after.append(jnp.where(lane == W - 1, 0.0, pltpu.roll(row, W - 1, 1)))
    if len(before) == 1:
        return before[0], v, after[0]
    return jnp.concatenate(before, 1), v, jnp.concatenate(after, 1)


def at(row, rows):
    return pl.ds(pl.multiple_of(row * W, W), rows * W)


def fold(v, width):
    return sum(v[:, i : i + width] for i in range(0, v.shape[1], width))


def silu_parts(half):
    p = jnp.tanh(half) + 1.0
    out = half * p
    return out, p + out * (2.0 - p)


def one_hots(here):
    ids = lax.broadcasted_iota(jnp.int32, (256, here.shape[1]), 0).astype(F32)
    onehots, highs = [], []
    for v in range(2):
        code = here[4 + v : 5 + v]
        high = code < 0.0
        low = jnp.where(high, code + 256.0, code)
        onehots.append(jnp.where(ids == low, 1.0, 0.0).astype(BF))
        highs.append(high)
    return onehots, highs


def quantized(onehots, highs, bt):
    quants = []
    for onehot, high, book in zip(onehots, highs, bt):
        both = dot(book, onehot)
        quants.append(jnp.where(high, both[64:128], both[0:64]))
    return jnp.concatenate(quants, 0)


def books(mine, theirs, bottom):
    a, b = (jnp.concatenate([pack[R_BT : R_BT + 128], pack[R_BT + 128 : R_BT + 256]], 1) for pack in (mine, theirs))
    return jnp.where(bottom, a, b), jnp.where(bottom, b, a)


def either(mine, theirs, bottom, start, size):
    a, b = mine[start : start + size], theirs[start : start + size]
    return jnp.where(bottom, a, b), jnp.where(bottom, b, a)


def encoder_weights(mine, theirs, bottom, et, zt):
    one, zero = either(mine, theirs, bottom, R_ET, 128)
    et[0:128] = (0.5 * one.astype(F32)).astype(BF)
    et[128:256] = (0.5 * zero.astype(F32)).astype(BF)
    one, zero = either(mine, theirs, bottom, R_ZT, 64)
    blank = jnp.zeros((64, 128), BF)
    zt[0:64] = jnp.concatenate([one, blank], 1)
    zt[64:128] = jnp.concatenate([blank, zero], 1)


def encoded(x, u, k, onehots, highs, et, zt, g_s):
    h, slope = silu_parts(dot(et[:, 0:PATCH], x))
    h = h.astype(BF)
    z = dot(zt[...], h)
    gap = z - u
    kept = k * gap
    z = k * z.astype(BF).astype(F32)
    row = lax.broadcasted_iota(jnp.int32, (16, z.shape[1]), 0)
    for v in range(2):
        part_z = z[v * 64 : v * 64 + 64]
        high = highs[v]
        low_k = jnp.where(high, 0.0, k)
        high_k = jnp.where(high, k, 0.0)
        left = jnp.concatenate(
            [
                jnp.where(high, 0.0, part_z),
                jnp.where(high, part_z, 0.0),
                jnp.where(row == 0, low_k, jnp.where(row == 1, high_k, 0.0)),
            ],
            0,
        ).astype(BF)
        g_s[v] += dot(left, onehots[v], NT)
    return h, slope, 0.5 * kept, kept * gap


def early_kernel(
    tile, mine, theirs,
    u_s, h_s, slope_s, gap_s, x_s, g_s, l_s, et, zt,
    *, batches, rows,
):
    level = lax.axis_index("level")
    bottom = level == 1
    edge = level * (rows - 1)
    bt = books(mine, theirs, bottom)
    encoder_weights(mine, theirs, bottom, et, zt)
    for ref in (g_s, l_s):
        ref[...] = jnp.zeros_like(ref)

    def batch(b, _):
        def row(i):
            return tile[pl.ds(pl.multiple_of((b * 2 * rows + i) * 8, 8), 8), :]

        run = [row(jnp.clip(level * rows + r, 0, 2 * rows - 1)) for r in range(-1, rows + 2)]
        value = jnp.concatenate([jnp.concatenate(run[i : i + 2], 0) for i in range(rows + 2)], 1)
        for dc, view in enumerate(sides(value)):
            x_s[dc, :, at(b * (rows + 2), rows + 2)] = view.astype(BF)
        own = run[1 : rows + 1]
        beyond = [row(rows - 2 * level + i) for i in range(2)]
        onehots, highs = one_hots(jnp.concatenate(own + beyond, 1))
        u = quantized(onehots, highs, bt)
        inner = slice(0, rows * W)
        for k, view in enumerate(sides(u)):
            view = view.astype(BF)
            u_s[k, :, at(b * (rows + 4) + 2, rows)] = view[:, inner]
            u_s[k, :, at(b * (rows + 4) + (rows + 2) * (1 - level), 2)] = view[:, rows * W :]
        k = jnp.concatenate([jnp.where(edge == i, 0.0, own[i][3:4]) for i in range(rows)], 1)
        h, slope, gap, error = encoded(
            patches(x_s, b * (rows + 2), rows), u[:, inner], k,
            [item[:, inner] for item in onehots], [item[:, inner] for item in highs], et, zt, g_s,
        )
        h_s[b] = h
        slope_s[b] = slope
        gap_s[b] = gap
        l_s[0:128] += fold(error, 256)
        return 0

    lax.fori_loop(0, batches, batch, 0)


def patches(x_s, row, n):
    return jnp.concatenate([x_s[dc, :, at(row + pair, n)] for pair in (0, 2) for dc in range(3)], 0)


def giver(bottom, send):
    def give(start, one, zero, keep, offset, shift=0):
        n = one.shape[0]
        keep[start - shift : start - shift + n] = jnp.where(bottom, one, zero).astype(keep.dtype)
        start = offset + start - shift
        send[start : start + n] = jnp.where(bottom, zero, one).astype(BF)

    return give


def spread_back(dn, da):
    rows = da.shape[1] // W - 2
    near = jnp.concatenate([da[:, (2 - dr) * W : (2 - dr + rows) * W] for dr in range(3)], 0)
    spread = dot(dn[...], near)
    _, _, after = sides(spread[0:128])
    before, _, _ = sides(spread[256:384])
    return after + spread[128:256] + before


def encoder_back(du, gap, h, slope, x, zn, g_z, g_e):
    dz = (du + gap).astype(BF)
    g_z[...] += dot(dz, h, NT)
    dpre = (dot(zn[...], dz) * slope).astype(BF)
    g_e[...] += dot(x, dpre, NT)


def step_kernel(
    tile, near, mine, theirs, *refs,
    batches, rows,
):
    (keep_big, keep_small, send, h_out, slope_out, gap_out, da_out, x_out, dn_out, zn_out,
     u_s, h_s, slope_s, gap_s, x_s, g_s, l_s,
     t_s, dt, et, zt, ot, on, da_s, dn, zn, g_d, g_o, sems, fixed_sems) = refs[7:]
    level, me, devices = lax.axis_index("level"), lax.axis_index("dp"), lax.axis_size("dp")
    band, ext = 2 * rows, rows + 4
    above, below = (me + 1) * band, (me + 2) * band
    top_ok = (lax.rem(above, CROP) != 0) & (me > 0)
    bottom_ok = (lax.rem(below, CROP) != 0) & (me < devices - 1)
    valid = jnp.where(level == 0, top_ok.astype(jnp.int32), bottom_ok.astype(jnp.int32))
    bottom = level == 1

    def pair(start, size):
        return either(mine, theirs, bottom, start, size)

    for t in range(9):
        one, zero = pair(t * 128, 128)
        zero = jnp.concatenate([jnp.zeros((64, 128), BF), zero[0:64]], 0)
        dr, dc = t // 3, t % 3
        dn[dc * 128 : (dc + 1) * 128, dr * 256 : dr * 256 + 128] = one
        dn[dc * 128 : (dc + 1) * 128, dr * 256 + 128 : (dr + 1) * 256] = zero
        dt[0:128, t * 128 : (t + 1) * 128] = (0.5 * one.astype(F32)).T.astype(BF)
        dt[128:256, t * 128 : (t + 1) * 128] = (0.5 * zero.astype(F32)).T.astype(BF)
    encoder_weights(mine, theirs, bottom, et, zt)
    one, zero = pair(R_ZN, 128)
    zn[0:128] = (0.5 * one.astype(F32)).astype(BF)
    zn[128:256] = pltpu.roll(0.5 * zero.astype(F32), 64, 1).astype(BF)
    one, zero = pair(R_OT, 16)
    blank = jnp.zeros((8, 128), F32)
    out_t = jnp.concatenate(
        [
            jnp.concatenate([one[0:8].astype(F32), blank], 1),
            jnp.concatenate([blank, zero[0:8].astype(F32)], 1),
        ],
        0,
    )
    ot[...] = out_t.astype(BF)
    on[...] = (0.5 * out_t).T.astype(BF)
    bt = books(mine, theirs, bottom)
    fixed = [
        pltpu.make_async_copy(a, o, fixed_sems.at[n])
        for n, (a, o) in enumerate(((x_s, x_out), (dn, dn_out), (zn, zn_out)))
    ]
    fixed[1].start()
    fixed[2].start()

    sub = lax.broadcasted_iota(jnp.int32, (8, W), 0)
    nothing = jnp.where((sub == 4) | (sub == 5), NOBODY, 0.0)

    outside = []
    for b in range(batches):
        both = near[b * 16 : (b + 1) * 16].astype(F32)
        for r in range(2):
            outside.append(jnp.where(valid > 0, both[r * 8 : (r + 1) * 8], nothing))
    for i, shown in enumerate(outside):
        t_s[i] = shown

    def row(b, r):
        return tile[pl.ds(pl.multiple_of((b * band + r) * 8, 8), 8), :]

    for ref in (g_d, g_o):
        ref[...] = jnp.zeros_like(ref)

    def spread_rows(u, b, e, n):
        for k, view in enumerate(sides(u)):
            u_s[k, :, at(b * ext + e, n)] = view.astype(BF)

    first = level * rows
    runs = []
    for b in range(batches):
        low, high = outside[2 * b], outside[2 * b + 1]
        runs.append(jnp.concatenate([jnp.where(bottom, row(b, band - 1), high), jnp.where(bottom, low, row(b, 0))], 0))
        runs.append(jnp.concatenate([jnp.where(bottom, low, row(b, 0)), jnp.where(bottom, high, row(b, 1))], 0))
    for dc, view in enumerate(sides(jnp.concatenate(runs, 1))):
        view = view.astype(BF)
        for b in range(batches):
            x_s[dc, :, at(b * (rows + 2) + first, 2)] = view[:, b * 2 * W : (b + 1) * 2 * W]
    outer, edge = jnp.where(bottom, rows + 2, 0), level * (rows - 1)
    u = quantized(*one_hots(jnp.concatenate(outside, 1)), bt)
    for b in range(batches):
        spread_rows(u[:, b * 2 * W : (b + 1) * 2 * W], b, outer, 2)
    here = jnp.concatenate([row(b, level * (band - 1)) for b in range(batches)], 1)
    u = jnp.concatenate([u_s[1, :, at(b * ext + 2 + edge, 1)] for b in range(batches)], 1).astype(F32)
    x = jnp.concatenate([patches(x_s, b * (rows + 2) + edge, 1) for b in range(batches)], 1)
    h, slope, gap, error = encoded(x, u, here[3:4], *one_hots(here), et, zt, g_s)
    l_s[0:128, 0:W] += fold(error, W)
    for b in range(batches):
        cols = slice(b * W, (b + 1) * W)
        h_s[b, :, at(edge, 1)] = h[:, cols]
        slope_s[b, :, at(edge, 1)] = slope[:, cols]
        gap_s[b, :, at(edge, 1)] = gap[:, cols]

    pairs = ((h_s, h_out), (slope_s, slope_out), (gap_s, gap_out), (da_s, da_out))

    def leave(b, which=range(4)):
        return [pltpu.make_async_copy(pairs[n][0].at[b], pairs[n][1].at[b], sems.at[n, b]) for n in which]

    fixed[0].start()
    for b in range(batches):
        for copy in leave(b, range(3)):
            copy.start()

    def decode(b, _):
        u = jnp.concatenate(
            [u_s[dc, :, at(b * ext + dr, rows + 2)] for dr in range(3) for dc in range(3)], 0
        )
        inner = slice(W, (1 + rows) * W)
        g, slope = silu_parts(dot(dt[...], u))
        g = g.astype(BF)
        y = dot(ot[...], g)
        shown = [row(b, jnp.clip(level * rows + r, 0, band - 1)) for r in range(-1, rows + 1)]
        shown[0] = jnp.where(bottom, shown[0], t_s[2 * b + 1])
        shown[-1] = jnp.where(bottom, t_s[2 * b], shown[-1])
        here = jnp.concatenate(shown, 1)
        k = here[3:4]
        x = jnp.where(lax.broadcasted_iota(jnp.int32, here.shape, 0) < 3, here, 0.0)
        diff = y - jnp.concatenate([x, x], 0)
        kept = k * diff
        dy = (2.0 * kept).astype(BF)
        da = (dot(on[...], dy) * slope).astype(BF)
        da_s[b] = da
        leave(b, [3])[0].start()
        l_s[128:144] += fold((kept * diff)[:, inner], 256)
        g_o[...] += dot(g[:, inner], dy[:, inner], NT)
        g_d[...] += dot(u[:, inner], da[:, inner], NT)
        return 0

    lax.fori_loop(0, batches, decode, 0)
    give = giver(bottom, send)
    for t in range(9):
        top = jnp.concatenate([g_d[t * 128 + 64 : (t + 1) * 128, 128:256], jnp.zeros((64, 128), F32)], 0)
        give(t * 128, g_d[t * 128 : (t + 1) * 128, 0:128], top, keep_big, 0)
    for half in range(2):
        cols = slice(half * 128, (half + 1) * 128)
        give(TAPS + half * 128, g_s[0, 0:128, cols], g_s[1, 0:128, cols], keep_big, 0)
    pad = keep_big.shape[0]
    if pad > BIG:
        keep_big[BIG:pad] = jnp.zeros((pad - BIG, W), F32)
        send[BIG:pad] = jnp.zeros((pad - BIG, W), BF)
    readouts = g_o[...].T
    blank = jnp.zeros((8, 128), F32)
    give(
        S_O,
        jnp.concatenate([readouts[0:8, 0:128], blank], 0),
        jnp.concatenate([readouts[8:16, 128:256], blank], 0),
        keep_small,
        pad,
        LATE,
    )
    valid_sum = jnp.sum(g_s[0, 128:130])
    loss = 0.25 * jnp.sum(l_s[0:128]) + jnp.sum(l_s[128:144])
    lane = lax.broadcasted_iota(jnp.int32, (1, W), 1)
    other = jnp.where(lane == 0, loss, jnp.where(lane == 1, valid_sum, 0.0))
    exact = []
    for v in range(2):
        runs = [g_s[v, 128 + hi : 129 + hi, half * 128 : (half + 1) * 128] for hi in range(2) for half in range(2)]
        pieces = part(jnp.concatenate(runs + [other], 0), 3)
        exact.append(jnp.concatenate([p.astype(F32) for p in pieces] + [jnp.zeros((1, 128), F32)], 0))
    give(S_X, exact[0], exact[1], keep_small, pad, LATE)
    for copy in fixed + [copy for b in range(batches) for copy in leave(b)]:
        copy.wait()


def back_kernel(
    h_in, slope_in, gap_in, da_in, x_in, dn_in, zn_in, _,
    keep, send, h_s, slope_s, gap_s, da_s, x_s, dn, zn, g_e, g_z, sems, fixed_sems,
    *, batches, rows,
):
    bottom = lax.axis_index("level") == 1
    pairs = ((h_in, h_s), (slope_in, slope_s), (gap_in, gap_s), (da_in, da_s))

    def fetch(b):
        return [pltpu.make_async_copy(a.at[b], o.at[b], sems.at[n, b]) for n, (a, o) in enumerate(pairs)]

    fixed = [
        pltpu.make_async_copy(a, o, fixed_sems.at[n])
        for n, (a, o) in enumerate(((dn_in, dn), (zn_in, zn), (x_in, x_s)))
    ]
    count = h_s.shape[0]
    copies = [fetch(b) for b in range(count)]
    for copy in [fixed[0], copies[0][3], copies[0][2], fixed[1], *copies[0][:2], fixed[2]]:
        copy.start()
    g_e[...] = jnp.zeros_like(g_e)
    g_z[...] = jnp.zeros_like(g_z)
    fixed[0].wait()
    copies[0][3].wait()
    for b in range(1, count):
        for n in (3, 2, 0, 1):
            copies[b][n].start()
    du = spread_back(dn, da_s[0])
    for copy in [fixed[1], fixed[2]]:
        copy.wait()
    for b in range(count):
        for copy in copies[b][:3]:
            copy.wait()
        if b + 1 < count:
            copies[b + 1][3].wait()
        row = b * (rows + 2)
        encoder_back(du, gap_s[b], h_s[b], slope_s[b], patches(x_s, row, rows), zn, g_z, g_e)
        if b + 1 < count:
            du = spread_back(dn, da_s[b + 1])
    give = giver(bottom, send)
    give(S_Z, g_z[0:64, 0:128], g_z[64:128, 128:256], keep, 0)
    enc = []
    for cols in (slice(0, 128), slice(128, 256)):
        runs = [g_e[patch_row(t) : patch_row(t) + 3, cols] for t in range(9)]
        enc.append(jnp.concatenate(runs + [jnp.zeros((5, 128), F32)], 0))
    give(S_E, enc[0], enc[1], keep, 0)


def exact_sum(total, first):
    value = sum(total[first + EXACT * i : first + EXACT * (i + 1)] for i in range(3))
    pieces = [piece.astype(F32) for piece in part(value, 3)]
    return jnp.concatenate([total[:first], *pieces, total[first + 3 * EXACT :]], 0).astype(BF)


def merge_kernel(keep, early, got, big, early_out):
    size = keep.shape[0]
    big[...] = (keep[...] + got[0:size].astype(F32)).astype(BF)
    total = early[...].astype(F32) + got[size : size + SMALL - LATE].astype(F32)
    early_out[...] = exact_sum(total, S_X - LATE)


def sum_kernel(parts, out):
    total = parts[0].astype(F32)
    for i in range(1, parts.shape[0]):
        total = total + parts[i].astype(F32)
    out[...] = total.astype(BF)


def update_kernel(
    *refs, stages, start, other
):
    (parts, refs) = refs[:stages], refs[stages:]
    (count, total, ew, e1, e2, zw, z1, z2, dw, d1, d2, ow, o1, o2,
     loss_out, valid_out, count_out, total_out,
     em, es, ep, ec, zm, zs, zp, zc, dm, ds, dp, dc, om, os, op, oc, big, rows) = refs
    share = big.shape[0] // stages
    top = lax.axis_index("level") == 0
    index = (lax.axis_index("dp") >> jnp.where(top, start, other)) & (stages - 1)
    size = big.shape[0] // lax.axis_size("dp")
    small = jnp.zeros((SMALL, W), F32)
    for n, ref in enumerate(parts):
        value = ref[0:share].astype(F32)
        for h in range(share // size):
            place = h * stages + (index ^ n)
            if other != start:
                place = jnp.where(top, place, (index ^ n) * (share // size) + h)
            row = pl.multiple_of(place * size, 8)
            big[pl.ds(row, size), :] = value[h * size : (h + 1) * size]
        small = small + ref[share : share + SMALL].astype(F32)
    exact = sum(small[S_X + EXACT * i : S_X + EXACT * (i + 1)] for i in range(3))
    loss = jnp.sum(exact[4:5, 0:1])
    valid = jnp.sum(exact[4:5, 1:2])
    loss_out[0, 0] = loss
    valid_out[0, 0] = valid
    counts = jnp.concatenate([exact[i : i + 1] for i in range(4)], 1)
    count_out[...] = 0.99 * count[...] + 0.01 * counts
    for quarter in range(4):
        row = TAPS + (quarter % 2) * 128 + (quarter // 2) * 64
        cols = slice(quarter * 128, (quarter + 1) * 128)
        total_out[0, :, cols] = 0.99 * total[0, :, cols] + 0.01 * big[row : row + 64]

    scale = 1.0 - 0.5**STEP

    def adamw(grad, weight, first, second, rate):
        grad = grad / valid
        moment = 0.5 * first + 0.5 * grad
        square = 0.5 * second + 0.5 * grad * grad
        master = weight - rate * (moment / scale / (jnp.sqrt(square / scale) + 1e-08) + 0.01 * weight)
        return moment, square, master

    def whole(grad, w, first, second, rate, outs):
        outs[0][0], outs[1][0], master = adamw(grad, w[0], first[0], second[0], rate)
        outs[2][0] = master
        outs[3][0] = master.astype(BF)

    def by_row(grad, w, first, second, rate, outs):
        n = w.shape[0]
        for i in range(n):
            outs[0][i], outs[1][i], master = adamw(grad[i : i + 1], w[i], first[i], second[i], rate)
            outs[2][i] = master
            rows[i : i + 1] = master
        outs[3][0] = rows[0:n].astype(BF)

    by_row(small[S_E : S_E + 27], ew, e1, e2, RATES[0], (em, es, ep, ec))
    whole(small[S_Z : S_Z + 64], zw, z1, z2, RATES[1], (zm, zs, zp, zc))
    whole(big[0:TAPS], dw, d1, d2, RATES[2], (dm, ds, dp, dc))
    by_row(small[S_O : S_O + 3], ow, o1, o2, RATES[3], (om, os, op, oc))


def radices(devices):
    bits = devices.bit_length() - 1
    return [(start, min(2, bits - start)) for start in range(0, bits, 2)]


def partners(start, width):
    return [k << start for k in range(1, 1 << width)]


def xor_pairs(devices, by, other):
    return [(i, i ^ by) for i in range(devices)] + [(devices + i, devices + (i ^ other)) for i in range(devices)]


def lowered(value):
    return lax.reduce_precision(value, 8, 7)


def sum_small(parts, first):
    total = sum(item.astype(F32) for item in parts)
    value = sum(total[first + EXACT * i : first + EXACT * (i + 1)] for i in range(3))
    high = lowered(value)
    middle = lowered(value - high)
    low = value - high - middle
    rest = total[first + 3 * EXACT :]
    return jnp.concatenate([total[:first], high, middle, low, rest], 0).astype(BF)


def local(
    image, mask, codes, ema_count, ema_sum,
    encoder_weight, encoder_first, encoder_second,
    latent_weight, latent_first, latent_second,
    decoder_weight, decoder_first, decoder_second,
    readout_weight, readout_first, readout_second,
):
    batches, _, band, width = image.shape
    rows = band // 2
    me, devices = lax.axis_index("dp"), lax.axis_size("dp")
    ema_sum = jnp.swapaxes(ema_sum, 1, 2)
    encoder_weight, encoder_first, encoder_second = (
        jnp.swapaxes(item, 0, 1) for item in (encoder_weight, encoder_first, encoder_second)
    )
    latent_weight, latent_first, latent_second = (
        jnp.swapaxes(item, 1, 2) for item in (latent_weight, latent_first, latent_second)
    )
    readout_weight, readout_first, readout_second = (
        jnp.transpose(item, (2, 0, 1)) for item in (readout_weight, readout_first, readout_second)
    )

    def limit(mib):
        return pltpu.CompilerParams(vmem_limit_bytes=mib * 1024 * 1024)

    def outside(*items):
        return [pltpu.with_memory_space_constraint(item, pltpu.HBM) for item in items]

    def inside_vmem(item):
        return pltpu.with_memory_space_constraint(item, pltpu.VMEM)

    swap = [(0, 1), (1, 0)]
    others = lax.ppermute(codes, "level", swap)
    weights = outside(ema_count, ema_sum, encoder_weight, latent_weight, decoder_weight, readout_weight)
    pack = pl.pallas_call(
        pack_kernel,
        out_shape=pltpu.VMEM((PACKED, W), BF),
        in_specs=[VMEM] * 6,
        out_specs=VMEM,
        scratch_shapes=[pltpu.VMEM((128, 128), F32)],
        compiler_params=limit(56),
    )(*weights)
    others, pack = lax.optimization_barrier((others, pack))
    tile, near = pl.pallas_call(
        rows_kernel,
        out_shape=[pltpu.VMEM((batches * band * 8, W), F32), pltpu.VMEM((batches * 16, W), BF)],
        in_specs=[VMEM] * 4,
        out_specs=[VMEM] * 2,
        compiler_params=limit(56),
    )(*outside(image, mask, codes), others)

    both = ("level", "dp")
    inside = [d for d in range(1, devices) if (d + 1) * band % CROP != 0]
    pairs = [(d - 1, d) for d in inside] + [(devices + d, devices + d - 1) for d in inside]
    near = lax.ppermute(near, both, pairs)
    theirs = lax.ppermute(pack, "level", swap)

    ext = rows + 4
    ext = rows + 4
    pixels = batches * rows * W
    framed = batches * (rows + 2) * W
    held = [
        ((batches, 256, rows * W), BF),
        ((batches, 256, rows * W), F32),
        ((batches, 128, rows * W), F32),
        ((batches, 256, (rows + 2) * W), BF),
    ]
    fixed = [((3, 16, framed), BF), ((384, 768), BF), ((256, 128), BF)]
    size = -(-BIG // (8 * devices)) * 8
    padded = size * devices
    shape = jax.ShapeDtypeStruct
    staged = [
        pltpu.VMEM((3, 128, batches * ext * W), BF),
        *[pltpu.VMEM(*item) for item in held[:3]],
        pltpu.VMEM(*fixed[0]),
        pltpu.VMEM((2, 144, 256), F32),
        pltpu.VMEM((144, 256), F32),
    ]
    stages_early = pl.pallas_call(
        functools.partial(early_kernel, batches=batches, rows=rows),
        out_shape=staged,
        in_specs=[VMEM] * 3,
        out_specs=[VMEM] * 7,
        scratch_shapes=[pltpu.VMEM((256, 128), BF), pltpu.VMEM((128, 256), BF)],
        compiler_params=limit(EARLY_MIB),
        cost_estimate=pl.CostEstimate(flops=3 << 30, bytes_accessed=1 << 20, transcendentals=0),
    )(*[inside_vmem(item) for item in (tile, pack, theirs)])
    results = pl.pallas_call(
        functools.partial(step_kernel, batches=batches, rows=rows),
        out_shape=[
            pltpu.VMEM((padded, W), F32),
            pltpu.VMEM((SMALL - LATE, W), BF),
            pltpu.VMEM((padded + SMALL - LATE, W), BF),
            *[shape(*item) for item in held + fixed],
            *staged,
        ],
        in_specs=[VMEM] * 11,
        out_specs=[VMEM] * 3 + [AWAY] * 7 + [VMEM] * 7,
        input_output_aliases={4 + i: 10 + i for i in range(7)},
        scratch_shapes=[
            pltpu.VMEM((2 * batches, 8, W), F32),
            pltpu.VMEM((256, TAPS), BF),
            pltpu.VMEM((256, 128), BF),
            pltpu.VMEM((128, 256), BF),
            pltpu.VMEM((16, 256), BF),
            pltpu.VMEM((256, 16), BF),
            pltpu.VMEM(*held[3]),
            *[pltpu.VMEM(*item) for item in fixed[1:]],
            pltpu.VMEM((TAPS, 256), F32),
            pltpu.VMEM((256, 16), F32),
            pltpu.SemaphoreType.DMA((4, batches)),
            pltpu.SemaphoreType.DMA((3,)),
        ],
        compiler_params=limit(STEP_MIB),
    )(*[inside_vmem(item) for item in (tile, near, pack, theirs, *stages_early)])
    keep, early, send = results[:3]
    kept = results[3:10]

    got = lax.ppermute(send, "level", swap)
    big, early = pl.pallas_call(
        merge_kernel,
        out_shape=[pltpu.VMEM((padded, W), BF), pltpu.VMEM((SMALL - LATE, W), BF)],
        in_specs=[VMEM] * 3,
        out_specs=[VMEM] * 2,
        compiler_params=limit(32),
    )(*[inside_vmem(item) for item in (keep, early, got)])
    big = lax.all_to_all(big.reshape(devices, size, W), "dp", 0, 0)

    late, send = pl.pallas_call(
        functools.partial(back_kernel, batches=batches, rows=rows),
        out_shape=[pltpu.VMEM((LATE, W), BF), pltpu.VMEM((LATE, W), BF)],
        in_specs=[AWAY] * 8,
        out_specs=[VMEM] * 2,
        scratch_shapes=[
            *[pltpu.VMEM(*item) for item in held + fixed],
            pltpu.VMEM((PATCH, 256), F32),
            pltpu.VMEM((128, 256), F32),
            pltpu.SemaphoreType.DMA((4, batches)),
            pltpu.SemaphoreType.DMA((3,)),
        ],
        compiler_params=limit(BACK_MIB),
        cost_estimate=pl.CostEstimate(flops=2 * pixels * 98304 * 4, bytes_accessed=1 << 20, transcendentals=0),
    )(*outside(*kept), got)
    got = lax.ppermute(send, "level", swap)
    late = (late.astype(F32) + got.astype(F32)).astype(BF)
    small = jnp.concatenate([late, early], 0)

    big = pl.pallas_call(
        sum_kernel,
        out_shape=pltpu.VMEM((size, W), BF),
        in_specs=[VMEM],
        out_specs=VMEM,
        compiler_params=limit(32),
        cost_estimate=pl.CostEstimate(flops=1 << 34, bytes_accessed=1 << 20, transcendentals=0),
    )(inside_vmem(big))[None]
    stages = radices(devices)
    crossed = len(stages) == 2 and stages[0][1] == stages[1][1]
    for number, (start, width_bits) in enumerate(reversed(stages)):
        count = 1 << width_bits
        other = stages[number][0] if crossed else start
        index = (me >> jnp.where(lax.axis_index("level") == 0, start, other)) & (count - 1)
        payload = jnp.concatenate([big.reshape(-1, W), small], 0)
        parts = [payload] + [
            lax.ppermute(payload, both, xor_pairs(devices, k << start, k << other)) for k in range(1, count)
        ]
        if number == len(stages) - 1:
            break
        high = big.shape[0]
        stacked = jnp.zeros((high, count, size, W), BF)
        far_first = [0, *range(count - 1, 0, -1)]
        for k in far_first:
            piece = parts[k][: high * size].reshape(high, size, W)
            stacked = lax.dynamic_update_index_in_dim(stacked, piece, index ^ k, 1)
        small = sum_small([parts[k][high * size :] for k in far_first], S_X)
        big = stacked.reshape(high * count, size, W)

    state = (
        ema_count, ema_sum,
        encoder_weight, encoder_first, encoder_second, latent_weight, latent_first, latent_second,
        decoder_weight, decoder_first, decoder_second, readout_weight, readout_first, readout_second,
    )
    outs = [jax.ShapeDtypeStruct((1, 1), F32)] * 2
    outs += [jax.ShapeDtypeStruct(ema_count.shape, F32), jax.ShapeDtypeStruct(ema_sum.shape, F32)]
    for item in (encoder_weight, latent_weight, decoder_weight, readout_weight):
        copy = item.shape if item.shape[0] == 1 else (1, item.shape[0], item.shape[2])
        outs += [jax.ShapeDtypeStruct(item.shape, F32)] * 3 + [jax.ShapeDtypeStruct(copy, BF)]
    result = pl.pallas_call(
        functools.partial(update_kernel, stages=len(parts), start=start, other=other),
        out_shape=outs,
        in_specs=[VMEM] * (len(parts) + len(state)),
        out_specs=[SMEM] * 2 + [VMEM] * (len(outs) - 2),
        scratch_shapes=[pltpu.VMEM((padded, W), F32), pltpu.VMEM((32, W), F32)],
        compiler_params=limit(16),
    )(*parts, *state)
    loss, valid, count_new, total_new = result[:4]
    enc, lat, dec, read = (list(result[4 * n : 4 * n + 4]) for n in range(1, 5))
    enc[:3] = [jnp.swapaxes(item, 0, 1) for item in enc[:3]]
    lat = [jnp.swapaxes(item, 1, 2) for item in lat]
    read = [jnp.transpose(item, (1, 2, 0)) for item in read[:3]] + [jnp.swapaxes(read[3], 1, 2)]
    return (loss.reshape(()), valid.reshape(()), count_new, jnp.swapaxes(total_new, 1, 2), *enc, *lat, *dec, *read)


def solution(mesh):
    rank = (0, 0, 2, 3) + (3,) * 16
    in_specs = (P(None, None, "dp", None), P(None, "dp", None), P("level", None, "dp", None), P("level", None))
    in_specs += (P("level", None, None),) * 13
    out_specs = tuple(P(*(("level",) + (None,) * (n - 1) if n else ())) for n in rank)
    return jax.shard_map(local, mesh=mesh, in_specs=in_specs, out_specs=out_specs, check_vma=False)
```

```python
import functools

import jax
import jax.numpy as jnp
from jax import lax
from jax.experimental import pallas as pl
from jax.experimental.pallas import tpu as pltpu
from jax.sharding import PartitionSpec as P

CROP = 128
STEP = 5
RATES = (0.05, 0.03, 0.01, 0.03)

F32 = jnp.float32
BF = jnp.bfloat16
W = 128
EARLY_MIB, STEP_MIB, BACK_MIB = 36, 36, 56
NOBODY = 300.0

TAPS = 9 * 128
R_ET = TAPS
R_ZN = R_ET + 128
R_ZT = R_ZN + 128
R_OT = R_ZT + 64
R_BT = R_OT + 16
PACKED = R_BT + 256
BIG = TAPS + 256
S_Z, S_E, S_O, S_X = 0, 64, 96, 112
LATE, SMALL = 96, 128
EXACT = 5
PATCH = 96

NN = (((1,), (0,)), ((), ()))
NT = (((1,), (1,)), ((), ()))
VMEM = pl.BlockSpec(memory_space=pltpu.VMEM)
SMEM = pl.BlockSpec(memory_space=pltpu.SMEM)
AWAY = pl.BlockSpec(memory_space=pl.ANY)


def dot(a, b, dims=NN):
    return lax.dot_general(a, b, dims, preferred_element_type=F32)


def part(value, count):
    out = []
    for _ in range(count):
        piece = value.astype(BF)
        out.append(piece)
        value = value - piece.astype(F32)
    return out


def patch_row(t):
    dr, dc = t // 3, t % 3
    return ((dr // 2) * 3 + dc) * 16 + (dr % 2) * 8


def fitted(code):
    return jnp.where(code < 256, code, code - 512).astype(F32)


def rows_kernel(_, others, tile, near):
    level = lax.axis_index("level")
    _, batches, band, _ = others.shape
    for b in range(batches):
        bottom_rows, top_rows = (pl.ds(b * band * 8 + c, band, stride=8) for c in (4, 5))
        mine, theirs = tile[bottom_rows, :], fitted(others[0, b])
        tile[bottom_rows, :] = jnp.where(level == 1, mine, theirs)
        tile[top_rows, :] = jnp.where(level == 1, theirs, mine)
    for b in range(batches):
        row = jnp.where(level == 0, band - 2, 0)
        start = pl.multiple_of((b * band + row) * 8, 8)
        near[b * 16 : (b + 1) * 16] = tile[pl.ds(start, 16), :].astype(BF)


def pack_kernel(image, mask, codes, count, total, enc, lat, dec, read, pack, tile, flat):
    batches, _, band, _ = image.shape
    for b in range(batches):
        planes = [image[b, c].astype(F32) for c in range(3)] + [mask[b].astype(F32), fitted(codes[0, b])]
        planes += [jnp.zeros((band, W), F32)] * 3
        for c, plane in enumerate(planes):
            tile[pl.ds(b * band * 8 + c, band, stride=8), :] = plane
    pack[0:TAPS] = dec[0].astype(BF)
    flat[...] = jnp.zeros_like(flat)
    for t in range(9):
        for c in range(3):
            row = patch_row(t) + c
            flat[row : row + 1] = enc[3 * t + c]
    pack[R_ET : R_ET + 128] = flat[...].T.astype(BF)
    flat[...] = jnp.zeros_like(flat)
    flat[0:64] = lat[0]
    pack[R_ZT : R_ZT + 64] = lat[0].astype(BF)
    pack[R_ZN : R_ZN + 128] = flat[...].T.astype(BF)
    blank = jnp.zeros((13, 128), F32)
    pack[R_OT : R_OT + 16] = jnp.concatenate([read[0], read[1], read[2], blank], 0).astype(BF)
    book = total[0] / count[...]
    for quarter in range(4):
        row = R_BT + (quarter % 2) * 128 + (quarter // 2) * 64
        pack[row : row + 64] = book[:, quarter * 128 : (quarter + 1) * 128].astype(BF)


def sides(v):
    lane = lax.broadcasted_iota(jnp.int32, (v.shape[0], W), 1)
    before, after = [], []
    for i in range(v.shape[1] // W):
        row = v[:, i * W : (i + 1) * W]
        before.append(jnp.where(lane == 0, 0.0, pltpu.roll(row, 1, 1)))
        after.append(jnp.where(lane == W - 1, 0.0, pltpu.roll(row, W - 1, 1)))
    if len(before) == 1:
        return before[0], v, after[0]
    return jnp.concatenate(before, 1), v, jnp.concatenate(after, 1)


def at(row, rows):
    return pl.ds(pl.multiple_of(row * W, W), rows * W)


def fold(v, width):
    return sum(v[:, i : i + width] for i in range(0, v.shape[1], width))


def silu_parts(half):
    p = jnp.tanh(half) + 1.0
    out = half * p
    return out, p + out * (2.0 - p)


def one_hots(here):
    ids = lax.broadcasted_iota(jnp.int32, (256, here.shape[1]), 0).astype(F32)
    onehots, highs = [], []
    for v in range(2):
        code = here[4 + v : 5 + v]
        high = code < 0.0
        low = jnp.where(high, code + 256.0, code)
        onehots.append(jnp.where(ids == low, 1.0, 0.0).astype(BF))
        highs.append(high)
    return onehots, highs


def quantized(onehots, highs, bt):
    quants = []
    for onehot, high, book in zip(onehots, highs, bt):
        both = dot(book, onehot)
        quants.append(jnp.where(high, both[64:128], both[0:64]))
    return jnp.concatenate(quants, 0)


def books(mine, theirs, bottom):
    a, b = (jnp.concatenate([pack[R_BT : R_BT + 128], pack[R_BT + 128 : R_BT + 256]], 1) for pack in (mine, theirs))
    return jnp.where(bottom, a, b), jnp.where(bottom, b, a)


def either(mine, theirs, bottom, start, size):
    a, b = mine[start : start + size], theirs[start : start + size]
    return jnp.where(bottom, a, b), jnp.where(bottom, b, a)


def encoder_weights(mine, theirs, bottom, et, zt):
    one, zero = either(mine, theirs, bottom, R_ET, 128)
    et[0:128] = (0.5 * one.astype(F32)).astype(BF)
    et[128:256] = (0.5 * zero.astype(F32)).astype(BF)
    one, zero = either(mine, theirs, bottom, R_ZT, 64)
    blank = jnp.zeros((64, 128), BF)
    zt[0:64] = jnp.concatenate([one, blank], 1)
    zt[64:128] = jnp.concatenate([blank, zero], 1)


def encoded(x, u, k, onehots, highs, et, zt, g_s):
    h, slope = silu_parts(dot(et[:, 0:PATCH], x))
    h = h.astype(BF)
    z = dot(zt[...], h)
    gap = z - u
    kept = k * gap
    z = k * z.astype(BF).astype(F32)
    row = lax.broadcasted_iota(jnp.int32, (16, z.shape[1]), 0)
    for v in range(2):
        part_z = z[v * 64 : v * 64 + 64]
        high = highs[v]
        low_k = jnp.where(high, 0.0, k)
        high_k = jnp.where(high, k, 0.0)
        left = jnp.concatenate(
            [
                jnp.where(high, 0.0, part_z),
                jnp.where(high, part_z, 0.0),
                jnp.where(row == 0, low_k, jnp.where(row == 1, high_k, 0.0)),
            ],
            0,
        ).astype(BF)
        g_s[v] += dot(left, onehots[v], NT)
    return h, slope, 0.5 * kept, kept * gap


def early_kernel(
    tile, mine, theirs,
    u_s, h_s, slope_s, gap_s, x_s, g_s, l_s, et, zt,
    *, batches, rows,
):
    level = lax.axis_index("level")
    bottom = level == 1
    edge = level * (rows - 1)
    bt = books(mine, theirs, bottom)
    encoder_weights(mine, theirs, bottom, et, zt)
    for ref in (g_s, l_s):
        ref[...] = jnp.zeros_like(ref)

    def batch(b, _):
        def row(i):
            return tile[pl.ds(pl.multiple_of((b * 2 * rows + i) * 8, 8), 8), :]

        run = [row(jnp.clip(level * rows + r, 0, 2 * rows - 1)) for r in range(-1, rows + 2)]
        value = jnp.concatenate([jnp.concatenate(run[i : i + 2], 0) for i in range(rows + 2)], 1)
        for dc, view in enumerate(sides(value)):
            x_s[dc, :, at(b * (rows + 2), rows + 2)] = view.astype(BF)
        own = run[1 : rows + 1]
        beyond = [row(rows - 2 * level + i) for i in range(2)]
        onehots, highs = one_hots(jnp.concatenate(own + beyond, 1))
        u = quantized(onehots, highs, bt)
        inner = slice(0, rows * W)
        for k, view in enumerate(sides(u)):
            view = view.astype(BF)
            u_s[k, :, at(b * (rows + 4) + 2, rows)] = view[:, inner]
            u_s[k, :, at(b * (rows + 4) + (rows + 2) * (1 - level), 2)] = view[:, rows * W :]
        k = jnp.concatenate([jnp.where(edge == i, 0.0, own[i][3:4]) for i in range(rows)], 1)
        h, slope, gap, error = encoded(
            patches(x_s, b * (rows + 2), rows), u[:, inner], k,
            [item[:, inner] for item in onehots], [item[:, inner] for item in highs], et, zt, g_s,
        )
        h_s[b] = h
        slope_s[b] = slope
        gap_s[b] = gap
        l_s[0:128] += fold(error, 256)
        return 0

    lax.fori_loop(0, batches, batch, 0)


def patches(x_s, row, n):
    return jnp.concatenate([x_s[dc, :, at(row + pair, n)] for pair in (0, 2) for dc in range(3)], 0)


def giver(bottom, send):
    def give(start, one, zero, keep, offset, shift=0):
        n = one.shape[0]
        keep[start - shift : start - shift + n] = jnp.where(bottom, one, zero).astype(keep.dtype)
        start = offset + start - shift
        send[start : start + n] = jnp.where(bottom, zero, one).astype(BF)

    return give


def spread_back(dn, da):
    rows = da.shape[1] // W - 2
    near = jnp.concatenate([da[:, (2 - dr) * W : (2 - dr + rows) * W] for dr in range(3)], 0)
    spread = dot(dn[...], near)
    _, _, after = sides(spread[0:128])
    before, _, _ = sides(spread[256:384])
    return after + spread[128:256] + before


def encoder_back(du, gap, h, slope, x, zn, g_z, g_e):
    dz = (du + gap).astype(BF)
    g_z[...] += dot(dz, h, NT)
    dpre = (dot(zn[...], dz) * slope).astype(BF)
    g_e[...] += dot(x, dpre, NT)


def step_kernel(
    tile, near, mine, theirs, *refs,
    batches, rows,
):
    (keep_big, keep_small, send, h_out, slope_out, gap_out, da_out, x_out, dn_out, zn_out,
     u_s, h_s, slope_s, gap_s, x_s, g_s, l_s,
     t_s, dt, et, zt, ot, on, da_s, dn, zn, g_d, g_o, sems, fixed_sems) = refs[7:]
    level, me, devices = lax.axis_index("level"), lax.axis_index("dp"), lax.axis_size("dp")
    band, ext = 2 * rows, rows + 4
    above, below = (me + 1) * band, (me + 2) * band
    top_ok = (lax.rem(above, CROP) != 0) & (me > 0)
    bottom_ok = (lax.rem(below, CROP) != 0) & (me < devices - 1)
    valid = jnp.where(level == 0, top_ok.astype(jnp.int32), bottom_ok.astype(jnp.int32))
    bottom = level == 1

    def pair(start, size):
        return either(mine, theirs, bottom, start, size)

    for t in range(9):
        one, zero = pair(t * 128, 128)
        zero = jnp.concatenate([jnp.zeros((64, 128), BF), zero[0:64]], 0)
        dr, dc = t // 3, t % 3
        dn[dc * 128 : (dc + 1) * 128, dr * 256 : dr * 256 + 128] = one
        dn[dc * 128 : (dc + 1) * 128, dr * 256 + 128 : (dr + 1) * 256] = zero
        dt[0:128, t * 128 : (t + 1) * 128] = (0.5 * one.astype(F32)).T.astype(BF)
        dt[128:256, t * 128 : (t + 1) * 128] = (0.5 * zero.astype(F32)).T.astype(BF)
    encoder_weights(mine, theirs, bottom, et, zt)
    one, zero = pair(R_ZN, 128)
    zn[0:128] = (0.5 * one.astype(F32)).astype(BF)
    zn[128:256] = pltpu.roll(0.5 * zero.astype(F32), 64, 1).astype(BF)
    one, zero = pair(R_OT, 16)
    blank = jnp.zeros((8, 128), F32)
    out_t = jnp.concatenate(
        [
            jnp.concatenate([one[0:8].astype(F32), blank], 1),
            jnp.concatenate([blank, zero[0:8].astype(F32)], 1),
        ],
        0,
    )
    ot[...] = out_t.astype(BF)
    on[...] = (0.5 * out_t).T.astype(BF)
    bt = books(mine, theirs, bottom)
    fixed = [
        pltpu.make_async_copy(a, o, fixed_sems.at[n])
        for n, (a, o) in enumerate(((x_s, x_out), (dn, dn_out), (zn, zn_out)))
    ]
    fixed[1].start()
    fixed[2].start()

    sub = lax.broadcasted_iota(jnp.int32, (8, W), 0)
    nothing = jnp.where((sub == 4) | (sub == 5), NOBODY, 0.0)

    outside = []
    for b in range(batches):
        both = near[b * 16 : (b + 1) * 16].astype(F32)
        for r in range(2):
            outside.append(jnp.where(valid > 0, both[r * 8 : (r + 1) * 8], nothing))
    for i, shown in enumerate(outside):
        t_s[i] = shown

    def row(b, r):
        return tile[pl.ds(pl.multiple_of((b * band + r) * 8, 8), 8), :]

    for ref in (g_d, g_o):
        ref[...] = jnp.zeros_like(ref)

    def spread_rows(u, b, e, n):
        for k, view in enumerate(sides(u)):
            u_s[k, :, at(b * ext + e, n)] = view.astype(BF)

    first = level * rows
    runs = []
    for b in range(batches):
        low, high = outside[2 * b], outside[2 * b + 1]
        runs.append(jnp.concatenate([jnp.where(bottom, row(b, band - 1), high), jnp.where(bottom, low, row(b, 0))], 0))
        runs.append(jnp.concatenate([jnp.where(bottom, low, row(b, 0)), jnp.where(bottom, high, row(b, 1))], 0))
    for dc, view in enumerate(sides(jnp.concatenate(runs, 1))):
        view = view.astype(BF)
        for b in range(batches):
            x_s[dc, :, at(b * (rows + 2) + first, 2)] = view[:, b * 2 * W : (b + 1) * 2 * W]
    outer, edge = jnp.where(bottom, rows + 2, 0), level * (rows - 1)
    u = quantized(*one_hots(jnp.concatenate(outside, 1)), bt)
    for b in range(batches):
        spread_rows(u[:, b * 2 * W : (b + 1) * 2 * W], b, outer, 2)
    here = jnp.concatenate([row(b, level * (band - 1)) for b in range(batches)], 1)
    u = jnp.concatenate([u_s[1, :, at(b * ext + 2 + edge, 1)] for b in range(batches)], 1).astype(F32)
    x = jnp.concatenate([patches(x_s, b * (rows + 2) + edge, 1) for b in range(batches)], 1)
    h, slope, gap, error = encoded(x, u, here[3:4], *one_hots(here), et, zt, g_s)
    l_s[0:128, 0:W] += fold(error, W)
    for b in range(batches):
        cols = slice(b * W, (b + 1) * W)
        h_s[b, :, at(edge, 1)] = h[:, cols]
        slope_s[b, :, at(edge, 1)] = slope[:, cols]
        gap_s[b, :, at(edge, 1)] = gap[:, cols]

    pairs = ((h_s, h_out), (slope_s, slope_out), (gap_s, gap_out), (da_s, da_out))

    def leave(b, which=range(4)):
        return [pltpu.make_async_copy(pairs[n][0].at[b], pairs[n][1].at[b], sems.at[n, b]) for n in which]

    fixed[0].start()
    for b in range(batches):
        for copy in leave(b, range(3)):
            copy.start()

    def decode(b, _):
        u = jnp.concatenate(
            [u_s[dc, :, at(b * ext + dr, rows + 2)] for dr in range(3) for dc in range(3)], 0
        )
        inner = slice(W, (1 + rows) * W)
        g, slope = silu_parts(dot(dt[...], u))
        g = g.astype(BF)
        y = dot(ot[...], g)
        shown = [row(b, jnp.clip(level * rows + r, 0, band - 1)) for r in range(-1, rows + 1)]
        shown[0] = jnp.where(bottom, shown[0], t_s[2 * b + 1])
        shown[-1] = jnp.where(bottom, t_s[2 * b], shown[-1])
        here = jnp.concatenate(shown, 1)
        k = here[3:4]
        x = jnp.where(lax.broadcasted_iota(jnp.int32, here.shape, 0) < 3, here, 0.0)
        diff = y - jnp.concatenate([x, x], 0)
        kept = k * diff
        dy = (2.0 * kept).astype(BF)
        da = (dot(on[...], dy) * slope).astype(BF)
        da_s[b] = da
        leave(b, [3])[0].start()
        l_s[128:144] += fold((kept * diff)[:, inner], 256)
        g_o[...] += dot(g[:, inner], dy[:, inner], NT)
        g_d[...] += dot(u[:, inner], da[:, inner], NT)
        return 0

    lax.fori_loop(0, batches, decode, 0)
    give = giver(bottom, send)
    for t in range(9):
        top = jnp.concatenate([g_d[t * 128 + 64 : (t + 1) * 128, 128:256], jnp.zeros((64, 128), F32)], 0)
        give(t * 128, g_d[t * 128 : (t + 1) * 128, 0:128], top, keep_big, 0)
    for half in range(2):
        cols = slice(half * 128, (half + 1) * 128)
        give(TAPS + half * 128, g_s[0, 0:128, cols], g_s[1, 0:128, cols], keep_big, 0)
    pad = keep_big.shape[0]
    if pad > BIG:
        keep_big[BIG:pad] = jnp.zeros((pad - BIG, W), F32)
        send[BIG:pad] = jnp.zeros((pad - BIG, W), BF)
    readouts = g_o[...].T
    blank = jnp.zeros((8, 128), F32)
    give(
        S_O,
        jnp.concatenate([readouts[0:8, 0:128], blank], 0),
        jnp.concatenate([readouts[8:16, 128:256], blank], 0),
        keep_small,
        pad,
        LATE,
    )
    valid_sum = jnp.sum(g_s[0, 128:130])
    loss = 0.25 * jnp.sum(l_s[0:128]) + jnp.sum(l_s[128:144])
    lane = lax.broadcasted_iota(jnp.int32, (1, W), 1)
    other = jnp.where(lane == 0, loss, jnp.where(lane == 1, valid_sum, 0.0))
    exact = []
    for v in range(2):
        runs = [g_s[v, 128 + hi : 129 + hi, half * 128 : (half + 1) * 128] for hi in range(2) for half in range(2)]
        pieces = part(jnp.concatenate(runs + [other], 0), 3)
        exact.append(jnp.concatenate([p.astype(F32) for p in pieces] + [jnp.zeros((1, 128), F32)], 0))
    give(S_X, exact[0], exact[1], keep_small, pad, LATE)
    for copy in fixed + [copy for b in range(batches) for copy in leave(b)]:
        copy.wait()


def back_kernel(
    h_in, slope_in, gap_in, da_in, x_in, dn_in, zn_in, _,
    keep, send, h_s, slope_s, gap_s, da_s, x_s, dn, zn, g_e, g_z, sems, fixed_sems,
    *, batches, rows,
):
    bottom = lax.axis_index("level") == 1
    pairs = ((h_in, h_s), (slope_in, slope_s), (gap_in, gap_s), (da_in, da_s))

    def fetch(b):
        return [pltpu.make_async_copy(a.at[b], o.at[b], sems.at[n, b]) for n, (a, o) in enumerate(pairs)]

    fixed = [
        pltpu.make_async_copy(a, o, fixed_sems.at[n])
        for n, (a, o) in enumerate(((dn_in, dn), (zn_in, zn), (x_in, x_s)))
    ]
    count = h_s.shape[0]
    copies = [fetch(b) for b in range(count)]
    for copy in [fixed[0], copies[0][3], copies[0][2], fixed[1], *copies[0][:2], fixed[2]]:
        copy.start()
    g_e[...] = jnp.zeros_like(g_e)
    g_z[...] = jnp.zeros_like(g_z)
    fixed[0].wait()
    copies[0][3].wait()
    for b in range(1, count):
        for n in (3, 2, 0, 1):
            copies[b][n].start()
    du = spread_back(dn, da_s[0])
    for copy in [fixed[1], fixed[2]]:
        copy.wait()
    for b in range(count):
        for copy in copies[b][:3]:
            copy.wait()
        if b + 1 < count:
            copies[b + 1][3].wait()
        row = b * (rows + 2)
        encoder_back(du, gap_s[b], h_s[b], slope_s[b], patches(x_s, row, rows), zn, g_z, g_e)
        if b + 1 < count:
            du = spread_back(dn, da_s[b + 1])
    give = giver(bottom, send)
    give(S_Z, g_z[0:64, 0:128], g_z[64:128, 128:256], keep, 0)
    enc = []
    for cols in (slice(0, 128), slice(128, 256)):
        runs = [g_e[patch_row(t) : patch_row(t) + 3, cols] for t in range(9)]
        enc.append(jnp.concatenate(runs + [jnp.zeros((5, 128), F32)], 0))
    give(S_E, enc[0], enc[1], keep, 0)


def exact_sum(total, first):
    value = sum(total[first + EXACT * i : first + EXACT * (i + 1)] for i in range(3))
    pieces = [piece.astype(F32) for piece in part(value, 3)]
    return jnp.concatenate([total[:first], *pieces, total[first + 3 * EXACT :]], 0).astype(BF)


def merge_kernel(keep, early, got, big, early_out):
    size = keep.shape[0]
    big[...] = (keep[...] + got[0:size].astype(F32)).astype(BF)
    total = early[...].astype(F32) + got[size : size + SMALL - LATE].astype(F32)
    early_out[...] = exact_sum(total, S_X - LATE)


def sum_kernel(parts, out):
    total = parts[0].astype(F32)
    for i in range(1, parts.shape[0]):
        total = total + parts[i].astype(F32)
    out[...] = total.astype(BF)


def update_kernel(
    *refs, stages, start, other
):
    (parts, refs) = refs[:stages], refs[stages:]
    (count, total, ew, e1, e2, zw, z1, z2, dw, d1, d2, ow, o1, o2,
     loss_out, valid_out, count_out, total_out,
     em, es, ep, ec, zm, zs, zp, zc, dm, ds, dp, dc, om, os, op, oc, big, rows) = refs
    share = big.shape[0] // stages
    top = lax.axis_index("level") == 0
    index = (lax.axis_index("dp") >> jnp.where(top, start, other)) & (stages - 1)
    size = big.shape[0] // lax.axis_size("dp")
    small = jnp.zeros((SMALL, W), F32)
    for n, ref in enumerate(parts):
        value = ref[0:share].astype(F32)
        for h in range(share // size):
            place = h * stages + (index ^ n)
            if other != start:
                place = jnp.where(top, place, (index ^ n) * (share // size) + h)
            row = pl.multiple_of(place * size, 8)
            big[pl.ds(row, size), :] = value[h * size : (h + 1) * size]
        small = small + ref[share : share + SMALL].astype(F32)
    exact = sum(small[S_X + EXACT * i : S_X + EXACT * (i + 1)] for i in range(3))
    loss = jnp.sum(exact[4:5, 0:1])
    valid = jnp.sum(exact[4:5, 1:2])
    loss_out[0, 0] = loss
    valid_out[0, 0] = valid
    counts = jnp.concatenate([exact[i : i + 1] for i in range(4)], 1)
    count_out[...] = 0.99 * count[...] + 0.01 * counts
    for quarter in range(4):
        row = TAPS + (quarter % 2) * 128 + (quarter // 2) * 64
        cols = slice(quarter * 128, (quarter + 1) * 128)
        total_out[0, :, cols] = 0.99 * total[0, :, cols] + 0.01 * big[row : row + 64]

    scale = 1.0 - 0.5**STEP

    def adamw(grad, weight, first, second, rate):
        grad = grad / valid
        moment = 0.5 * first + 0.5 * grad
        square = 0.5 * second + 0.5 * grad * grad
        master = weight - rate * (moment / scale / (jnp.sqrt(square / scale) + 1e-08) + 0.01 * weight)
        return moment, square, master

    def whole(grad, w, first, second, rate, outs):
        outs[0][0], outs[1][0], master = adamw(grad, w[0], first[0], second[0], rate)
        outs[2][0] = master
        outs[3][0] = master.astype(BF)

    def by_row(grad, w, first, second, rate, outs):
        n = w.shape[0]
        for i in range(n):
            outs[0][i], outs[1][i], master = adamw(grad[i : i + 1], w[i], first[i], second[i], rate)
            outs[2][i] = master
            rows[i : i + 1] = master
        outs[3][0] = rows[0:n].astype(BF)

    by_row(small[S_E : S_E + 27], ew, e1, e2, RATES[0], (em, es, ep, ec))
    whole(small[S_Z : S_Z + 64], zw, z1, z2, RATES[1], (zm, zs, zp, zc))
    whole(big[0:TAPS], dw, d1, d2, RATES[2], (dm, ds, dp, dc))
    by_row(small[S_O : S_O + 3], ow, o1, o2, RATES[3], (om, os, op, oc))


def radices(devices):
    bits = devices.bit_length() - 1
    return [(start, min(2, bits - start)) for start in range(0, bits, 2)]


def partners(start, width):
    return [k << start for k in range(1, 1 << width)]


def xor_pairs(devices, by, other):
    return [(i, i ^ by) for i in range(devices)] + [(devices + i, devices + (i ^ other)) for i in range(devices)]


def lowered(value):
    return lax.reduce_precision(value, 8, 7)


def sum_small(parts, first):
    total = sum(item.astype(F32) for item in parts)
    value = sum(total[first + EXACT * i : first + EXACT * (i + 1)] for i in range(3))
    high = lowered(value)
    middle = lowered(value - high)
    low = value - high - middle
    rest = total[first + 3 * EXACT :]
    return jnp.concatenate([total[:first], high, middle, low, rest], 0).astype(BF)


def local(
    image, mask, codes, ema_count, ema_sum,
    encoder_weight, encoder_first, encoder_second,
    latent_weight, latent_first, latent_second,
    decoder_weight, decoder_first, decoder_second,
    readout_weight, readout_first, readout_second,
):
    batches, _, band, width = image.shape
    rows = band // 2
    me, devices = lax.axis_index("dp"), lax.axis_size("dp")
    ema_sum = jnp.swapaxes(ema_sum, 1, 2)
    encoder_weight, encoder_first, encoder_second = (
        jnp.swapaxes(item, 0, 1) for item in (encoder_weight, encoder_first, encoder_second)
    )
    latent_weight, latent_first, latent_second = (
        jnp.swapaxes(item, 1, 2) for item in (latent_weight, latent_first, latent_second)
    )
    readout_weight, readout_first, readout_second = (
        jnp.transpose(item, (2, 0, 1)) for item in (readout_weight, readout_first, readout_second)
    )

    def limit(mib):
        return pltpu.CompilerParams(vmem_limit_bytes=mib * 1024 * 1024)

    def outside(*items):
        return [pltpu.with_memory_space_constraint(item, pltpu.HBM) for item in items]

    def inside_vmem(item):
        return pltpu.with_memory_space_constraint(item, pltpu.VMEM)

    swap = [(0, 1), (1, 0)]
    others = lax.ppermute(codes, "level", swap)
    tiled = pltpu.VMEM((batches * band * 8, W), F32)
    pack, tile = pl.pallas_call(
        pack_kernel,
        out_shape=[pltpu.VMEM((PACKED, W), BF), tiled],
        in_specs=[VMEM] * 9,
        out_specs=[VMEM] * 2,
        scratch_shapes=[pltpu.VMEM((128, 128), F32)],
        compiler_params=limit(56),
    )(
        *outside(
            image, mask, codes, ema_count, ema_sum, encoder_weight, latent_weight, decoder_weight, readout_weight
        )
    )
    others, pack, tile = lax.optimization_barrier((others, pack, tile))
    tile, near = pl.pallas_call(
        rows_kernel,
        out_shape=[tiled, pltpu.VMEM((batches * 16, W), BF)],
        in_specs=[VMEM] * 2,
        out_specs=[VMEM] * 2,
        input_output_aliases={0: 0},
        compiler_params=limit(32),
    )(inside_vmem(tile), inside_vmem(others))

    both = ("level", "dp")
    inside = [d for d in range(1, devices) if (d + 1) * band % CROP != 0]
    pairs = [(d - 1, d) for d in inside] + [(devices + d, devices + d - 1) for d in inside]
    near = lax.ppermute(near, both, pairs)
    theirs = lax.ppermute(pack, "level", swap)

    ext = rows + 4
    ext = rows + 4
    pixels = batches * rows * W
    framed = batches * (rows + 2) * W
    held = [
        ((batches, 256, rows * W), BF),
        ((batches, 256, rows * W), F32),
        ((batches, 128, rows * W), F32),
        ((batches, 256, (rows + 2) * W), BF),
    ]
    fixed = [((3, 16, framed), BF), ((384, 768), BF), ((256, 128), BF)]
    size = -(-BIG // (8 * devices)) * 8
    padded = size * devices
    shape = jax.ShapeDtypeStruct
    staged = [
        pltpu.VMEM((3, 128, batches * ext * W), BF),
        *[pltpu.VMEM(*item) for item in held[:3]],
        pltpu.VMEM(*fixed[0]),
        pltpu.VMEM((2, 144, 256), F32),
        pltpu.VMEM((144, 256), F32),
    ]
    stages_early = pl.pallas_call(
        functools.partial(early_kernel, batches=batches, rows=rows),
        out_shape=staged,
        in_specs=[VMEM] * 3,
        out_specs=[VMEM] * 7,
        scratch_shapes=[pltpu.VMEM((256, 128), BF), pltpu.VMEM((128, 256), BF)],
        compiler_params=limit(EARLY_MIB),
        cost_estimate=pl.CostEstimate(flops=3 << 30, bytes_accessed=1 << 20, transcendentals=0),
    )(*[inside_vmem(item) for item in (tile, pack, theirs)])
    results = pl.pallas_call(
        functools.partial(step_kernel, batches=batches, rows=rows),
        out_shape=[
            pltpu.VMEM((padded, W), F32),
            pltpu.VMEM((SMALL - LATE, W), BF),
            pltpu.VMEM((padded + SMALL - LATE, W), BF),
            *[shape(*item) for item in held + fixed],
            *staged,
        ],
        in_specs=[VMEM] * 11,
        out_specs=[VMEM] * 3 + [AWAY] * 7 + [VMEM] * 7,
        input_output_aliases={4 + i: 10 + i for i in range(7)},
        scratch_shapes=[
            pltpu.VMEM((2 * batches, 8, W), F32),
            pltpu.VMEM((256, TAPS), BF),
            pltpu.VMEM((256, 128), BF),
            pltpu.VMEM((128, 256), BF),
            pltpu.VMEM((16, 256), BF),
            pltpu.VMEM((256, 16), BF),
            pltpu.VMEM(*held[3]),
            *[pltpu.VMEM(*item) for item in fixed[1:]],
            pltpu.VMEM((TAPS, 256), F32),
            pltpu.VMEM((256, 16), F32),
            pltpu.SemaphoreType.DMA((4, batches)),
            pltpu.SemaphoreType.DMA((3,)),
        ],
        compiler_params=limit(STEP_MIB),
    )(*[inside_vmem(item) for item in (tile, near, pack, theirs, *stages_early)])
    keep, early, send = results[:3]
    kept = results[3:10]

    got = lax.ppermute(send, "level", swap)
    big, early = pl.pallas_call(
        merge_kernel,
        out_shape=[pltpu.VMEM((padded, W), BF), pltpu.VMEM((SMALL - LATE, W), BF)],
        in_specs=[VMEM] * 3,
        out_specs=[VMEM] * 2,
        compiler_params=limit(32),
    )(*[inside_vmem(item) for item in (keep, early, got)])
    big = lax.all_to_all(big.reshape(devices, size, W), "dp", 0, 0)

    late, send = pl.pallas_call(
        functools.partial(back_kernel, batches=batches, rows=rows),
        out_shape=[pltpu.VMEM((LATE, W), BF), pltpu.VMEM((LATE, W), BF)],
        in_specs=[AWAY] * 8,
        out_specs=[VMEM] * 2,
        scratch_shapes=[
            *[pltpu.VMEM(*item) for item in held + fixed],
            pltpu.VMEM((PATCH, 256), F32),
            pltpu.VMEM((128, 256), F32),
            pltpu.SemaphoreType.DMA((4, batches)),
            pltpu.SemaphoreType.DMA((3,)),
        ],
        compiler_params=limit(BACK_MIB),
        cost_estimate=pl.CostEstimate(flops=2 * pixels * 98304 * 4, bytes_accessed=1 << 20, transcendentals=0),
    )(*outside(*kept), got)
    got = lax.ppermute(send, "level", swap)
    late = (late.astype(F32) + got.astype(F32)).astype(BF)
    small = jnp.concatenate([late, early], 0)

    big = pl.pallas_call(
        sum_kernel,
        out_shape=pltpu.VMEM((size, W), BF),
        in_specs=[VMEM],
        out_specs=VMEM,
        compiler_params=limit(32),
        cost_estimate=pl.CostEstimate(flops=1 << 34, bytes_accessed=1 << 20, transcendentals=0),
    )(inside_vmem(big))[None]
    stages = radices(devices)
    crossed = len(stages) == 2 and stages[0][1] == stages[1][1]
    for number, (start, width_bits) in enumerate(reversed(stages)):
        count = 1 << width_bits
        other = stages[number][0] if crossed else start
        index = (me >> jnp.where(lax.axis_index("level") == 0, start, other)) & (count - 1)
        payload = jnp.concatenate([big.reshape(-1, W), small], 0)
        parts = [payload] + [
            lax.ppermute(payload, both, xor_pairs(devices, k << start, k << other)) for k in range(1, count)
        ]
        if number == len(stages) - 1:
            break
        high = big.shape[0]
        stacked = jnp.zeros((high, count, size, W), BF)
        far_first = [0, *range(count - 1, 0, -1)]
        for k in far_first:
            piece = parts[k][: high * size].reshape(high, size, W)
            stacked = lax.dynamic_update_index_in_dim(stacked, piece, index ^ k, 1)
        small = sum_small([parts[k][high * size :] for k in far_first], S_X)
        big = stacked.reshape(high * count, size, W)

    state = (
        ema_count, ema_sum,
        encoder_weight, encoder_first, encoder_second, latent_weight, latent_first, latent_second,
        decoder_weight, decoder_first, decoder_second, readout_weight, readout_first, readout_second,
    )
    outs = [jax.ShapeDtypeStruct((1, 1), F32)] * 2
    outs += [jax.ShapeDtypeStruct(ema_count.shape, F32), jax.ShapeDtypeStruct(ema_sum.shape, F32)]
    for item in (encoder_weight, latent_weight, decoder_weight, readout_weight):
        copy = item.shape if item.shape[0] == 1 else (1, item.shape[0], item.shape[2])
        outs += [jax.ShapeDtypeStruct(item.shape, F32)] * 3 + [jax.ShapeDtypeStruct(copy, BF)]
    result = pl.pallas_call(
        functools.partial(update_kernel, stages=len(parts), start=start, other=other),
        out_shape=outs,
        in_specs=[VMEM] * (len(parts) + len(state)),
        out_specs=[SMEM] * 2 + [VMEM] * (len(outs) - 2),
        scratch_shapes=[pltpu.VMEM((padded, W), F32), pltpu.VMEM((32, W), F32)],
        compiler_params=limit(16),
    )(*parts, *state)
    loss, valid, count_new, total_new = result[:4]
    enc, lat, dec, read = (list(result[4 * n : 4 * n + 4]) for n in range(1, 5))
    enc[:3] = [jnp.swapaxes(item, 0, 1) for item in enc[:3]]
    lat = [jnp.swapaxes(item, 1, 2) for item in lat]
    read = [jnp.transpose(item, (1, 2, 0)) for item in read[:3]] + [jnp.swapaxes(read[3], 1, 2)]
    return (loss.reshape(()), valid.reshape(()), count_new, jnp.swapaxes(total_new, 1, 2), *enc, *lat, *dec, *read)


def solution(mesh):
    rank = (0, 0, 2, 3) + (3,) * 16
    in_specs = (P(None, None, "dp", None), P(None, "dp", None), P("level", None, "dp", None), P("level", None))
    in_specs += (P("level", None, None),) * 13
    out_specs = tuple(P(*(("level",) + (None,) * (n - 1) if n else ())) for n in rank)
    return jax.shard_map(local, mesh=mesh, in_specs=in_specs, out_specs=out_specs, check_vma=False)
```

```python
import functools

import jax
import jax.numpy as jnp
from jax import lax
from jax.experimental import pallas as pl
from jax.experimental.pallas import tpu as pltpu
from jax.sharding import PartitionSpec as P

CROP = 128
STEP = 5
RATES = (0.05, 0.03, 0.01, 0.03)

F32 = jnp.float32
BF = jnp.bfloat16
W = 128
EARLY_MIB, STEP_MIB, BACK_MIB = 36, 36, 56
NOBODY = 300.0

TAPS = 9 * 128
R_ET = TAPS
R_ZN = R_ET + 128
R_ZT = R_ZN + 128
R_OT = R_ZT + 64
R_BT = R_OT + 16
PACKED = R_BT + 256
BIG = TAPS + 256
S_Z, S_E, S_O, S_X = 0, 64, 96, 112
LATE, SMALL = 96, 128
EXACT = 5
PATCH = 96

NN = (((1,), (0,)), ((), ()))
NT = (((1,), (1,)), ((), ()))
VMEM = pl.BlockSpec(memory_space=pltpu.VMEM)
SMEM = pl.BlockSpec(memory_space=pltpu.SMEM)
AWAY = pl.BlockSpec(memory_space=pl.ANY)


def dot(a, b, dims=NN):
    return lax.dot_general(a, b, dims, preferred_element_type=F32)


def part(value, count):
    out = []
    for _ in range(count):
        piece = value.astype(BF)
        out.append(piece)
        value = value - piece.astype(F32)
    return out


def patch_row(t):
    dr, dc = t // 3, t % 3
    return ((dr // 2) * 3 + dc) * 16 + (dr % 2) * 8


def fitted(code):
    return jnp.where(code < 256, code, code - 512).astype(F32)


def rows_kernel(_, others, tile, near):
    level = lax.axis_index("level")
    _, batches, band, _ = others.shape
    for b in range(batches):
        bottom_rows, top_rows = (pl.ds(b * band * 8 + c, band, stride=8) for c in (4, 5))
        mine, theirs = tile[bottom_rows, :], fitted(others[0, b])
        tile[bottom_rows, :] = jnp.where(level == 1, mine, theirs)
        tile[top_rows, :] = jnp.where(level == 1, theirs, mine)
    for b in range(batches):
        row = jnp.where(level == 0, band - 2, 0)
        start = pl.multiple_of((b * band + row) * 8, 8)
        near[b * 16 : (b + 1) * 16] = tile[pl.ds(start, 16), :].astype(BF)


def pack_kernel(image, mask, codes, count, total, enc, lat, dec, read, pack, tile, flat):
    batches, _, band, _ = image.shape
    for b in range(batches):
        planes = [image[b, c].astype(F32) for c in range(3)] + [mask[b].astype(F32), fitted(codes[0, b])]
        planes += [jnp.zeros((band, W), F32)] * 3
        for c, plane in enumerate(planes):
            tile[pl.ds(b * band * 8 + c, band, stride=8), :] = plane
    pack[0:TAPS] = dec[0].astype(BF)
    flat[...] = jnp.zeros_like(flat)
    for t in range(9):
        for c in range(3):
            row = patch_row(t) + c
            flat[row : row + 1] = enc[3 * t + c]
    pack[R_ET : R_ET + 128] = flat[...].T.astype(BF)
    flat[...] = jnp.zeros_like(flat)
    flat[0:64] = lat[0]
    pack[R_ZT : R_ZT + 64] = lat[0].astype(BF)
    pack[R_ZN : R_ZN + 128] = flat[...].T.astype(BF)
    blank = jnp.zeros((13, 128), F32)
    pack[R_OT : R_OT + 16] = jnp.concatenate([read[0], read[1], read[2], blank], 0).astype(BF)
    book = total[0] / count[...]
    for quarter in range(4):
        row = R_BT + (quarter % 2) * 128 + (quarter // 2) * 64
        pack[row : row + 64] = book[:, quarter * 128 : (quarter + 1) * 128].astype(BF)


def sides(v):
    lane = lax.broadcasted_iota(jnp.int32, (v.shape[0], W), 1)
    before, after = [], []
    for i in range(v.shape[1] // W):
        row = v[:, i * W : (i + 1) * W]
        before.append(jnp.where(lane == 0, 0.0, pltpu.roll(row, 1, 1)))
        after.append(jnp.where(lane == W - 1, 0.0, pltpu.roll(row, W - 1, 1)))
    if len(before) == 1:
        return before[0], v, after[0]
    return jnp.concatenate(before, 1), v, jnp.concatenate(after, 1)


def at(row, rows):
    return pl.ds(pl.multiple_of(row * W, W), rows * W)


def fold(v, width):
    return sum(v[:, i : i + width] for i in range(0, v.shape[1], width))


def silu_parts(half):
    p = jnp.tanh(half) + 1.0
    out = half * p
    return out, p + out * (2.0 - p)


def one_hots(here):
    ids = lax.broadcasted_iota(jnp.int32, (256, here.shape[1]), 0).astype(F32)
    onehots, highs = [], []
    for v in range(2):
        code = here[4 + v : 5 + v]
        high = code < 0.0
        low = jnp.where(high, code + 256.0, code)
        onehots.append(jnp.where(ids == low, 1.0, 0.0).astype(BF))
        highs.append(high)
    return onehots, highs


def quantized(onehots, highs, bt):
    quants = []
    for onehot, high, book in zip(onehots, highs, bt):
        both = dot(book, onehot)
        quants.append(jnp.where(high, both[64:128], both[0:64]))
    return jnp.concatenate(quants, 0)


def books(mine, theirs, bottom):
    a, b = (jnp.concatenate([pack[R_BT : R_BT + 128], pack[R_BT + 128 : R_BT + 256]], 1) for pack in (mine, theirs))
    return jnp.where(bottom, a, b), jnp.where(bottom, b, a)


def either(mine, theirs, bottom, start, size):
    a, b = mine[start : start + size], theirs[start : start + size]
    return jnp.where(bottom, a, b), jnp.where(bottom, b, a)


def encoder_weights(mine, theirs, bottom, et, zt):
    one, zero = either(mine, theirs, bottom, R_ET, 128)
    et[0:128] = (0.5 * one.astype(F32)).astype(BF)
    et[128:256] = (0.5 * zero.astype(F32)).astype(BF)
    one, zero = either(mine, theirs, bottom, R_ZT, 64)
    blank = jnp.zeros((64, 128), BF)
    zt[0:64] = jnp.concatenate([one, blank], 1)
    zt[64:128] = jnp.concatenate([blank, zero], 1)


def encoded(x, u, k, onehots, highs, et, zt, g_s):
    h, slope = silu_parts(dot(et[:, 0:PATCH], x))
    h = h.astype(BF)
    z = dot(zt[...], h)
    gap = z - u
    kept = k * gap
    z = k * z.astype(BF).astype(F32)
    row = lax.broadcasted_iota(jnp.int32, (16, z.shape[1]), 0)
    for v in range(2):
        part_z = z[v * 64 : v * 64 + 64]
        high = highs[v]
        low_k = jnp.where(high, 0.0, k)
        high_k = jnp.where(high, k, 0.0)
        left = jnp.concatenate(
            [
                jnp.where(high, 0.0, part_z),
                jnp.where(high, part_z, 0.0),
                jnp.where(row == 0, low_k, jnp.where(row == 1, high_k, 0.0)),
            ],
            0,
        ).astype(BF)
        g_s[v] += dot(left, onehots[v], NT)
    return h, slope, 0.5 * kept, kept * gap


def early_kernel(
    tile, mine, theirs,
    u_s, h_s, slope_s, gap_s, x_s, g_s, l_s, et, zt,
    *, batches, rows,
):
    level = lax.axis_index("level")
    bottom = level == 1
    edge = level * (rows - 1)
    bt = books(mine, theirs, bottom)
    encoder_weights(mine, theirs, bottom, et, zt)
    for ref in (g_s, l_s):
        ref[...] = jnp.zeros_like(ref)

    def batch(b, _):
        def row(i):
            return tile[pl.ds(pl.multiple_of((b * 2 * rows + i) * 8, 8), 8), :]

        run = [row(jnp.clip(level * rows + r, 0, 2 * rows - 1)) for r in range(-1, rows + 2)]
        value = jnp.concatenate([jnp.concatenate(run[i : i + 2], 0) for i in range(rows + 2)], 1)
        for dc, view in enumerate(sides(value)):
            x_s[dc, :, at(b * (rows + 2), rows + 2)] = view.astype(BF)
        own = run[1 : rows + 1]
        beyond = [row(rows - 2 * level + i) for i in range(2)]
        onehots, highs = one_hots(jnp.concatenate(own + beyond, 1))
        u = quantized(onehots, highs, bt)
        inner = slice(0, rows * W)
        for k, view in enumerate(sides(u)):
            view = view.astype(BF)
            u_s[k, :, at(b * (rows + 4) + 2, rows)] = view[:, inner]
            u_s[k, :, at(b * (rows + 4) + (rows + 2) * (1 - level), 2)] = view[:, rows * W :]
        k = jnp.concatenate([jnp.where(edge == i, 0.0, own[i][3:4]) for i in range(rows)], 1)
        h, slope, gap, error = encoded(
            patches(x_s, b * (rows + 2), rows), u[:, inner], k,
            [item[:, inner] for item in onehots], [item[:, inner] for item in highs], et, zt, g_s,
        )
        h_s[b] = h
        slope_s[b] = slope.astype(BF)
        gap_s[b] = gap
        l_s[0:128] += fold(error, 256)
        return 0

    lax.fori_loop(0, batches, batch, 0, unroll=True)


def patches(x_s, row, n):
    return jnp.concatenate([x_s[dc, :, at(row + pair, n)] for pair in (0, 2) for dc in range(3)], 0)


def giver(bottom, send):
    def give(start, one, zero, keep, offset, shift=0):
        n = one.shape[0]
        keep[start - shift : start - shift + n] = jnp.where(bottom, one, zero).astype(keep.dtype)
        start = offset + start - shift
        send[start : start + n] = jnp.where(bottom, zero, one).astype(BF)

    return give


def spread_back(dn, da):
    rows = da.shape[1] // W - 2
    near = jnp.concatenate([da[:, (2 - dr) * W : (2 - dr + rows) * W] for dr in range(3)], 0)
    spread = dot(dn[...], near)
    _, _, after = sides(spread[0:128])
    before, _, _ = sides(spread[256:384])
    return after + spread[128:256] + before


def encoder_back(du, gap, h, slope, x, zn, g_z, g_e):
    dz = (du + gap).astype(BF)
    g_z[...] += dot(dz, h, NT)
    dpre = (dot(zn[...], dz) * slope).astype(BF)
    g_e[...] += dot(x, dpre, NT)


def step_kernel(
    tile, near, mine, theirs, *refs,
    batches, rows,
):
    (keep_big, keep_small, send, h_out, slope_out, gap_out, da_out, x_out, dn_out, zn_out,
     u_s, h_s, slope_s, gap_s, x_s, g_s, l_s,
     t_s, dt, et, zt, ot, on, da_s, dn, zn, g_d, g_o, sems, fixed_sems) = refs[7:]
    level, me, devices = lax.axis_index("level"), lax.axis_index("dp"), lax.axis_size("dp")
    band, ext = 2 * rows, rows + 4
    above, below = (me + 1) * band, (me + 2) * band
    top_ok = (lax.rem(above, CROP) != 0) & (me > 0)
    bottom_ok = (lax.rem(below, CROP) != 0) & (me < devices - 1)
    valid = jnp.where(level == 0, top_ok.astype(jnp.int32), bottom_ok.astype(jnp.int32))
    bottom = level == 1

    def pair(start, size):
        return either(mine, theirs, bottom, start, size)

    for t in range(9):
        one, zero = pair(t * 128, 128)
        zero = jnp.concatenate([jnp.zeros((64, 128), BF), zero[0:64]], 0)
        dr, dc = t // 3, t % 3
        dn[dc * 128 : (dc + 1) * 128, dr * 256 : dr * 256 + 128] = one
        dn[dc * 128 : (dc + 1) * 128, dr * 256 + 128 : (dr + 1) * 256] = zero
        dt[0:128, t * 128 : (t + 1) * 128] = (0.5 * one.astype(F32)).T.astype(BF)
        dt[128:256, t * 128 : (t + 1) * 128] = (0.5 * zero.astype(F32)).T.astype(BF)
    encoder_weights(mine, theirs, bottom, et, zt)
    one, zero = pair(R_ZN, 128)
    zn[0:128] = (0.5 * one.astype(F32)).astype(BF)
    zn[128:256] = pltpu.roll(0.5 * zero.astype(F32), 64, 1).astype(BF)
    one, zero = pair(R_OT, 16)
    blank = jnp.zeros((8, 128), F32)
    out_t = jnp.concatenate(
        [
            jnp.concatenate([one[0:8].astype(F32), blank], 1),
            jnp.concatenate([blank, zero[0:8].astype(F32)], 1),
        ],
        0,
    )
    ot[...] = out_t.astype(BF)
    on[...] = (0.5 * out_t).T.astype(BF)
    bt = books(mine, theirs, bottom)
    fixed = [
        pltpu.make_async_copy(a, o, fixed_sems.at[n])
        for n, (a, o) in enumerate(((x_s, x_out), (dn, dn_out), (zn, zn_out)))
    ]
    fixed[1].start()
    fixed[2].start()

    sub = lax.broadcasted_iota(jnp.int32, (8, W), 0)
    nothing = jnp.where((sub == 4) | (sub == 5), NOBODY, 0.0)

    outside = []
    for b in range(batches):
        both = near[b * 16 : (b + 1) * 16].astype(F32)
        for r in range(2):
            outside.append(jnp.where(valid > 0, both[r * 8 : (r + 1) * 8], nothing))
    for i, shown in enumerate(outside):
        t_s[i] = shown

    def row(b, r):
        return tile[pl.ds(pl.multiple_of((b * band + r) * 8, 8), 8), :]

    for ref in (g_d, g_o):
        ref[...] = jnp.zeros_like(ref)

    def spread_rows(u, b, e, n):
        for k, view in enumerate(sides(u)):
            u_s[k, :, at(b * ext + e, n)] = view.astype(BF)

    first = level * rows
    runs = []
    for b in range(batches):
        low, high = outside[2 * b], outside[2 * b + 1]
        runs.append(jnp.concatenate([jnp.where(bottom, row(b, band - 1), high), jnp.where(bottom, low, row(b, 0))], 0))
        runs.append(jnp.concatenate([jnp.where(bottom, low, row(b, 0)), jnp.where(bottom, high, row(b, 1))], 0))
    for dc, view in enumerate(sides(jnp.concatenate(runs, 1))):
        view = view.astype(BF)
        for b in range(batches):
            x_s[dc, :, at(b * (rows + 2) + first, 2)] = view[:, b * 2 * W : (b + 1) * 2 * W]
    outer, edge = jnp.where(bottom, rows + 2, 0), level * (rows - 1)
    u = quantized(*one_hots(jnp.concatenate(outside, 1)), bt)
    for b in range(batches):
        spread_rows(u[:, b * 2 * W : (b + 1) * 2 * W], b, outer, 2)
    here = jnp.concatenate([row(b, level * (band - 1)) for b in range(batches)], 1)
    u = jnp.concatenate([u_s[1, :, at(b * ext + 2 + edge, 1)] for b in range(batches)], 1).astype(F32)
    x = jnp.concatenate([patches(x_s, b * (rows + 2) + edge, 1) for b in range(batches)], 1)
    h, slope, gap, error = encoded(x, u, here[3:4], *one_hots(here), et, zt, g_s)
    l_s[0:128, 0:W] += fold(error, W)
    for b in range(batches):
        cols = slice(b * W, (b + 1) * W)
        h_s[b, :, at(edge, 1)] = h[:, cols]
        slope_s[b, :, at(edge, 1)] = slope[:, cols].astype(BF)
        gap_s[b, :, at(edge, 1)] = gap[:, cols]

    pairs = ((h_s, h_out), (slope_s, slope_out), (gap_s, gap_out), (da_s, da_out))

    def leave(b, which=range(4)):
        return [pltpu.make_async_copy(pairs[n][0].at[b], pairs[n][1].at[b], sems.at[n, b]) for n in which]

    fixed[0].start()
    for b in range(batches):
        for copy in leave(b, range(3)):
            copy.start()

    def decode(b, _):
        u = jnp.concatenate(
            [u_s[dc, :, at(b * ext + dr, rows + 2)] for dr in range(3) for dc in range(3)], 0
        )
        inner = slice(W, (1 + rows) * W)
        g, slope = silu_parts(dot(dt[...], u))
        g = g.astype(BF)
        y = dot(ot[...], g)
        shown = [row(b, jnp.clip(level * rows + r, 0, band - 1)) for r in range(-1, rows + 1)]
        shown[0] = jnp.where(bottom, shown[0], t_s[2 * b + 1])
        shown[-1] = jnp.where(bottom, t_s[2 * b], shown[-1])
        here = jnp.concatenate(shown, 1)
        k = here[3:4]
        x = jnp.where(lax.broadcasted_iota(jnp.int32, here.shape, 0) < 3, here, 0.0)
        diff = y - jnp.concatenate([x, x], 0)
        kept = k * diff
        dy = (2.0 * kept).astype(BF)
        da = (dot(on[...], dy) * slope).astype(BF)
        da_s[b] = da
        leave(b, [3])[0].start()
        l_s[128:144] += fold((kept * diff)[:, inner], 256)
        g_o[...] += dot(g[:, inner], dy[:, inner], NT)
        g_d[...] += dot(u[:, inner], da[:, inner], NT)
        return 0

    lax.fori_loop(0, batches, decode, 0)
    give = giver(bottom, send)
    for t in range(9):
        top = jnp.concatenate([g_d[t * 128 + 64 : (t + 1) * 128, 128:256], jnp.zeros((64, 128), F32)], 0)
        give(t * 128, g_d[t * 128 : (t + 1) * 128, 0:128], top, keep_big, 0)
    for half in range(2):
        cols = slice(half * 128, (half + 1) * 128)
        give(TAPS + half * 128, g_s[0, 0:128, cols], g_s[1, 0:128, cols], keep_big, 0)
    pad = keep_big.shape[0]
    if pad > BIG:
        keep_big[BIG:pad] = jnp.zeros((pad - BIG, W), F32)
        send[BIG:pad] = jnp.zeros((pad - BIG, W), BF)
    readouts = g_o[...].T
    blank = jnp.zeros((8, 128), F32)
    give(
        S_O,
        jnp.concatenate([readouts[0:8, 0:128], blank], 0),
        jnp.concatenate([readouts[8:16, 128:256], blank], 0),
        keep_small,
        pad,
        LATE,
    )
    valid_sum = jnp.sum(g_s[0, 128:130])
    loss = 0.25 * jnp.sum(l_s[0:128]) + jnp.sum(l_s[128:144])
    lane = lax.broadcasted_iota(jnp.int32, (1, W), 1)
    other = jnp.where(lane == 0, loss, jnp.where(lane == 1, valid_sum, 0.0))
    exact = []
    for v in range(2):
        runs = [g_s[v, 128 + hi : 129 + hi, half * 128 : (half + 1) * 128] for hi in range(2) for half in range(2)]
        pieces = part(jnp.concatenate(runs + [other], 0), 3)
        exact.append(jnp.concatenate([p.astype(F32) for p in pieces] + [jnp.zeros((1, 128), F32)], 0))
    give(S_X, exact[0], exact[1], keep_small, pad, LATE)
    for copy in fixed + [copy for b in range(batches) for copy in leave(b)]:
        copy.wait()


def back_kernel(
    h_in, slope_in, gap_in, da_in, x_in, dn_in, zn_in, _,
    keep, send, h_s, slope_s, gap_s, da_s, x_s, dn, zn, g_e, g_z, sems, fixed_sems,
    *, batches, rows,
):
    bottom = lax.axis_index("level") == 1
    pairs = ((h_in, h_s), (slope_in, slope_s), (gap_in, gap_s), (da_in, da_s))

    def fetch(b):
        return [pltpu.make_async_copy(a.at[b], o.at[b], sems.at[n, b]) for n, (a, o) in enumerate(pairs)]

    fixed = [
        pltpu.make_async_copy(a, o, fixed_sems.at[n])
        for n, (a, o) in enumerate(((dn_in, dn), (zn_in, zn), (x_in, x_s)))
    ]
    count = h_s.shape[0]
    copies = [fetch(b) for b in range(count)]
    for copy in [fixed[0], copies[0][3], copies[0][2], fixed[1], *copies[0][:2], fixed[2]]:
        copy.start()
    g_e[...] = jnp.zeros_like(g_e)
    g_z[...] = jnp.zeros_like(g_z)
    fixed[0].wait()
    copies[0][3].wait()
    for b in range(1, count):
        for n in (3, 2, 0, 1):
            copies[b][n].start()
    du = spread_back(dn, da_s[0])
    for copy in [fixed[1], fixed[2]]:
        copy.wait()
    for b in range(count):
        for copy in copies[b][:3]:
            copy.wait()
        if b + 1 < count:
            copies[b + 1][3].wait()
        row = b * (rows + 2)
        encoder_back(du, gap_s[b], h_s[b], slope_s[b], patches(x_s, row, rows), zn, g_z, g_e)
        if b + 1 < count:
            du = spread_back(dn, da_s[b + 1])
    give = giver(bottom, send)
    give(S_Z, g_z[0:64, 0:128], g_z[64:128, 128:256], keep, 0)
    enc = []
    for cols in (slice(0, 128), slice(128, 256)):
        runs = [g_e[patch_row(t) : patch_row(t) + 3, cols] for t in range(9)]
        enc.append(jnp.concatenate(runs + [jnp.zeros((5, 128), F32)], 0))
    give(S_E, enc[0], enc[1], keep, 0)


def exact_sum(total, first):
    value = sum(total[first + EXACT * i : first + EXACT * (i + 1)] for i in range(3))
    pieces = [piece.astype(F32) for piece in part(value, 3)]
    return jnp.concatenate([total[:first], *pieces, total[first + 3 * EXACT :]], 0).astype(BF)


def merge_kernel(keep, early, got, big, early_out):
    size = keep.shape[0]
    big[...] = (keep[...] + got[0:size].astype(F32)).astype(BF)
    total = early[...].astype(F32) + got[size : size + SMALL - LATE].astype(F32)
    early_out[...] = exact_sum(total, S_X - LATE)


def sum_kernel(parts, out):
    total = parts[0].astype(F32)
    for i in range(1, parts.shape[0]):
        total = total + parts[i].astype(F32)
    out[...] = total.astype(BF)


def update_kernel(
    *refs, stages, start, other
):
    (parts, refs) = refs[:stages], refs[stages:]
    (count, total, ew, e1, e2, zw, z1, z2, dw, d1, d2, ow, o1, o2,
     loss_out, valid_out, count_out, total_out,
     em, es, ep, ec, zm, zs, zp, zc, dm, ds, dp, dc, om, os, op, oc, big, rows) = refs
    share = big.shape[0] // stages
    top = lax.axis_index("level") == 0
    index = (lax.axis_index("dp") >> jnp.where(top, start, other)) & (stages - 1)
    size = big.shape[0] // lax.axis_size("dp")
    small = jnp.zeros((SMALL, W), F32)
    for n, ref in enumerate(parts):
        value = ref[0:share].astype(F32)
        for h in range(share // size):
            place = h * stages + (index ^ n)
            if other != start:
                place = jnp.where(top, place, (index ^ n) * (share // size) + h)
            row = pl.multiple_of(place * size, 8)
            big[pl.ds(row, size), :] = value[h * size : (h + 1) * size]
        small = small + ref[share : share + SMALL].astype(F32)
    exact = sum(small[S_X + EXACT * i : S_X + EXACT * (i + 1)] for i in range(3))
    loss = jnp.sum(exact[4:5, 0:1])
    valid = jnp.sum(exact[4:5, 1:2])
    loss_out[0, 0] = loss
    valid_out[0, 0] = valid
    counts = jnp.concatenate([exact[i : i + 1] for i in range(4)], 1)
    count_out[...] = 0.99 * count[...] + 0.01 * counts
    for quarter in range(4):
        row = TAPS + (quarter % 2) * 128 + (quarter // 2) * 64
        cols = slice(quarter * 128, (quarter + 1) * 128)
        total_out[0, :, cols] = 0.99 * total[0, :, cols] + 0.01 * big[row : row + 64]

    scale = 1.0 - 0.5**STEP

    def adamw(grad, weight, first, second, rate):
        grad = grad / valid
        moment = 0.5 * first + 0.5 * grad
        square = 0.5 * second + 0.5 * grad * grad
        master = weight - rate * (moment / scale / (jnp.sqrt(square / scale) + 1e-08) + 0.01 * weight)
        return moment, square, master

    def whole(grad, w, first, second, rate, outs):
        outs[0][0], outs[1][0], master = adamw(grad, w[0], first[0], second[0], rate)
        outs[2][0] = master
        outs[3][0] = master.astype(BF)

    def by_row(grad, w, first, second, rate, outs):
        n = w.shape[0]
        for i in range(n):
            outs[0][i], outs[1][i], master = adamw(grad[i : i + 1], w[i], first[i], second[i], rate)
            outs[2][i] = master
            rows[i : i + 1] = master
        outs[3][0] = rows[0:n].astype(BF)

    by_row(small[S_E : S_E + 27], ew, e1, e2, RATES[0], (em, es, ep, ec))
    whole(small[S_Z : S_Z + 64], zw, z1, z2, RATES[1], (zm, zs, zp, zc))
    whole(big[0:TAPS], dw, d1, d2, RATES[2], (dm, ds, dp, dc))
    by_row(small[S_O : S_O + 3], ow, o1, o2, RATES[3], (om, os, op, oc))


def radices(devices):
    bits = devices.bit_length() - 1
    return [(start, min(2, bits - start)) for start in range(0, bits, 2)]


def partners(start, width):
    return [k << start for k in range(1, 1 << width)]


def xor_pairs(devices, by, other):
    return [(i, i ^ by) for i in range(devices)] + [(devices + i, devices + (i ^ other)) for i in range(devices)]


def lowered(value):
    return lax.reduce_precision(value, 8, 7)


def sum_small(parts, first):
    total = sum(item.astype(F32) for item in parts)
    value = sum(total[first + EXACT * i : first + EXACT * (i + 1)] for i in range(3))
    high = lowered(value)
    middle = lowered(value - high)
    low = value - high - middle
    rest = total[first + 3 * EXACT :]
    return jnp.concatenate([total[:first], high, middle, low, rest], 0).astype(BF)


def local(
    image, mask, codes, ema_count, ema_sum,
    encoder_weight, encoder_first, encoder_second,
    latent_weight, latent_first, latent_second,
    decoder_weight, decoder_first, decoder_second,
    readout_weight, readout_first, readout_second,
):
    batches, _, band, width = image.shape
    rows = band // 2
    me, devices = lax.axis_index("dp"), lax.axis_size("dp")
    ema_sum = jnp.swapaxes(ema_sum, 1, 2)
    encoder_weight, encoder_first, encoder_second = (
        jnp.swapaxes(item, 0, 1) for item in (encoder_weight, encoder_first, encoder_second)
    )
    latent_weight, latent_first, latent_second = (
        jnp.swapaxes(item, 1, 2) for item in (latent_weight, latent_first, latent_second)
    )
    readout_weight, readout_first, readout_second = (
        jnp.transpose(item, (2, 0, 1)) for item in (readout_weight, readout_first, readout_second)
    )

    def limit(mib):
        return pltpu.CompilerParams(vmem_limit_bytes=mib * 1024 * 1024)

    def outside(*items):
        return [pltpu.with_memory_space_constraint(item, pltpu.HBM) for item in items]

    def inside_vmem(item):
        return pltpu.with_memory_space_constraint(item, pltpu.VMEM)

    swap = [(0, 1), (1, 0)]
    others = lax.ppermute(codes, "level", swap)
    tiled = pltpu.VMEM((batches * band * 8, W), F32)
    pack, tile = pl.pallas_call(
        pack_kernel,
        out_shape=[pltpu.VMEM((PACKED, W), BF), tiled],
        in_specs=[VMEM] * 9,
        out_specs=[VMEM] * 2,
        scratch_shapes=[pltpu.VMEM((128, 128), F32)],
        compiler_params=limit(56),
    )(
        *outside(
            image, mask, codes, ema_count, ema_sum, encoder_weight, latent_weight, decoder_weight, readout_weight
        )
    )
    others, pack, tile = lax.optimization_barrier((others, pack, tile))
    tile, near = pl.pallas_call(
        rows_kernel,
        out_shape=[tiled, pltpu.VMEM((batches * 16, W), BF)],
        in_specs=[VMEM] * 2,
        out_specs=[VMEM] * 2,
        input_output_aliases={0: 0},
        compiler_params=limit(32),
    )(inside_vmem(tile), inside_vmem(others))

    both = ("level", "dp")
    inside = [d for d in range(1, devices) if (d + 1) * band % CROP != 0]
    pairs = [(d - 1, d) for d in inside] + [(devices + d, devices + d - 1) for d in inside]
    near = lax.ppermute(near, both, pairs)
    theirs = lax.ppermute(pack, "level", swap)

    ext = rows + 4
    ext = rows + 4
    pixels = batches * rows * W
    framed = batches * (rows + 2) * W
    held = [
        ((batches, 256, rows * W), BF),
        ((batches, 256, rows * W), BF),
        ((batches, 128, rows * W), F32),
        ((batches, 256, (rows + 2) * W), BF),
    ]
    fixed = [((3, 16, framed), BF), ((384, 768), BF), ((256, 128), BF)]
    size = -(-BIG // (8 * devices)) * 8
    padded = size * devices
    shape = jax.ShapeDtypeStruct
    staged = [
        pltpu.VMEM((3, 128, batches * ext * W), BF),
        *[pltpu.VMEM(*item) for item in held[:3]],
        pltpu.VMEM(*fixed[0]),
        pltpu.VMEM((2, 144, 256), F32),
        pltpu.VMEM((144, 256), F32),
    ]
    stages_early = pl.pallas_call(
        functools.partial(early_kernel, batches=batches, rows=rows),
        out_shape=staged,
        in_specs=[VMEM] * 3,
        out_specs=[VMEM] * 7,
        scratch_shapes=[pltpu.VMEM((256, 128), BF), pltpu.VMEM((128, 256), BF)],
        compiler_params=limit(EARLY_MIB),
        cost_estimate=pl.CostEstimate(flops=3 << 30, bytes_accessed=1 << 20, transcendentals=0),
    )(*[inside_vmem(item) for item in (tile, pack, theirs)])
    results = pl.pallas_call(
        functools.partial(step_kernel, batches=batches, rows=rows),
        out_shape=[
            pltpu.VMEM((padded, W), F32),
            pltpu.VMEM((SMALL - LATE, W), BF),
            pltpu.VMEM((padded + SMALL - LATE, W), BF),
            *[shape(*item) for item in held + fixed],
            *staged,
        ],
        in_specs=[VMEM] * 11,
        out_specs=[VMEM] * 3 + [AWAY] * 7 + [VMEM] * 7,
        input_output_aliases={4 + i: 10 + i for i in range(7)},
        scratch_shapes=[
            pltpu.VMEM((2 * batches, 8, W), F32),
            pltpu.VMEM((256, TAPS), BF),
            pltpu.VMEM((256, 128), BF),
            pltpu.VMEM((128, 256), BF),
            pltpu.VMEM((16, 256), BF),
            pltpu.VMEM((256, 16), BF),
            pltpu.VMEM(*held[3]),
            *[pltpu.VMEM(*item) for item in fixed[1:]],
            pltpu.VMEM((TAPS, 256), F32),
            pltpu.VMEM((256, 16), F32),
            pltpu.SemaphoreType.DMA((4, batches)),
            pltpu.SemaphoreType.DMA((3,)),
        ],
        compiler_params=limit(STEP_MIB),
    )(*[inside_vmem(item) for item in (tile, near, pack, theirs, *stages_early)])
    keep, early, send = results[:3]
    kept = results[3:10]

    got = lax.ppermute(send, "level", swap)
    big, early = pl.pallas_call(
        merge_kernel,
        out_shape=[pltpu.VMEM((padded, W), BF), pltpu.VMEM((SMALL - LATE, W), BF)],
        in_specs=[VMEM] * 3,
        out_specs=[VMEM] * 2,
        compiler_params=limit(32),
    )(*[inside_vmem(item) for item in (keep, early, got)])
    big = lax.all_to_all(big.reshape(devices, size, W), "dp", 0, 0)

    late, send = pl.pallas_call(
        functools.partial(back_kernel, batches=batches, rows=rows),
        out_shape=[pltpu.VMEM((LATE, W), BF), pltpu.VMEM((LATE, W), BF)],
        in_specs=[AWAY] * 8,
        out_specs=[VMEM] * 2,
        scratch_shapes=[
            *[pltpu.VMEM(*item) for item in held + fixed],
            pltpu.VMEM((PATCH, 256), F32),
            pltpu.VMEM((128, 256), F32),
            pltpu.SemaphoreType.DMA((4, batches)),
            pltpu.SemaphoreType.DMA((3,)),
        ],
        compiler_params=limit(BACK_MIB),
        cost_estimate=pl.CostEstimate(flops=2 * pixels * 98304 * 4, bytes_accessed=1 << 20, transcendentals=0),
    )(*outside(*kept), got)
    got = lax.ppermute(send, "level", swap)
    late = (late.astype(F32) + got.astype(F32)).astype(BF)
    small = jnp.concatenate([late, early], 0)

    big = pl.pallas_call(
        sum_kernel,
        out_shape=pltpu.VMEM((size, W), BF),
        in_specs=[VMEM],
        out_specs=VMEM,
        compiler_params=limit(32),
        cost_estimate=pl.CostEstimate(flops=1 << 34, bytes_accessed=1 << 20, transcendentals=0),
    )(inside_vmem(big))[None]
    stages = radices(devices)
    crossed = len(stages) == 2 and stages[0][1] == stages[1][1]
    for number, (start, width_bits) in enumerate(reversed(stages)):
        count = 1 << width_bits
        other = stages[number][0] if crossed else start
        index = (me >> jnp.where(lax.axis_index("level") == 0, start, other)) & (count - 1)
        payload = jnp.concatenate([big.reshape(-1, W), small], 0)
        parts = [payload] + [
            lax.ppermute(payload, both, xor_pairs(devices, k << start, k << other)) for k in range(1, count)
        ]
        if number == len(stages) - 1:
            break
        high = big.shape[0]
        stacked = jnp.zeros((high, count, size, W), BF)
        far_first = [0, *range(count - 1, 0, -1)]
        for k in far_first:
            piece = parts[k][: high * size].reshape(high, size, W)
            stacked = lax.dynamic_update_index_in_dim(stacked, piece, index ^ k, 1)
        small = sum_small([parts[k][high * size :] for k in far_first], S_X)
        big = stacked.reshape(high * count, size, W)

    state = (
        ema_count, ema_sum,
        encoder_weight, encoder_first, encoder_second, latent_weight, latent_first, latent_second,
        decoder_weight, decoder_first, decoder_second, readout_weight, readout_first, readout_second,
    )
    outs = [jax.ShapeDtypeStruct((1, 1), F32)] * 2
    outs += [jax.ShapeDtypeStruct(ema_count.shape, F32), jax.ShapeDtypeStruct(ema_sum.shape, F32)]
    for item in (encoder_weight, latent_weight, decoder_weight, readout_weight):
        copy = item.shape if item.shape[0] == 1 else (1, item.shape[0], item.shape[2])
        outs += [jax.ShapeDtypeStruct(item.shape, F32)] * 3 + [jax.ShapeDtypeStruct(copy, BF)]
    result = pl.pallas_call(
        functools.partial(update_kernel, stages=len(parts), start=start, other=other),
        out_shape=outs,
        in_specs=[VMEM] * (len(parts) + len(state)),
        out_specs=[SMEM] * 2 + [VMEM] * (len(outs) - 2),
        scratch_shapes=[pltpu.VMEM((padded, W), F32), pltpu.VMEM((32, W), F32)],
        compiler_params=limit(16),
    )(*parts, *state)
    loss, valid, count_new, total_new = result[:4]
    enc, lat, dec, read = (list(result[4 * n : 4 * n + 4]) for n in range(1, 5))
    enc[:3] = [jnp.swapaxes(item, 0, 1) for item in enc[:3]]
    lat = [jnp.swapaxes(item, 1, 2) for item in lat]
    read = [jnp.transpose(item, (1, 2, 0)) for item in read[:3]] + [jnp.swapaxes(read[3], 1, 2)]
    return (loss.reshape(()), valid.reshape(()), count_new, jnp.swapaxes(total_new, 1, 2), *enc, *lat, *dec, *read)


def solution(mesh):
    rank = (0, 0, 2, 3) + (3,) * 16
    in_specs = (P(None, None, "dp", None), P(None, "dp", None), P("level", None, "dp", None), P("level", None))
    in_specs += (P("level", None, None),) * 13
    out_specs = tuple(P(*(("level",) + (None,) * (n - 1) if n else ())) for n in rank)
    return jax.shard_map(local, mesh=mesh, in_specs=in_specs, out_specs=out_specs, check_vma=False)
```

```python
import functools

import jax
import jax.numpy as jnp
from jax import lax
from jax.experimental import pallas as pl
from jax.experimental.pallas import tpu as pltpu
from jax.sharding import PartitionSpec as P

CROP = 128
STEP = 5
RATES = (0.05, 0.03, 0.01, 0.03)

F32 = jnp.float32
BF = jnp.bfloat16
W = 128
EARLY_MIB, STEP_MIB, BACK_MIB = 36, 36, 56
NOBODY = 300.0

TAPS = 9 * 128
R_ET = TAPS
R_ZN = R_ET + 128
R_ZT = R_ZN + 128
R_OT = R_ZT + 64
R_BT = R_OT + 16
PACKED = R_BT + 256
BIG = TAPS + 256
S_Z, S_E, S_O, S_X = 0, 64, 96, 112
LATE, SMALL = 96, 128
EXACT = 5
PATCH = 96

NN = (((1,), (0,)), ((), ()))
NT = (((1,), (1,)), ((), ()))
VMEM = pl.BlockSpec(memory_space=pltpu.VMEM)
SMEM = pl.BlockSpec(memory_space=pltpu.SMEM)
AWAY = pl.BlockSpec(memory_space=pl.ANY)


def dot(a, b, dims=NN):
    return lax.dot_general(a, b, dims, preferred_element_type=F32)


def part(value, count):
    out = []
    for _ in range(count):
        piece = value.astype(BF)
        out.append(piece)
        value = value - piece.astype(F32)
    return out


def patch_row(t):
    dr, dc = t // 3, t % 3
    return ((dr // 2) * 3 + dc) * 16 + (dr % 2) * 8


def fitted(code):
    return jnp.where(code < 256, code, code - 512).astype(F32)


def rows_kernel(_, others, tile, near):
    level = lax.axis_index("level")
    _, batches, band, _ = others.shape
    for b in range(batches):
        bottom_rows, top_rows = (pl.ds(b * band * 8 + c, band, stride=8) for c in (4, 5))
        mine, theirs = tile[bottom_rows, :], fitted(others[0, b])
        tile[bottom_rows, :] = jnp.where(level == 1, mine, theirs)
        tile[top_rows, :] = jnp.where(level == 1, theirs, mine)
    for b in range(batches):
        row = jnp.where(level == 0, band - 2, 0)
        start = pl.multiple_of((b * band + row) * 8, 8)
        near[b * 16 : (b + 1) * 16] = tile[pl.ds(start, 16), :].astype(BF)


def pack_kernel(image, mask, codes, count, total, enc, lat, dec, read, pack, tile, flat):
    batches, _, band, _ = image.shape
    for b in range(batches):
        planes = [image[b, c].astype(F32) for c in range(3)] + [mask[b].astype(F32), fitted(codes[0, b])]
        planes += [jnp.zeros((band, W), F32)] * 3
        for c, plane in enumerate(planes):
            tile[pl.ds(b * band * 8 + c, band, stride=8), :] = plane
    pack[0:TAPS] = dec[0].astype(BF)
    flat[...] = jnp.zeros_like(flat)
    for t in range(9):
        for c in range(3):
            row = patch_row(t) + c
            flat[row : row + 1] = enc[3 * t + c]
    pack[R_ET : R_ET + 128] = flat[...].T.astype(BF)
    flat[...] = jnp.zeros_like(flat)
    flat[0:64] = lat[0]
    pack[R_ZT : R_ZT + 64] = lat[0].astype(BF)
    pack[R_ZN : R_ZN + 128] = flat[...].T.astype(BF)
    blank = jnp.zeros((13, 128), F32)
    pack[R_OT : R_OT + 16] = jnp.concatenate([read[0], read[1], read[2], blank], 0).astype(BF)
    book = total[0] / count[...]
    for quarter in range(4):
        row = R_BT + (quarter % 2) * 128 + (quarter // 2) * 64
        pack[row : row + 64] = book[:, quarter * 128 : (quarter + 1) * 128].astype(BF)


def sides(v):
    lane = lax.broadcasted_iota(jnp.int32, (v.shape[0], W), 1)
    before, after = [], []
    for i in range(v.shape[1] // W):
        row = v[:, i * W : (i + 1) * W]
        before.append(jnp.where(lane == 0, 0.0, pltpu.roll(row, 1, 1)))
        after.append(jnp.where(lane == W - 1, 0.0, pltpu.roll(row, W - 1, 1)))
    if len(before) == 1:
        return before[0], v, after[0]
    return jnp.concatenate(before, 1), v, jnp.concatenate(after, 1)


def at(row, rows):
    return pl.ds(pl.multiple_of(row * W, W), rows * W)


def fold(v, width):
    return sum(v[:, i : i + width] for i in range(0, v.shape[1], width))


def silu_parts(half):
    p = jnp.tanh(half) + 1.0
    out = half * p
    return out, p + out * (2.0 - p)


def one_hots(here):
    ids = lax.broadcasted_iota(jnp.int32, (256, here.shape[1]), 0).astype(F32)
    onehots, highs = [], []
    for v in range(2):
        code = here[4 + v : 5 + v]
        high = code < 0.0
        low = jnp.where(high, code + 256.0, code)
        onehots.append(jnp.where(ids == low, 1.0, 0.0).astype(BF))
        highs.append(high)
    return onehots, highs


def quantized(onehots, highs, bt):
    quants = []
    for onehot, high, book in zip(onehots, highs, bt):
        both = dot(book, onehot)
        quants.append(jnp.where(high, both[64:128], both[0:64]))
    return jnp.concatenate(quants, 0)


def books(mine, theirs, bottom):
    a, b = (jnp.concatenate([pack[R_BT : R_BT + 128], pack[R_BT + 128 : R_BT + 256]], 1) for pack in (mine, theirs))
    return jnp.where(bottom, a, b), jnp.where(bottom, b, a)


def either(mine, theirs, bottom, start, size):
    a, b = mine[start : start + size], theirs[start : start + size]
    return jnp.where(bottom, a, b), jnp.where(bottom, b, a)


def encoder_weights(mine, theirs, bottom, et, zt):
    one, zero = either(mine, theirs, bottom, R_ET, 128)
    et[0:128] = (0.5 * one.astype(F32)).astype(BF)
    et[128:256] = (0.5 * zero.astype(F32)).astype(BF)
    one, zero = either(mine, theirs, bottom, R_ZT, 64)
    blank = jnp.zeros((64, 128), BF)
    zt[0:64] = jnp.concatenate([one, blank], 1)
    zt[64:128] = jnp.concatenate([blank, zero], 1)


def encoded(x, u, k, onehots, highs, et, zt, g_s):
    h, slope = silu_parts(dot(et[:, 0:PATCH], x))
    h = h.astype(BF)
    z = dot(zt[...], h)
    gap = z - u
    kept = k * gap
    z = k * z.astype(BF).astype(F32)
    row = lax.broadcasted_iota(jnp.int32, (16, z.shape[1]), 0)
    for v in range(2):
        part_z = z[v * 64 : v * 64 + 64]
        high = highs[v]
        low_k = jnp.where(high, 0.0, k)
        high_k = jnp.where(high, k, 0.0)
        left = jnp.concatenate(
            [
                jnp.where(high, 0.0, part_z),
                jnp.where(high, part_z, 0.0),
                jnp.where(row == 0, low_k, jnp.where(row == 1, high_k, 0.0)),
            ],
            0,
        ).astype(BF)
        g_s[v] += dot(left, onehots[v], NT)
    return h, slope, 0.5 * kept, kept * gap


def early_kernel(
    tile, mine, theirs,
    u_s, h_s, slope_s, gap_s, x_s, g_s, l_s, et, zt,
    *, batches, rows,
):
    level = lax.axis_index("level")
    bottom = level == 1
    edge = level * (rows - 1)
    bt = books(mine, theirs, bottom)
    encoder_weights(mine, theirs, bottom, et, zt)
    for ref in (g_s, l_s):
        ref[...] = jnp.zeros_like(ref)

    def batch(b, _):
        def row(i):
            return tile[pl.ds(pl.multiple_of((b * 2 * rows + i) * 8, 8), 8), :]

        run = [row(jnp.clip(level * rows + r, 0, 2 * rows - 1)) for r in range(-1, rows + 2)]
        value = jnp.concatenate([jnp.concatenate(run[i : i + 2], 0) for i in range(rows + 2)], 1)
        for dc, view in enumerate(sides(value)):
            x_s[dc, :, at(b * (rows + 2), rows + 2)] = view.astype(BF)
        own = run[1 : rows + 1]
        beyond = [row(rows - 2 * level + i) for i in range(2)]
        onehots, highs = one_hots(jnp.concatenate(own + beyond, 1))
        u = quantized(onehots, highs, bt)
        inner = slice(0, rows * W)
        for k, view in enumerate(sides(u)):
            view = view.astype(BF)
            u_s[k, :, at(b * (rows + 4) + 2, rows)] = view[:, inner]
            u_s[k, :, at(b * (rows + 4) + (rows + 2) * (1 - level), 2)] = view[:, rows * W :]
        k = jnp.concatenate([jnp.where(edge == i, 0.0, own[i][3:4]) for i in range(rows)], 1)
        h, slope, gap, error = encoded(
            patches(x_s, b * (rows + 2), rows), u[:, inner], k,
            [item[:, inner] for item in onehots], [item[:, inner] for item in highs], et, zt, g_s,
        )
        h_s[b] = h
        slope_s[b] = slope.astype(BF)
        gap_s[b] = gap
        l_s[0:128] += fold(error, 256)
        return 0

    lax.fori_loop(0, batches, batch, 0, unroll=True)


def patches(x_s, row, n):
    return jnp.concatenate([x_s[dc, :, at(row + pair, n)] for pair in (0, 2) for dc in range(3)], 0)


def giver(bottom, send):
    def give(start, one, zero, keep, offset, shift=0):
        n = one.shape[0]
        keep[start - shift : start - shift + n] = jnp.where(bottom, one, zero).astype(keep.dtype)
        start = offset + start - shift
        send[start : start + n] = jnp.where(bottom, zero, one).astype(BF)

    return give


def spread_back(dn, da):
    rows = da.shape[1] // W - 2
    near = jnp.concatenate([da[:, (2 - dr) * W : (2 - dr + rows) * W] for dr in range(3)], 0)
    spread = dot(dn[...], near)
    _, _, after = sides(spread[0:128])
    before, _, _ = sides(spread[256:384])
    return after + spread[128:256] + before


def encoder_back(du, gap, h, slope, x, zn, g_z, g_e):
    dz = (du + gap).astype(BF)
    g_z[...] += dot(dz, h, NT)
    dpre = (dot(zn[...], dz) * slope).astype(BF)
    g_e[...] += dot(x, dpre, NT)


def step_kernel(
    tile, near, mine, theirs, *refs,
    batches, rows,
):
    (keep_big, keep_small, send, h_out, slope_out, gap_out, da_out, x_out, dn_out, zn_out,
     u_s, h_s, slope_s, gap_s, x_s, g_s, l_s,
     t_s, dt, et, zt, ot, on, da_s, dn, zn, g_d, g_o, sems, fixed_sems) = refs[7:]
    level, me, devices = lax.axis_index("level"), lax.axis_index("dp"), lax.axis_size("dp")
    band, ext = 2 * rows, rows + 4
    above, below = (me + 1) * band, (me + 2) * band
    top_ok = (lax.rem(above, CROP) != 0) & (me > 0)
    bottom_ok = (lax.rem(below, CROP) != 0) & (me < devices - 1)
    valid = jnp.where(level == 0, top_ok.astype(jnp.int32), bottom_ok.astype(jnp.int32))
    bottom = level == 1

    def pair(start, size):
        return either(mine, theirs, bottom, start, size)

    for t in range(9):
        one, zero = pair(t * 128, 128)
        zero = jnp.concatenate([jnp.zeros((64, 128), BF), zero[0:64]], 0)
        dr, dc = t // 3, t % 3
        dn[dc * 128 : (dc + 1) * 128, dr * 256 : dr * 256 + 128] = one
        dn[dc * 128 : (dc + 1) * 128, dr * 256 + 128 : (dr + 1) * 256] = zero
        dt[0:128, t * 128 : (t + 1) * 128] = (0.5 * one.astype(F32)).T.astype(BF)
        dt[128:256, t * 128 : (t + 1) * 128] = (0.5 * zero.astype(F32)).T.astype(BF)
    encoder_weights(mine, theirs, bottom, et, zt)
    one, zero = pair(R_ZN, 128)
    zn[0:128] = (0.5 * one.astype(F32)).astype(BF)
    zn[128:256] = pltpu.roll(0.5 * zero.astype(F32), 64, 1).astype(BF)
    one, zero = pair(R_OT, 16)
    blank = jnp.zeros((8, 128), F32)
    out_t = jnp.concatenate(
        [
            jnp.concatenate([one[0:8].astype(F32), blank], 1),
            jnp.concatenate([blank, zero[0:8].astype(F32)], 1),
        ],
        0,
    )
    ot[...] = out_t.astype(BF)
    on[...] = (0.5 * out_t).T.astype(BF)
    bt = books(mine, theirs, bottom)
    fixed = [
        pltpu.make_async_copy(a, o, fixed_sems.at[n])
        for n, (a, o) in enumerate(((x_s, x_out), (dn, dn_out), (zn, zn_out)))
    ]
    fixed[1].start()
    fixed[2].start()

    sub = lax.broadcasted_iota(jnp.int32, (8, W), 0)
    nothing = jnp.where((sub == 4) | (sub == 5), NOBODY, 0.0)

    outside = []
    for b in range(batches):
        both = near[b * 16 : (b + 1) * 16].astype(F32)
        for r in range(2):
            outside.append(jnp.where(valid > 0, both[r * 8 : (r + 1) * 8], nothing))
    for i, shown in enumerate(outside):
        t_s[i] = shown

    def row(b, r):
        return tile[pl.ds(pl.multiple_of((b * band + r) * 8, 8), 8), :]

    for ref in (g_d, g_o):
        ref[...] = jnp.zeros_like(ref)

    def spread_rows(u, b, e, n):
        for k, view in enumerate(sides(u)):
            u_s[k, :, at(b * ext + e, n)] = view.astype(BF)

    first = level * rows
    runs = []
    for b in range(batches):
        low, high = outside[2 * b], outside[2 * b + 1]
        runs.append(jnp.concatenate([jnp.where(bottom, row(b, band - 1), high), jnp.where(bottom, low, row(b, 0))], 0))
        runs.append(jnp.concatenate([jnp.where(bottom, low, row(b, 0)), jnp.where(bottom, high, row(b, 1))], 0))
    for dc, view in enumerate(sides(jnp.concatenate(runs, 1))):
        view = view.astype(BF)
        for b in range(batches):
            x_s[dc, :, at(b * (rows + 2) + first, 2)] = view[:, b * 2 * W : (b + 1) * 2 * W]
    outer, edge = jnp.where(bottom, rows + 2, 0), level * (rows - 1)
    u = quantized(*one_hots(jnp.concatenate(outside, 1)), bt)
    for b in range(batches):
        spread_rows(u[:, b * 2 * W : (b + 1) * 2 * W], b, outer, 2)
    here = jnp.concatenate([row(b, level * (band - 1)) for b in range(batches)], 1)
    u = jnp.concatenate([u_s[1, :, at(b * ext + 2 + edge, 1)] for b in range(batches)], 1).astype(F32)
    x = jnp.concatenate([patches(x_s, b * (rows + 2) + edge, 1) for b in range(batches)], 1)
    h, slope, gap, error = encoded(x, u, here[3:4], *one_hots(here), et, zt, g_s)
    l_s[0:128, 0:W] += fold(error, W)
    for b in range(batches):
        cols = slice(b * W, (b + 1) * W)
        h_s[b, :, at(edge, 1)] = h[:, cols]
        slope_s[b, :, at(edge, 1)] = slope[:, cols].astype(BF)
        gap_s[b, :, at(edge, 1)] = gap[:, cols]

    pairs = ((h_s, h_out), (slope_s, slope_out), (gap_s, gap_out), (da_s, da_out))

    def leave(b, which=range(4)):
        return [pltpu.make_async_copy(pairs[n][0].at[b], pairs[n][1].at[b], sems.at[n, b]) for n in which]

    fixed[0].start()
    for b in range(batches):
        for copy in leave(b, range(3)):
            copy.start()

    def decode(b, _):
        u = jnp.concatenate(
            [u_s[dc, :, at(b * ext + dr, rows + 2)] for dr in range(3) for dc in range(3)], 0
        )
        inner = slice(W, (1 + rows) * W)
        g, slope = silu_parts(dot(dt[...], u))
        g = g.astype(BF)
        y = dot(ot[...], g)
        shown = [row(b, jnp.clip(level * rows + r, 0, band - 1)) for r in range(-1, rows + 1)]
        shown[0] = jnp.where(bottom, shown[0], t_s[2 * b + 1])
        shown[-1] = jnp.where(bottom, t_s[2 * b], shown[-1])
        here = jnp.concatenate(shown, 1)
        k = here[3:4]
        x = jnp.where(lax.broadcasted_iota(jnp.int32, here.shape, 0) < 3, here, 0.0)
        diff = y - jnp.concatenate([x, x], 0)
        kept = k * diff
        dy = (2.0 * kept).astype(BF)
        da = (dot(on[...], dy) * slope).astype(BF)
        da_s[b] = da
        leave(b, [3])[0].start()
        l_s[128:144] += fold((kept * diff)[:, inner], 256)
        g_d[...] += dot(u[:, inner], da[:, inner], NT)
        g_o[...] += dot(g[:, inner], dy[:, inner], NT)
        return 0

    lax.fori_loop(0, batches, decode, 0)
    give = giver(bottom, send)
    for t in range(9):
        top = jnp.concatenate([g_d[t * 128 + 64 : (t + 1) * 128, 128:256], jnp.zeros((64, 128), F32)], 0)
        give(t * 128, g_d[t * 128 : (t + 1) * 128, 0:128], top, keep_big, 0)
    for half in range(2):
        cols = slice(half * 128, (half + 1) * 128)
        give(TAPS + half * 128, g_s[0, 0:128, cols], g_s[1, 0:128, cols], keep_big, 0)
    pad = keep_big.shape[0]
    if pad > BIG:
        keep_big[BIG:pad] = jnp.zeros((pad - BIG, W), F32)
        send[BIG:pad] = jnp.zeros((pad - BIG, W), BF)
    readouts = g_o[...].T
    blank = jnp.zeros((8, 128), F32)
    give(
        S_O,
        jnp.concatenate([readouts[0:8, 0:128], blank], 0),
        jnp.concatenate([readouts[8:16, 128:256], blank], 0),
        keep_small,
        pad,
        LATE,
    )
    valid_sum = jnp.sum(g_s[0, 128:130])
    loss = 0.25 * jnp.sum(l_s[0:128]) + jnp.sum(l_s[128:144])
    lane = lax.broadcasted_iota(jnp.int32, (1, W), 1)
    other = jnp.where(lane == 0, loss, jnp.where(lane == 1, valid_sum, 0.0))
    exact = []
    for v in range(2):
        runs = [g_s[v, 128 + hi : 129 + hi, half * 128 : (half + 1) * 128] for hi in range(2) for half in range(2)]
        pieces = part(jnp.concatenate(runs + [other], 0), 3)
        exact.append(jnp.concatenate([p.astype(F32) for p in pieces] + [jnp.zeros((1, 128), F32)], 0))
    give(S_X, exact[0], exact[1], keep_small, pad, LATE)
    for copy in fixed + [copy for b in range(batches) for copy in leave(b)]:
        copy.wait()


def back_kernel(
    h_in, slope_in, gap_in, da_in, x_in, dn_in, zn_in, _,
    keep, send, h_s, slope_s, gap_s, da_s, x_s, dn, zn, g_e, g_z, sems, fixed_sems,
    *, batches, rows,
):
    bottom = lax.axis_index("level") == 1
    pairs = ((h_in, h_s), (slope_in, slope_s), (gap_in, gap_s), (da_in, da_s))

    def fetch(b):
        return [pltpu.make_async_copy(a.at[b], o.at[b], sems.at[n, b]) for n, (a, o) in enumerate(pairs)]

    fixed = [
        pltpu.make_async_copy(a, o, fixed_sems.at[n])
        for n, (a, o) in enumerate(((dn_in, dn), (zn_in, zn), (x_in, x_s)))
    ]
    count = h_s.shape[0]
    copies = [fetch(b) for b in range(count)]
    for copy in [fixed[0], copies[0][3], copies[0][2], fixed[1], *copies[0][:2], fixed[2]]:
        copy.start()
    g_e[...] = jnp.zeros_like(g_e)
    g_z[...] = jnp.zeros_like(g_z)
    fixed[0].wait()
    copies[0][3].wait()
    for b in range(1, count):
        for n in (3, 2, 0, 1):
            copies[b][n].start()
    du = spread_back(dn, da_s[0])
    for copy in [fixed[1], fixed[2]]:
        copy.wait()
    for b in range(count):
        for copy in copies[b][:3]:
            copy.wait()
        if b + 1 < count:
            copies[b + 1][3].wait()
        row = b * (rows + 2)
        encoder_back(du, gap_s[b], h_s[b], slope_s[b], patches(x_s, row, rows), zn, g_z, g_e)
        if b + 1 < count:
            du = spread_back(dn, da_s[b + 1])
    give = giver(bottom, send)
    give(S_Z, g_z[0:64, 0:128], g_z[64:128, 128:256], keep, 0)
    enc = []
    for cols in (slice(0, 128), slice(128, 256)):
        runs = [g_e[patch_row(t) : patch_row(t) + 3, cols] for t in range(9)]
        enc.append(jnp.concatenate(runs + [jnp.zeros((5, 128), F32)], 0))
    give(S_E, enc[0], enc[1], keep, 0)


def exact_sum(total, first):
    value = sum(total[first + EXACT * i : first + EXACT * (i + 1)] for i in range(3))
    pieces = [piece.astype(F32) for piece in part(value, 3)]
    return jnp.concatenate([total[:first], *pieces, total[first + 3 * EXACT :]], 0).astype(BF)


def merge_kernel(keep, early, got, big, early_out):
    size = keep.shape[0]
    big[...] = (keep[...] + got[0:size].astype(F32)).astype(BF)
    total = early[...].astype(F32) + got[size : size + SMALL - LATE].astype(F32)
    early_out[...] = exact_sum(total, S_X - LATE)


def sum_kernel(parts, out):
    total = parts[0].astype(F32)
    for i in range(1, parts.shape[0]):
        total = total + parts[i].astype(F32)
    out[...] = total.astype(BF)


def update_kernel(
    *refs, stages, start, other
):
    (parts, refs) = refs[:stages], refs[stages:]
    (count, total, ew, e1, e2, zw, z1, z2, dw, d1, d2, ow, o1, o2,
     loss_out, valid_out, count_out, total_out,
     em, es, ep, ec, zm, zs, zp, zc, dm, ds, dp, dc, om, os, op, oc, big, rows) = refs
    share = big.shape[0] // stages
    top = lax.axis_index("level") == 0
    index = (lax.axis_index("dp") >> jnp.where(top, start, other)) & (stages - 1)
    size = big.shape[0] // lax.axis_size("dp")
    small = jnp.zeros((SMALL, W), F32)
    for n, ref in enumerate(parts):
        value = ref[0:share].astype(F32)
        for h in range(share // size):
            place = h * stages + (index ^ n)
            if other != start:
                place = jnp.where(top, place, (index ^ n) * (share // size) + h)
            row = pl.multiple_of(place * size, 8)
            big[pl.ds(row, size), :] = value[h * size : (h + 1) * size]
        small = small + ref[share : share + SMALL].astype(F32)
    exact = sum(small[S_X + EXACT * i : S_X + EXACT * (i + 1)] for i in range(3))
    loss = jnp.sum(exact[4:5, 0:1])
    valid = jnp.sum(exact[4:5, 1:2])
    loss_out[0, 0] = loss
    valid_out[0, 0] = valid
    counts = jnp.concatenate([exact[i : i + 1] for i in range(4)], 1)
    count_out[...] = 0.99 * count[...] + 0.01 * counts
    for quarter in range(4):
        row = TAPS + (quarter % 2) * 128 + (quarter // 2) * 64
        cols = slice(quarter * 128, (quarter + 1) * 128)
        total_out[0, :, cols] = 0.99 * total[0, :, cols] + 0.01 * big[row : row + 64]

    scale = 1.0 - 0.5**STEP

    def adamw(grad, weight, first, second, rate):
        grad = grad / valid
        moment = 0.5 * first + 0.5 * grad
        square = 0.5 * second + 0.5 * grad * grad
        master = weight - rate * (moment / scale / (jnp.sqrt(square / scale) + 1e-08) + 0.01 * weight)
        return moment, square, master

    def whole(grad, w, first, second, rate, outs):
        outs[0][0], outs[1][0], master = adamw(grad, w[0], first[0], second[0], rate)
        outs[2][0] = master
        outs[3][0] = master.astype(BF)

    def by_row(grad, w, first, second, rate, outs):
        n = w.shape[0]
        for i in range(n):
            outs[0][i], outs[1][i], master = adamw(grad[i : i + 1], w[i], first[i], second[i], rate)
            outs[2][i] = master
            rows[i : i + 1] = master
        outs[3][0] = rows[0:n].astype(BF)

    by_row(small[S_E : S_E + 27], ew, e1, e2, RATES[0], (em, es, ep, ec))
    whole(small[S_Z : S_Z + 64], zw, z1, z2, RATES[1], (zm, zs, zp, zc))
    whole(big[0:TAPS], dw, d1, d2, RATES[2], (dm, ds, dp, dc))
    by_row(small[S_O : S_O + 3], ow, o1, o2, RATES[3], (om, os, op, oc))


def radices(devices):
    bits = devices.bit_length() - 1
    return [(start, min(2, bits - start)) for start in range(0, bits, 2)]


def partners(start, width):
    return [k << start for k in range(1, 1 << width)]


def xor_pairs(devices, by, other):
    return [(i, i ^ by) for i in range(devices)] + [(devices + i, devices + (i ^ other)) for i in range(devices)]


def lowered(value):
    return lax.reduce_precision(value, 8, 7)


def sum_small(parts, first):
    total = sum(item.astype(F32) for item in parts)
    value = sum(total[first + EXACT * i : first + EXACT * (i + 1)] for i in range(3))
    high = lowered(value)
    middle = lowered(value - high)
    low = value - high - middle
    rest = total[first + 3 * EXACT :]
    return jnp.concatenate([total[:first], high, middle, low, rest], 0).astype(BF)


def local(
    image, mask, codes, ema_count, ema_sum,
    encoder_weight, encoder_first, encoder_second,
    latent_weight, latent_first, latent_second,
    decoder_weight, decoder_first, decoder_second,
    readout_weight, readout_first, readout_second,
):
    batches, _, band, width = image.shape
    rows = band // 2
    me, devices = lax.axis_index("dp"), lax.axis_size("dp")
    ema_sum = jnp.swapaxes(ema_sum, 1, 2)
    encoder_weight, encoder_first, encoder_second = (
        jnp.swapaxes(item, 0, 1) for item in (encoder_weight, encoder_first, encoder_second)
    )
    latent_weight, latent_first, latent_second = (
        jnp.swapaxes(item, 1, 2) for item in (latent_weight, latent_first, latent_second)
    )
    readout_weight, readout_first, readout_second = (
        jnp.transpose(item, (2, 0, 1)) for item in (readout_weight, readout_first, readout_second)
    )

    def limit(mib):
        return pltpu.CompilerParams(vmem_limit_bytes=mib * 1024 * 1024)

    def outside(*items):
        return [pltpu.with_memory_space_constraint(item, pltpu.HBM) for item in items]

    def inside_vmem(item):
        return pltpu.with_memory_space_constraint(item, pltpu.VMEM)

    swap = [(0, 1), (1, 0)]
    others = lax.ppermute(codes, "level", swap)
    tiled = pltpu.VMEM((batches * band * 8, W), F32)
    pack, tile = pl.pallas_call(
        pack_kernel,
        out_shape=[pltpu.VMEM((PACKED, W), BF), tiled],
        in_specs=[VMEM] * 9,
        out_specs=[VMEM] * 2,
        scratch_shapes=[pltpu.VMEM((128, 128), F32)],
        compiler_params=limit(56),
    )(
        *outside(
            image, mask, codes, ema_count, ema_sum, encoder_weight, latent_weight, decoder_weight, readout_weight
        )
    )
    others, pack, tile = lax.optimization_barrier((others, pack, tile))
    tile, near = pl.pallas_call(
        rows_kernel,
        out_shape=[tiled, pltpu.VMEM((batches * 16, W), BF)],
        in_specs=[VMEM] * 2,
        out_specs=[VMEM] * 2,
        input_output_aliases={0: 0},
        compiler_params=limit(32),
    )(inside_vmem(tile), inside_vmem(others))

    both = ("level", "dp")
    inside = [d for d in range(1, devices) if (d + 1) * band % CROP != 0]
    pairs = [(d - 1, d) for d in inside] + [(devices + d, devices + d - 1) for d in inside]
    near = lax.ppermute(near, both, pairs)
    theirs = lax.ppermute(pack, "level", swap)

    ext = rows + 4
    ext = rows + 4
    pixels = batches * rows * W
    framed = batches * (rows + 2) * W
    held = [
        ((batches, 256, rows * W), BF),
        ((batches, 256, rows * W), BF),
        ((batches, 128, rows * W), F32),
        ((batches, 256, (rows + 2) * W), BF),
    ]
    fixed = [((3, 16, framed), BF), ((384, 768), BF), ((256, 128), BF)]
    size = -(-BIG // (8 * devices)) * 8
    padded = size * devices
    shape = jax.ShapeDtypeStruct
    staged = [
        pltpu.VMEM((3, 128, batches * ext * W), BF),
        *[pltpu.VMEM(*item) for item in held[:3]],
        pltpu.VMEM(*fixed[0]),
        pltpu.VMEM((2, 144, 256), F32),
        pltpu.VMEM((144, 256), F32),
    ]
    stages_early = pl.pallas_call(
        functools.partial(early_kernel, batches=batches, rows=rows),
        out_shape=staged,
        in_specs=[VMEM] * 3,
        out_specs=[VMEM] * 7,
        scratch_shapes=[pltpu.VMEM((256, 128), BF), pltpu.VMEM((128, 256), BF)],
        compiler_params=limit(EARLY_MIB),
        cost_estimate=pl.CostEstimate(flops=3 << 30, bytes_accessed=1 << 20, transcendentals=0),
    )(*[inside_vmem(item) for item in (tile, pack, theirs)])
    results = pl.pallas_call(
        functools.partial(step_kernel, batches=batches, rows=rows),
        out_shape=[
            pltpu.VMEM((padded, W), F32),
            pltpu.VMEM((SMALL - LATE, W), BF),
            pltpu.VMEM((padded + SMALL - LATE, W), BF),
            *[shape(*item) for item in held + fixed],
            *staged,
        ],
        in_specs=[VMEM] * 11,
        out_specs=[VMEM] * 3 + [AWAY] * 7 + [VMEM] * 7,
        input_output_aliases={4 + i: 10 + i for i in range(7)},
        scratch_shapes=[
            pltpu.VMEM((2 * batches, 8, W), F32),
            pltpu.VMEM((256, TAPS), BF),
            pltpu.VMEM((256, 128), BF),
            pltpu.VMEM((128, 256), BF),
            pltpu.VMEM((16, 256), BF),
            pltpu.VMEM((256, 16), BF),
            pltpu.VMEM(*held[3]),
            *[pltpu.VMEM(*item) for item in fixed[1:]],
            pltpu.VMEM((TAPS, 256), F32),
            pltpu.VMEM((256, 16), F32),
            pltpu.SemaphoreType.DMA((4, batches)),
            pltpu.SemaphoreType.DMA((3,)),
        ],
        compiler_params=limit(STEP_MIB),
    )(*[inside_vmem(item) for item in (tile, near, pack, theirs, *stages_early)])
    keep, early, send = results[:3]
    kept = results[3:10]

    got = lax.ppermute(send, "level", swap)
    big, early = pl.pallas_call(
        merge_kernel,
        out_shape=[pltpu.VMEM((padded, W), BF), pltpu.VMEM((SMALL - LATE, W), BF)],
        in_specs=[VMEM] * 3,
        out_specs=[VMEM] * 2,
        compiler_params=limit(32),
    )(*[inside_vmem(item) for item in (keep, early, got)])
    big = lax.all_to_all(big.reshape(devices, size, W), "dp", 0, 0)

    late, send = pl.pallas_call(
        functools.partial(back_kernel, batches=batches, rows=rows),
        out_shape=[pltpu.VMEM((LATE, W), BF), pltpu.VMEM((LATE, W), BF)],
        in_specs=[AWAY] * 8,
        out_specs=[VMEM] * 2,
        scratch_shapes=[
            *[pltpu.VMEM(*item) for item in held + fixed],
            pltpu.VMEM((PATCH, 256), F32),
            pltpu.VMEM((128, 256), F32),
            pltpu.SemaphoreType.DMA((4, batches)),
            pltpu.SemaphoreType.DMA((3,)),
        ],
        compiler_params=limit(BACK_MIB),
        cost_estimate=pl.CostEstimate(flops=2 * pixels * 98304 * 4, bytes_accessed=1 << 20, transcendentals=0),
    )(*outside(*kept), got)
    got = lax.ppermute(send, "level", swap)
    late = (late.astype(F32) + got.astype(F32)).astype(BF)
    small = jnp.concatenate([late, early], 0)

    big = pl.pallas_call(
        sum_kernel,
        out_shape=pltpu.VMEM((size, W), BF),
        in_specs=[VMEM],
        out_specs=VMEM,
        compiler_params=limit(32),
        cost_estimate=pl.CostEstimate(flops=1 << 34, bytes_accessed=1 << 20, transcendentals=0),
    )(inside_vmem(big))[None]
    stages = radices(devices)
    crossed = len(stages) == 2 and stages[0][1] == stages[1][1]
    for number, (start, width_bits) in enumerate(reversed(stages)):
        count = 1 << width_bits
        other = stages[number][0] if crossed else start
        index = (me >> jnp.where(lax.axis_index("level") == 0, start, other)) & (count - 1)
        payload = jnp.concatenate([big.reshape(-1, W), small], 0)
        parts = [payload] + [
            lax.ppermute(payload, both, xor_pairs(devices, k << start, k << other)) for k in range(1, count)
        ]
        if number == len(stages) - 1:
            break
        high = big.shape[0]
        stacked = jnp.zeros((high, count, size, W), BF)
        far_first = [0, *range(count - 1, 0, -1)]
        for k in far_first:
            piece = parts[k][: high * size].reshape(high, size, W)
            stacked = lax.dynamic_update_index_in_dim(stacked, piece, index ^ k, 1)
        small = sum_small([parts[k][high * size :] for k in far_first], S_X)
        big = stacked.reshape(high * count, size, W)

    state = (
        ema_count, ema_sum,
        encoder_weight, encoder_first, encoder_second, latent_weight, latent_first, latent_second,
        decoder_weight, decoder_first, decoder_second, readout_weight, readout_first, readout_second,
    )
    outs = [jax.ShapeDtypeStruct((1, 1), F32)] * 2
    outs += [jax.ShapeDtypeStruct(ema_count.shape, F32), jax.ShapeDtypeStruct(ema_sum.shape, F32)]
    for item in (encoder_weight, latent_weight, decoder_weight, readout_weight):
        copy = item.shape if item.shape[0] == 1 else (1, item.shape[0], item.shape[2])
        outs += [jax.ShapeDtypeStruct(item.shape, F32)] * 3 + [jax.ShapeDtypeStruct(copy, BF)]
    result = pl.pallas_call(
        functools.partial(update_kernel, stages=len(parts), start=start, other=other),
        out_shape=outs,
        in_specs=[VMEM] * (len(parts) + len(state)),
        out_specs=[SMEM] * 2 + [VMEM] * (len(outs) - 2),
        scratch_shapes=[pltpu.VMEM((padded, W), F32), pltpu.VMEM((32, W), F32)],
        compiler_params=limit(16),
    )(*parts, *state)
    loss, valid, count_new, total_new = result[:4]
    enc, lat, dec, read = (list(result[4 * n : 4 * n + 4]) for n in range(1, 5))
    enc[:3] = [jnp.swapaxes(item, 0, 1) for item in enc[:3]]
    lat = [jnp.swapaxes(item, 1, 2) for item in lat]
    read = [jnp.transpose(item, (1, 2, 0)) for item in read[:3]] + [jnp.swapaxes(read[3], 1, 2)]
    return (loss.reshape(()), valid.reshape(()), count_new, jnp.swapaxes(total_new, 1, 2), *enc, *lat, *dec, *read)


def solution(mesh):
    rank = (0, 0, 2, 3) + (3,) * 16
    in_specs = (P(None, None, "dp", None), P(None, "dp", None), P("level", None, "dp", None), P("level", None))
    in_specs += (P("level", None, None),) * 13
    out_specs = tuple(P(*(("level",) + (None,) * (n - 1) if n else ())) for n in rank)
    return jax.shard_map(local, mesh=mesh, in_specs=in_specs, out_specs=out_specs, check_vma=False)
```

```python
import functools

import jax
import jax.numpy as jnp
from jax import lax
from jax.experimental import pallas as pl
from jax.experimental.pallas import tpu as pltpu
from jax.sharding import PartitionSpec as P

CROP = 128
STEP = 5
RATES = (0.05, 0.03, 0.01, 0.03)

F32 = jnp.float32
BF = jnp.bfloat16
W = 128
EARLY_MIB, STEP_MIB, BACK_MIB = 36, 36, 56
NOBODY = 300.0

TAPS = 9 * 128
R_ET = TAPS
R_ZN = R_ET + 128
R_ZT = R_ZN + 128
R_OT = R_ZT + 64
R_BT = R_OT + 16
PACKED = R_BT + 256
BIG = TAPS + 256
S_Z, S_E, S_O, S_X = 0, 64, 96, 112
LATE, SMALL = 96, 128
EXACT = 5
PATCH = 96

NN = (((1,), (0,)), ((), ()))
NT = (((1,), (1,)), ((), ()))
VMEM = pl.BlockSpec(memory_space=pltpu.VMEM)
SMEM = pl.BlockSpec(memory_space=pltpu.SMEM)
AWAY = pl.BlockSpec(memory_space=pl.ANY)


def dot(a, b, dims=NN):
    return lax.dot_general(a, b, dims, preferred_element_type=F32)


def part(value, count):
    out = []
    for _ in range(count):
        piece = value.astype(BF)
        out.append(piece)
        value = value - piece.astype(F32)
    return out


def patch_row(t):
    dr, dc = t // 3, t % 3
    return ((dr // 2) * 3 + dc) * 16 + (dr % 2) * 8


def fitted(code):
    return jnp.where(code < 256, code, code - 512).astype(F32)


def rows_kernel(_, others, tile, near):
    level = lax.axis_index("level")
    _, batches, band, _ = others.shape
    for b in range(batches):
        bottom_rows, top_rows = (pl.ds(b * band * 8 + c, band, stride=8) for c in (4, 5))
        mine, theirs = tile[bottom_rows, :], fitted(others[0, b])
        tile[bottom_rows, :] = jnp.where(level == 1, mine, theirs)
        tile[top_rows, :] = jnp.where(level == 1, theirs, mine)
    for b in range(batches):
        row = jnp.where(level == 0, band - 2, 0)
        start = pl.multiple_of((b * band + row) * 8, 8)
        near[b * 16 : (b + 1) * 16] = tile[pl.ds(start, 16), :].astype(BF)


def pack_kernel(image, mask, codes, count, total, enc, lat, dec, read, pack, tile, flat):
    batches, _, band, _ = image.shape
    for b in range(batches):
        planes = [image[b, c].astype(F32) for c in range(3)] + [mask[b].astype(F32), fitted(codes[0, b])]
        planes += [jnp.zeros((band, W), F32)] * 3
        for c, plane in enumerate(planes):
            tile[pl.ds(b * band * 8 + c, band, stride=8), :] = plane
    pack[0:TAPS] = dec[0].astype(BF)
    flat[...] = jnp.zeros_like(flat)
    for t in range(9):
        for c in range(3):
            row = patch_row(t) + c
            flat[row : row + 1] = enc[3 * t + c]
    pack[R_ET : R_ET + 128] = flat[...].T.astype(BF)
    flat[...] = jnp.zeros_like(flat)
    flat[0:64] = lat[0]
    pack[R_ZT : R_ZT + 64] = lat[0].astype(BF)
    pack[R_ZN : R_ZN + 128] = flat[...].T.astype(BF)
    blank = jnp.zeros((13, 128), F32)
    pack[R_OT : R_OT + 16] = jnp.concatenate([read[0], read[1], read[2], blank], 0).astype(BF)
    book = total[0] / count[...]
    for quarter in range(4):
        row = R_BT + (quarter % 2) * 128 + (quarter // 2) * 64
        pack[row : row + 64] = book[:, quarter * 128 : (quarter + 1) * 128].astype(BF)


def sides(v):
    lane = lax.broadcasted_iota(jnp.int32, (v.shape[0], W), 1)
    before, after = [], []
    for i in range(v.shape[1] // W):
        row = v[:, i * W : (i + 1) * W]
        before.append(jnp.where(lane == 0, 0.0, pltpu.roll(row, 1, 1)))
        after.append(jnp.where(lane == W - 1, 0.0, pltpu.roll(row, W - 1, 1)))
    if len(before) == 1:
        return before[0], v, after[0]
    return jnp.concatenate(before, 1), v, jnp.concatenate(after, 1)


def at(row, rows):
    return pl.ds(pl.multiple_of(row * W, W), rows * W)


def fold(v, width):
    return sum(v[:, i : i + width] for i in range(0, v.shape[1], width))


def silu_parts(half):
    p = jnp.tanh(half) + 1.0
    out = half * p
    return out, p + out * (2.0 - p)


def one_hots(here):
    ids = lax.broadcasted_iota(jnp.int32, (256, here.shape[1]), 0).astype(F32)
    onehots, highs = [], []
    for v in range(2):
        code = here[4 + v : 5 + v]
        high = code < 0.0
        low = jnp.where(high, code + 256.0, code)
        onehots.append(jnp.where(ids == low, 1.0, 0.0).astype(BF))
        highs.append(high)
    return onehots, highs


def quantized(onehots, highs, bt):
    quants = []
    for onehot, high, book in zip(onehots, highs, bt):
        both = dot(book, onehot)
        quants.append(jnp.where(high, both[64:128], both[0:64]))
    return jnp.concatenate(quants, 0)


def books(mine, theirs, bottom):
    a, b = (jnp.concatenate([pack[R_BT : R_BT + 128], pack[R_BT + 128 : R_BT + 256]], 1) for pack in (mine, theirs))
    return jnp.where(bottom, a, b), jnp.where(bottom, b, a)


def either(mine, theirs, bottom, start, size):
    a, b = mine[start : start + size], theirs[start : start + size]
    return jnp.where(bottom, a, b), jnp.where(bottom, b, a)


def encoder_weights(mine, theirs, bottom, et, zt):
    one, zero = either(mine, theirs, bottom, R_ET, 128)
    et[0:128] = (0.5 * one.astype(F32)).astype(BF)
    et[128:256] = (0.5 * zero.astype(F32)).astype(BF)
    one, zero = either(mine, theirs, bottom, R_ZT, 64)
    blank = jnp.zeros((64, 128), BF)
    zt[0:64] = jnp.concatenate([one, blank], 1)
    zt[64:128] = jnp.concatenate([blank, zero], 1)


def encoded(x, u, k, onehots, highs, et, zt, g_s):
    h, slope = silu_parts(dot(et[:, 0:PATCH], x))
    h = h.astype(BF)
    z = dot(zt[...], h)
    gap = z - u
    kept = k * gap
    z = k * z.astype(BF).astype(F32)
    row = lax.broadcasted_iota(jnp.int32, (16, z.shape[1]), 0)
    for v in range(2):
        part_z = z[v * 64 : v * 64 + 64]
        high = highs[v]
        low_k = jnp.where(high, 0.0, k)
        high_k = jnp.where(high, k, 0.0)
        left = jnp.concatenate(
            [
                jnp.where(high, 0.0, part_z),
                jnp.where(high, part_z, 0.0),
                jnp.where(row == 0, low_k, jnp.where(row == 1, high_k, 0.0)),
            ],
            0,
        ).astype(BF)
        g_s[v] += dot(left, onehots[v], NT)
    return h, slope, 0.5 * kept, kept * gap


def early_kernel(
    tile, mine, theirs,
    u_s, h_s, slope_s, gap_s, x_s, g_s, l_s, et, zt,
    *, batches, rows,
):
    level = lax.axis_index("level")
    bottom = level == 1
    edge = level * (rows - 1)
    bt = books(mine, theirs, bottom)
    encoder_weights(mine, theirs, bottom, et, zt)
    for ref in (g_s, l_s):
        ref[...] = jnp.zeros_like(ref)

    def batch(b, _):
        def row(i):
            return tile[pl.ds(pl.multiple_of((b * 2 * rows + i) * 8, 8), 8), :]

        run = [row(jnp.clip(level * rows + r, 0, 2 * rows - 1)) for r in range(-1, rows + 2)]
        value = jnp.concatenate([jnp.concatenate(run[i : i + 2], 0) for i in range(rows + 2)], 1)
        for dc, view in enumerate(sides(value)):
            x_s[dc, :, at(b * (rows + 2), rows + 2)] = view.astype(BF)
        own = run[1 : rows + 1]
        beyond = [row(rows - 2 * level + i) for i in range(2)]
        onehots, highs = one_hots(jnp.concatenate(own + beyond, 1))
        u = quantized(onehots, highs, bt)
        inner = slice(0, rows * W)
        for k, view in enumerate(sides(u)):
            view = view.astype(BF)
            u_s[k, :, at(b * (rows + 4) + 2, rows)] = view[:, inner]
            u_s[k, :, at(b * (rows + 4) + (rows + 2) * (1 - level), 2)] = view[:, rows * W :]
        k = jnp.concatenate([jnp.where(edge == i, 0.0, own[i][3:4]) for i in range(rows)], 1)
        h, slope, gap, error = encoded(
            patches(x_s, b * (rows + 2), rows), u[:, inner], k,
            [item[:, inner] for item in onehots], [item[:, inner] for item in highs], et, zt, g_s,
        )
        h_s[b] = h
        slope_s[b] = slope.astype(BF)
        gap_s[b] = gap
        l_s[0:128] += fold(error, 256)
        return 0

    lax.fori_loop(0, batches, batch, 0, unroll=True)


def patches(x_s, row, n):
    return jnp.concatenate([x_s[dc, :, at(row + pair, n)] for pair in (0, 2) for dc in range(3)], 0)


def giver(bottom, send):
    def give(start, one, zero, keep, offset, shift=0):
        n = one.shape[0]
        keep[start - shift : start - shift + n] = jnp.where(bottom, one, zero).astype(keep.dtype)
        start = offset + start - shift
        send[start : start + n] = jnp.where(bottom, zero, one).astype(BF)

    return give


def spread_back(dn, da):
    rows = da.shape[1] // W - 2
    near = jnp.concatenate([da[:, (2 - dr) * W : (2 - dr + rows) * W] for dr in range(3)], 0)
    spread = dot(dn[...], near)
    _, _, after = sides(spread[0:128])
    before, _, _ = sides(spread[256:384])
    return after + spread[128:256] + before


def encoder_back(du, gap, h, slope, x, zn, g_z, g_e):
    dz = (du + gap).astype(BF)
    dpre = (dot(zn[...], dz) * slope).astype(BF)
    g_e[...] += dot(x, dpre, NT)
    g_z[...] += dot(dz, h, NT)


def step_kernel(
    tile, near, mine, theirs, *refs,
    batches, rows,
):
    (keep_big, keep_small, send, h_out, slope_out, gap_out, da_out, x_out, dn_out, zn_out,
     u_s, h_s, slope_s, gap_s, x_s, g_s, l_s,
     t_s, dt, et, zt, ot, on, da_s, dn, zn, g_d, g_o, sems, fixed_sems) = refs[7:]
    level, me, devices = lax.axis_index("level"), lax.axis_index("dp"), lax.axis_size("dp")
    band, ext = 2 * rows, rows + 4
    above, below = (me + 1) * band, (me + 2) * band
    top_ok = (lax.rem(above, CROP) != 0) & (me > 0)
    bottom_ok = (lax.rem(below, CROP) != 0) & (me < devices - 1)
    valid = jnp.where(level == 0, top_ok.astype(jnp.int32), bottom_ok.astype(jnp.int32))
    bottom = level == 1

    def pair(start, size):
        return either(mine, theirs, bottom, start, size)

    for t in range(9):
        one, zero = pair(t * 128, 128)
        zero = jnp.concatenate([jnp.zeros((64, 128), BF), zero[0:64]], 0)
        dr, dc = t // 3, t % 3
        dn[dc * 128 : (dc + 1) * 128, dr * 256 : dr * 256 + 128] = one
        dn[dc * 128 : (dc + 1) * 128, dr * 256 + 128 : (dr + 1) * 256] = zero
        dt[0:128, t * 128 : (t + 1) * 128] = (0.5 * one.astype(F32)).T.astype(BF)
        dt[128:256, t * 128 : (t + 1) * 128] = (0.5 * zero.astype(F32)).T.astype(BF)
    encoder_weights(mine, theirs, bottom, et, zt)
    one, zero = pair(R_ZN, 128)
    zn[0:128] = (0.5 * one.astype(F32)).astype(BF)
    zn[128:256] = pltpu.roll(0.5 * zero.astype(F32), 64, 1).astype(BF)
    one, zero = pair(R_OT, 16)
    blank = jnp.zeros((8, 128), F32)
    out_t = jnp.concatenate(
        [
            jnp.concatenate([one[0:8].astype(F32), blank], 1),
            jnp.concatenate([blank, zero[0:8].astype(F32)], 1),
        ],
        0,
    )
    ot[...] = out_t.astype(BF)
    on[...] = (0.5 * out_t).T.astype(BF)
    bt = books(mine, theirs, bottom)
    fixed = [
        pltpu.make_async_copy(a, o, fixed_sems.at[n])
        for n, (a, o) in enumerate(((x_s, x_out), (dn, dn_out), (zn, zn_out)))
    ]
    fixed[1].start()
    fixed[2].start()

    sub = lax.broadcasted_iota(jnp.int32, (8, W), 0)
    nothing = jnp.where((sub == 4) | (sub == 5), NOBODY, 0.0)

    outside = []
    for b in range(batches):
        both = near[b * 16 : (b + 1) * 16].astype(F32)
        for r in range(2):
            outside.append(jnp.where(valid > 0, both[r * 8 : (r + 1) * 8], nothing))
    for i, shown in enumerate(outside):
        t_s[i] = shown

    def row(b, r):
        return tile[pl.ds(pl.multiple_of((b * band + r) * 8, 8), 8), :]

    for ref in (g_d, g_o):
        ref[...] = jnp.zeros_like(ref)

    def spread_rows(u, b, e, n):
        for k, view in enumerate(sides(u)):
            u_s[k, :, at(b * ext + e, n)] = view.astype(BF)

    first = level * rows
    runs = []
    for b in range(batches):
        low, high = outside[2 * b], outside[2 * b + 1]
        runs.append(jnp.concatenate([jnp.where(bottom, row(b, band - 1), high), jnp.where(bottom, low, row(b, 0))], 0))
        runs.append(jnp.concatenate([jnp.where(bottom, low, row(b, 0)), jnp.where(bottom, high, row(b, 1))], 0))
    for dc, view in enumerate(sides(jnp.concatenate(runs, 1))):
        view = view.astype(BF)
        for b in range(batches):
            x_s[dc, :, at(b * (rows + 2) + first, 2)] = view[:, b * 2 * W : (b + 1) * 2 * W]
    outer, edge = jnp.where(bottom, rows + 2, 0), level * (rows - 1)
    u = quantized(*one_hots(jnp.concatenate(outside, 1)), bt)
    for b in range(batches):
        spread_rows(u[:, b * 2 * W : (b + 1) * 2 * W], b, outer, 2)
    here = jnp.concatenate([row(b, level * (band - 1)) for b in range(batches)], 1)
    u = jnp.concatenate([u_s[1, :, at(b * ext + 2 + edge, 1)] for b in range(batches)], 1).astype(F32)
    x = jnp.concatenate([patches(x_s, b * (rows + 2) + edge, 1) for b in range(batches)], 1)
    h, slope, gap, error = encoded(x, u, here[3:4], *one_hots(here), et, zt, g_s)
    l_s[0:128, 0:W] += fold(error, W)
    for b in range(batches):
        cols = slice(b * W, (b + 1) * W)
        h_s[b, :, at(edge, 1)] = h[:, cols]
        slope_s[b, :, at(edge, 1)] = slope[:, cols].astype(BF)
        gap_s[b, :, at(edge, 1)] = gap[:, cols]

    pairs = ((h_s, h_out), (slope_s, slope_out), (gap_s, gap_out), (da_s, da_out))

    def leave(b, which=range(4)):
        return [pltpu.make_async_copy(pairs[n][0].at[b], pairs[n][1].at[b], sems.at[n, b]) for n in which]

    fixed[0].start()
    for b in range(batches):
        for copy in leave(b, range(3)):
            copy.start()

    def decode(b, _):
        u = jnp.concatenate(
            [u_s[dc, :, at(b * ext + dr, rows + 2)] for dr in range(3) for dc in range(3)], 0
        )
        inner = slice(W, (1 + rows) * W)
        g, slope = silu_parts(dot(dt[...], u))
        g = g.astype(BF)
        y = dot(ot[...], g)
        shown = [row(b, jnp.clip(level * rows + r, 0, band - 1)) for r in range(-1, rows + 1)]
        shown[0] = jnp.where(bottom, shown[0], t_s[2 * b + 1])
        shown[-1] = jnp.where(bottom, t_s[2 * b], shown[-1])
        here = jnp.concatenate(shown, 1)
        k = here[3:4]
        x = jnp.where(lax.broadcasted_iota(jnp.int32, here.shape, 0) < 3, here, 0.0)
        diff = y - jnp.concatenate([x, x], 0)
        kept = k * diff
        dy = (2.0 * kept).astype(BF)
        da = (dot(on[...], dy) * slope).astype(BF)
        da_s[b] = da
        leave(b, [3])[0].start()
        l_s[128:144] += fold((kept * diff)[:, inner], 256)
        g_d[...] += dot(u[:, inner], da[:, inner], NT)
        g_o[...] += dot(g[:, inner], dy[:, inner], NT)
        return 0

    lax.fori_loop(0, batches, decode, 0)
    give = giver(bottom, send)
    for t in range(9):
        top = jnp.concatenate([g_d[t * 128 + 64 : (t + 1) * 128, 128:256], jnp.zeros((64, 128), F32)], 0)
        give(t * 128, g_d[t * 128 : (t + 1) * 128, 0:128], top, keep_big, 0)
    for half in range(2):
        cols = slice(half * 128, (half + 1) * 128)
        give(TAPS + half * 128, g_s[0, 0:128, cols], g_s[1, 0:128, cols], keep_big, 0)
    pad = keep_big.shape[0]
    if pad > BIG:
        keep_big[BIG:pad] = jnp.zeros((pad - BIG, W), F32)
        send[BIG:pad] = jnp.zeros((pad - BIG, W), BF)
    readouts = g_o[...].T
    blank = jnp.zeros((8, 128), F32)
    give(
        S_O,
        jnp.concatenate([readouts[0:8, 0:128], blank], 0),
        jnp.concatenate([readouts[8:16, 128:256], blank], 0),
        keep_small,
        pad,
        LATE,
    )
    valid_sum = jnp.sum(g_s[0, 128:130])
    loss = 0.25 * jnp.sum(l_s[0:128]) + jnp.sum(l_s[128:144])
    lane = lax.broadcasted_iota(jnp.int32, (1, W), 1)
    other = jnp.where(lane == 0, loss, jnp.where(lane == 1, valid_sum, 0.0))
    exact = []
    for v in range(2):
        runs = [g_s[v, 128 + hi : 129 + hi, half * 128 : (half + 1) * 128] for hi in range(2) for half in range(2)]
        pieces = part(jnp.concatenate(runs + [other], 0), 3)
        exact.append(jnp.concatenate([p.astype(F32) for p in pieces] + [jnp.zeros((1, 128), F32)], 0))
    give(S_X, exact[0], exact[1], keep_small, pad, LATE)
    for copy in fixed + [copy for b in range(batches) for copy in leave(b)]:
        copy.wait()


def back_kernel(
    h_in, slope_in, gap_in, da_in, x_in, dn_in, zn_in, _,
    keep, send, h_s, slope_s, gap_s, da_s, x_s, dn, zn, g_e, g_z, sems, fixed_sems,
    *, batches, rows,
):
    bottom = lax.axis_index("level") == 1
    pairs = ((h_in, h_s), (slope_in, slope_s), (gap_in, gap_s), (da_in, da_s))

    def fetch(b):
        return [pltpu.make_async_copy(a.at[b], o.at[b], sems.at[n, b]) for n, (a, o) in enumerate(pairs)]

    fixed = [
        pltpu.make_async_copy(a, o, fixed_sems.at[n])
        for n, (a, o) in enumerate(((dn_in, dn), (zn_in, zn), (x_in, x_s)))
    ]
    count = h_s.shape[0]
    copies = [fetch(b) for b in range(count)]
    for copy in [fixed[0], copies[0][3], copies[0][2], fixed[1], *copies[0][:2], fixed[2]]:
        copy.start()
    g_e[...] = jnp.zeros_like(g_e)
    g_z[...] = jnp.zeros_like(g_z)
    fixed[0].wait()
    copies[0][3].wait()
    for b in range(1, count):
        for n in (3, 2, 0, 1):
            copies[b][n].start()
    du = spread_back(dn, da_s[0])
    for copy in [fixed[1], fixed[2]]:
        copy.wait()
    for b in range(count):
        for copy in copies[b][:3]:
            copy.wait()
        if b + 1 < count:
            copies[b + 1][3].wait()
        row = b * (rows + 2)
        encoder_back(du, gap_s[b], h_s[b], slope_s[b], patches(x_s, row, rows), zn, g_z, g_e)
        if b + 1 < count:
            du = spread_back(dn, da_s[b + 1])
    give = giver(bottom, send)
    give(S_Z, g_z[0:64, 0:128], g_z[64:128, 128:256], keep, 0)
    enc = []
    for cols in (slice(0, 128), slice(128, 256)):
        runs = [g_e[patch_row(t) : patch_row(t) + 3, cols] for t in range(9)]
        enc.append(jnp.concatenate(runs + [jnp.zeros((5, 128), F32)], 0))
    give(S_E, enc[0], enc[1], keep, 0)


def exact_sum(total, first):
    value = sum(total[first + EXACT * i : first + EXACT * (i + 1)] for i in range(3))
    pieces = [piece.astype(F32) for piece in part(value, 3)]
    return jnp.concatenate([total[:first], *pieces, total[first + 3 * EXACT :]], 0).astype(BF)


def merge_kernel(keep, early, got, big, early_out):
    size = keep.shape[0]
    big[...] = (keep[...] + got[0:size].astype(F32)).astype(BF)
    total = early[...].astype(F32) + got[size : size + SMALL - LATE].astype(F32)
    early_out[...] = exact_sum(total, S_X - LATE)


def sum_kernel(parts, out):
    total = parts[0].astype(F32)
    for i in range(1, parts.shape[0]):
        total = total + parts[i].astype(F32)
    out[...] = total.astype(BF)


def update_kernel(
    *refs, stages, start, other
):
    (parts, refs) = refs[:stages], refs[stages:]
    (count, total, ew, e1, e2, zw, z1, z2, dw, d1, d2, ow, o1, o2,
     loss_out, valid_out, count_out, total_out,
     em, es, ep, ec, zm, zs, zp, zc, dm, ds, dp, dc, om, os, op, oc, big, rows) = refs
    share = big.shape[0] // stages
    top = lax.axis_index("level") == 0
    index = (lax.axis_index("dp") >> jnp.where(top, start, other)) & (stages - 1)
    size = big.shape[0] // lax.axis_size("dp")
    small = jnp.zeros((SMALL, W), F32)
    for n, ref in enumerate(parts):
        value = ref[0:share].astype(F32)
        for h in range(share // size):
            place = h * stages + (index ^ n)
            if other != start:
                place = jnp.where(top, place, (index ^ n) * (share // size) + h)
            row = pl.multiple_of(place * size, 8)
            big[pl.ds(row, size), :] = value[h * size : (h + 1) * size]
        small = small + ref[share : share + SMALL].astype(F32)
    exact = sum(small[S_X + EXACT * i : S_X + EXACT * (i + 1)] for i in range(3))
    loss = jnp.sum(exact[4:5, 0:1])
    valid = jnp.sum(exact[4:5, 1:2])
    loss_out[0, 0] = loss
    valid_out[0, 0] = valid
    counts = jnp.concatenate([exact[i : i + 1] for i in range(4)], 1)
    count_out[...] = 0.99 * count[...] + 0.01 * counts
    for quarter in range(4):
        row = TAPS + (quarter % 2) * 128 + (quarter // 2) * 64
        cols = slice(quarter * 128, (quarter + 1) * 128)
        total_out[0, :, cols] = 0.99 * total[0, :, cols] + 0.01 * big[row : row + 64]

    scale = 1.0 - 0.5**STEP

    def adamw(grad, weight, first, second, rate):
        grad = grad / valid
        moment = 0.5 * first + 0.5 * grad
        square = 0.5 * second + 0.5 * grad * grad
        master = weight - rate * (moment / scale / (jnp.sqrt(square / scale) + 1e-08) + 0.01 * weight)
        return moment, square, master

    def whole(grad, w, first, second, rate, outs):
        outs[0][0], outs[1][0], master = adamw(grad, w[0], first[0], second[0], rate)
        outs[2][0] = master
        outs[3][0] = master.astype(BF)

    def by_row(grad, w, first, second, rate, outs):
        n = w.shape[0]
        for i in range(n):
            outs[0][i], outs[1][i], master = adamw(grad[i : i + 1], w[i], first[i], second[i], rate)
            outs[2][i] = master
            rows[i : i + 1] = master
        outs[3][0] = rows[0:n].astype(BF)

    by_row(small[S_E : S_E + 27], ew, e1, e2, RATES[0], (em, es, ep, ec))
    whole(small[S_Z : S_Z + 64], zw, z1, z2, RATES[1], (zm, zs, zp, zc))
    whole(big[0:TAPS], dw, d1, d2, RATES[2], (dm, ds, dp, dc))
    by_row(small[S_O : S_O + 3], ow, o1, o2, RATES[3], (om, os, op, oc))


def radices(devices):
    bits = devices.bit_length() - 1
    return [(start, min(2, bits - start)) for start in range(0, bits, 2)]


def partners(start, width):
    return [k << start for k in range(1, 1 << width)]


def xor_pairs(devices, by, other):
    return [(i, i ^ by) for i in range(devices)] + [(devices + i, devices + (i ^ other)) for i in range(devices)]


def lowered(value):
    return lax.reduce_precision(value, 8, 7)


def sum_small(parts, first):
    total = sum(item.astype(F32) for item in parts)
    value = sum(total[first + EXACT * i : first + EXACT * (i + 1)] for i in range(3))
    high = lowered(value)
    middle = lowered(value - high)
    low = value - high - middle
    rest = total[first + 3 * EXACT :]
    return jnp.concatenate([total[:first], high, middle, low, rest], 0).astype(BF)


def local(
    image, mask, codes, ema_count, ema_sum,
    encoder_weight, encoder_first, encoder_second,
    latent_weight, latent_first, latent_second,
    decoder_weight, decoder_first, decoder_second,
    readout_weight, readout_first, readout_second,
):
    batches, _, band, width = image.shape
    rows = band // 2
    me, devices = lax.axis_index("dp"), lax.axis_size("dp")
    ema_sum = jnp.swapaxes(ema_sum, 1, 2)
    encoder_weight, encoder_first, encoder_second = (
        jnp.swapaxes(item, 0, 1) for item in (encoder_weight, encoder_first, encoder_second)
    )
    latent_weight, latent_first, latent_second = (
        jnp.swapaxes(item, 1, 2) for item in (latent_weight, latent_first, latent_second)
    )
    readout_weight, readout_first, readout_second = (
        jnp.transpose(item, (2, 0, 1)) for item in (readout_weight, readout_first, readout_second)
    )

    def limit(mib):
        return pltpu.CompilerParams(vmem_limit_bytes=mib * 1024 * 1024)

    def outside(*items):
        return [pltpu.with_memory_space_constraint(item, pltpu.HBM) for item in items]

    def inside_vmem(item):
        return pltpu.with_memory_space_constraint(item, pltpu.VMEM)

    swap = [(0, 1), (1, 0)]
    others = lax.ppermute(codes, "level", swap)
    tiled = pltpu.VMEM((batches * band * 8, W), F32)
    pack, tile = pl.pallas_call(
        pack_kernel,
        out_shape=[pltpu.VMEM((PACKED, W), BF), tiled],
        in_specs=[VMEM] * 9,
        out_specs=[VMEM] * 2,
        scratch_shapes=[pltpu.VMEM((128, 128), F32)],
        compiler_params=limit(56),
    )(
        *outside(
            image, mask, codes, ema_count, ema_sum, encoder_weight, latent_weight, decoder_weight, readout_weight
        )
    )
    others, pack, tile = lax.optimization_barrier((others, pack, tile))
    tile, near = pl.pallas_call(
        rows_kernel,
        out_shape=[tiled, pltpu.VMEM((batches * 16, W), BF)],
        in_specs=[VMEM] * 2,
        out_specs=[VMEM] * 2,
        input_output_aliases={0: 0},
        compiler_params=limit(32),
    )(inside_vmem(tile), inside_vmem(others))

    both = ("level", "dp")
    inside = [d for d in range(1, devices) if (d + 1) * band % CROP != 0]
    pairs = [(d - 1, d) for d in inside] + [(devices + d, devices + d - 1) for d in inside]
    near = lax.ppermute(near, both, pairs)
    theirs = lax.ppermute(pack, "level", swap)

    ext = rows + 4
    ext = rows + 4
    pixels = batches * rows * W
    framed = batches * (rows + 2) * W
    held = [
        ((batches, 256, rows * W), BF),
        ((batches, 256, rows * W), BF),
        ((batches, 128, rows * W), F32),
        ((batches, 256, (rows + 2) * W), BF),
    ]
    fixed = [((3, 16, framed), BF), ((384, 768), BF), ((256, 128), BF)]
    size = -(-BIG // (8 * devices)) * 8
    padded = size * devices
    shape = jax.ShapeDtypeStruct
    staged = [
        pltpu.VMEM((3, 128, batches * ext * W), BF),
        *[pltpu.VMEM(*item) for item in held[:3]],
        pltpu.VMEM(*fixed[0]),
        pltpu.VMEM((2, 144, 256), F32),
        pltpu.VMEM((144, 256), F32),
    ]
    stages_early = pl.pallas_call(
        functools.partial(early_kernel, batches=batches, rows=rows),
        out_shape=staged,
        in_specs=[VMEM] * 3,
        out_specs=[VMEM] * 7,
        scratch_shapes=[pltpu.VMEM((256, 128), BF), pltpu.VMEM((128, 256), BF)],
        compiler_params=limit(EARLY_MIB),
        cost_estimate=pl.CostEstimate(flops=3 << 30, bytes_accessed=1 << 20, transcendentals=0),
    )(*[inside_vmem(item) for item in (tile, pack, theirs)])
    results = pl.pallas_call(
        functools.partial(step_kernel, batches=batches, rows=rows),
        out_shape=[
            pltpu.VMEM((padded, W), F32),
            pltpu.VMEM((SMALL - LATE, W), BF),
            pltpu.VMEM((padded + SMALL - LATE, W), BF),
            *[shape(*item) for item in held + fixed],
            *staged,
        ],
        in_specs=[VMEM] * 11,
        out_specs=[VMEM] * 3 + [AWAY] * 7 + [VMEM] * 7,
        input_output_aliases={4 + i: 10 + i for i in range(7)},
        scratch_shapes=[
            pltpu.VMEM((2 * batches, 8, W), F32),
            pltpu.VMEM((256, TAPS), BF),
            pltpu.VMEM((256, 128), BF),
            pltpu.VMEM((128, 256), BF),
            pltpu.VMEM((16, 256), BF),
            pltpu.VMEM((256, 16), BF),
            pltpu.VMEM(*held[3]),
            *[pltpu.VMEM(*item) for item in fixed[1:]],
            pltpu.VMEM((TAPS, 256), F32),
            pltpu.VMEM((256, 16), F32),
            pltpu.SemaphoreType.DMA((4, batches)),
            pltpu.SemaphoreType.DMA((3,)),
        ],
        compiler_params=limit(STEP_MIB),
    )(*[inside_vmem(item) for item in (tile, near, pack, theirs, *stages_early)])
    keep, early, send = results[:3]
    kept = results[3:10]

    got = lax.ppermute(send, "level", swap)
    big, early = pl.pallas_call(
        merge_kernel,
        out_shape=[pltpu.VMEM((padded, W), BF), pltpu.VMEM((SMALL - LATE, W), BF)],
        in_specs=[VMEM] * 3,
        out_specs=[VMEM] * 2,
        compiler_params=limit(32),
    )(*[inside_vmem(item) for item in (keep, early, got)])
    big = lax.all_to_all(big.reshape(devices, size, W), "dp", 0, 0)

    late, send = pl.pallas_call(
        functools.partial(back_kernel, batches=batches, rows=rows),
        out_shape=[pltpu.VMEM((LATE, W), BF), pltpu.VMEM((LATE, W), BF)],
        in_specs=[AWAY] * 8,
        out_specs=[VMEM] * 2,
        scratch_shapes=[
            *[pltpu.VMEM(*item) for item in held + fixed],
            pltpu.VMEM((PATCH, 256), F32),
            pltpu.VMEM((128, 256), F32),
            pltpu.SemaphoreType.DMA((4, batches)),
            pltpu.SemaphoreType.DMA((3,)),
        ],
        compiler_params=limit(BACK_MIB),
        cost_estimate=pl.CostEstimate(flops=2 * pixels * 98304 * 4, bytes_accessed=1 << 20, transcendentals=0),
    )(*outside(*kept), got)
    got = lax.ppermute(send, "level", swap)
    late = (late.astype(F32) + got.astype(F32)).astype(BF)
    small = jnp.concatenate([late, early], 0)

    big = pl.pallas_call(
        sum_kernel,
        out_shape=pltpu.VMEM((size, W), BF),
        in_specs=[VMEM],
        out_specs=VMEM,
        compiler_params=limit(32),
        cost_estimate=pl.CostEstimate(flops=1 << 34, bytes_accessed=1 << 20, transcendentals=0),
    )(inside_vmem(big))[None]
    stages = radices(devices)
    crossed = len(stages) == 2 and stages[0][1] == stages[1][1]
    for number, (start, width_bits) in enumerate(reversed(stages)):
        count = 1 << width_bits
        other = stages[number][0] if crossed else start
        index = (me >> jnp.where(lax.axis_index("level") == 0, start, other)) & (count - 1)
        payload = jnp.concatenate([big.reshape(-1, W), small], 0)
        parts = [payload] + [
            lax.ppermute(payload, both, xor_pairs(devices, k << start, k << other)) for k in range(1, count)
        ]
        if number == len(stages) - 1:
            break
        high = big.shape[0]
        stacked = jnp.zeros((high, count, size, W), BF)
        far_first = [0, *range(count - 1, 0, -1)]
        for k in far_first:
            piece = parts[k][: high * size].reshape(high, size, W)
            stacked = lax.dynamic_update_index_in_dim(stacked, piece, index ^ k, 1)
        small = sum_small([parts[k][high * size :] for k in far_first], S_X)
        big = stacked.reshape(high * count, size, W)

    state = (
        ema_count, ema_sum,
        encoder_weight, encoder_first, encoder_second, latent_weight, latent_first, latent_second,
        decoder_weight, decoder_first, decoder_second, readout_weight, readout_first, readout_second,
    )
    outs = [jax.ShapeDtypeStruct((1, 1), F32)] * 2
    outs += [jax.ShapeDtypeStruct(ema_count.shape, F32), jax.ShapeDtypeStruct(ema_sum.shape, F32)]
    for item in (encoder_weight, latent_weight, decoder_weight, readout_weight):
        copy = item.shape if item.shape[0] == 1 else (1, item.shape[0], item.shape[2])
        outs += [jax.ShapeDtypeStruct(item.shape, F32)] * 3 + [jax.ShapeDtypeStruct(copy, BF)]
    result = pl.pallas_call(
        functools.partial(update_kernel, stages=len(parts), start=start, other=other),
        out_shape=outs,
        in_specs=[VMEM] * (len(parts) + len(state)),
        out_specs=[SMEM] * 2 + [VMEM] * (len(outs) - 2),
        scratch_shapes=[pltpu.VMEM((padded, W), F32), pltpu.VMEM((32, W), F32)],
        compiler_params=limit(16),
    )(*parts, *state)
    loss, valid, count_new, total_new = result[:4]
    enc, lat, dec, read = (list(result[4 * n : 4 * n + 4]) for n in range(1, 5))
    enc[:3] = [jnp.swapaxes(item, 0, 1) for item in enc[:3]]
    lat = [jnp.swapaxes(item, 1, 2) for item in lat]
    read = [jnp.transpose(item, (1, 2, 0)) for item in read[:3]] + [jnp.swapaxes(read[3], 1, 2)]
    return (loss.reshape(()), valid.reshape(()), count_new, jnp.swapaxes(total_new, 1, 2), *enc, *lat, *dec, *read)


def solution(mesh):
    rank = (0, 0, 2, 3) + (3,) * 16
    in_specs = (P(None, None, "dp", None), P(None, "dp", None), P("level", None, "dp", None), P("level", None))
    in_specs += (P("level", None, None),) * 13
    out_specs = tuple(P(*(("level",) + (None,) * (n - 1) if n else ())) for n in rank)
    return jax.shard_map(local, mesh=mesh, in_specs=in_specs, out_specs=out_specs, check_vma=False)
```
